32 devices in a mesh: dp: 8 (over z, x), mp: 4 (over y, core).
Axes of the slice: x: 2, y: 2, z: 4, core: 2. Of those that a mesh axis runs over, the one named last changes fastest.
Arguments:
- slow_input: float32 [192, 196, 1024], P('dp', None, 'mp')
- fast_input: float32 [768, 196, 128], P('dp')
- clip_starts: int32 [24], replicated, may hold values from 0 to 191, as said below
- fast_reduce: float32 [128, 32], replicated, may hold values from -0.5 to 0.5
- fast_reduce_gain: float32 [32], replicated, may hold values from 0.1 to 1.9
- fast_reduce_bias: float32 [32], replicated, may hold values from -1.5 to 1.5
- fast_temporal: float32 [3, 32, 32], replicated, may hold values from -0.625 to 0.625
- fast_temporal_gain: float32 [32], replicated, may hold values from 0.1 to 1.9
- fast_temporal_bias: float32 [32], replicated, may hold values from -1.5 to 1.5
- fast_expand: float32 [32, 128], replicated, may hold values from -1 to 1
- fast_expand_gain: float32 [128], replicated, may hold values from 0.1 to 1.9
- fast_expand_bias: float32 [128], replicated, may hold values from -1.5 to 1.5
- lateral_conv: float32 [5, 128, 256], P(None, None, 'mp'), may hold values from -0.25 to 0.25
- lateral_gain: float32 [256], P('mp'), may hold values from 0.1 to 1.9
- lateral_bias: float32 [256], P('mp'), may hold values from -1.5 to 1.5
- slow_reduce: float32 [1280, 256], P(None, 'mp'), may hold values from -0.15625 to 0.15625
- slow_reduce_gain: float32 [256], P('mp'), may hold values from 0.1 to 1.9
- slow_reduce_bias: float32 [256], P('mp'), may hold values from -1.5 to 1.5
- slow_temporal: float32 [3, 256, 256], P(None, None, 'mp'), may hold values from -0.21875 to 0.21875
- slow_temporal_gain: float32 [256], P('mp'), may hold values from 0.1 to 1.9
- slow_temporal_bias: float32 [256], P('mp'), may hold values from -1.5 to 1.5
- slow_expand: float32 [256, 1024], P('mp'), may hold values from -0.375 to 0.375
- slow_expand_gain: float32 [1024], P('mp'), may hold values from 0.1 to 1.9
- slow_expand_bias: float32 [1024], P('mp'), may hold values from -1.5 to 1.5
- shortcut_conv: float32 [1280, 1024], P(None, 'mp'), may hold values from -0.15625 to 0.15625
- shortcut_gain: float32 [1024], P('mp'), may hold values from 0.1 to 1.9
- shortcut_bias: float32 [1024], P('mp'), may hold values from -1.5 to 1.5
- slow_cotangent: float32 [192, 196, 1024], P('dp', None, 'mp')
- fast_cotangent: float32 [768, 196, 128], P('dp')
Outputs:
- slow_output: float32 [192, 196, 1024], P('dp', None, 'mp')
- fast_output: float32 [768, 196, 128], P('dp')
- slow_input_gradient: float32 [192, 196, 1024], P('dp', None, 'mp')
- fast_input_gradient: float32 [768, 196, 128], P('dp')
- fast_reduce_gradient: float32 [128, 32], replicated
- fast_reduce_gain_gradient: float32 [32], replicated
- fast_reduce_bias_gradient: float32 [32], replicated
- fast_temporal_gradient: float32 [3, 32, 32], replicated
- fast_temporal_gain_gradient: float32 [32], replicated
- fast_temporal_bias_gradient: float32 [32], replicated
- fast_expand_gradient: float32 [32, 128], replicated
- fast_expand_gain_gradient: float32 [128], replicated
- fast_expand_bias_gradient: float32 [128], replicated
- lateral_conv_gradient: float32 [5, 128, 256], P(None, None, 'mp')
- lateral_gain_gradient: float32 [256], P('mp')
- lateral_bias_gradient: float32 [256], P('mp')
- slow_reduce_gradient: float32 [1280, 256], P(None, 'mp')
- slow_reduce_gain_gradient: float32 [256], P('mp')
- slow_reduce_bias_gradient: float32 [256], P('mp')
- slow_temporal_gradient: float32 [3, 256, 256], P(None, None, 'mp')
- slow_temporal_gain_gradient: float32 [256], P('mp')
- slow_temporal_bias_gradient: float32 [256], P('mp')
- slow_expand_gradient: float32 [256, 1024], P('mp')
- slow_expand_gain_gradient: float32 [1024], P('mp')
- slow_expand_bias_gradient: float32 [1024], P('mp')
- shortcut_conv_gradient: float32 [1280, 1024], P(None, 'mp')
- shortcut_gain_gradient: float32 [1024], P('mp')
- shortcut_bias_gradient: float32 [1024], P('mp')
The draws below stay inside these ranges and needn't reach their ends.
Inputs may be any that keep to these rules, and one draw needn't show every extreme that they name: clip_starts[0] is 0; clip k from 1 to 22 starts at frame 8 * k plus 1 to 7; the last clip starts at 191; a clip runs up to the next start, the last one to the last frame.
All inputs are finite; a program needn't handle non-finite values.
Results may differ from the reference program's by a relative error of at most 0.0003.
Values sent between devices are 32-bit elements; how exact they have to be, the bound alone decides.
A program may use at most 384 MiB of HBM per device.

```python
import math
import jax
import jax.numpy as jnp
from jax import lax

PIXELS = 196
ALPHA = 4
CLIP = 8
SLOW_WIDTH = 1024
LATERAL_WIDTH = 256
SLOW_INNER = 256
FAST_WIDTH = 128
FAST_INNER = 32
FRAMES = 192
FAST_FRAMES = 768
CLIPS = 24
SLOW_IN = 1280


def rising(key, length):
    position = jnp.arange(length, dtype=jnp.float32) / float(max(length - 1, 1))
    roughness = jax.random.uniform(key, (length,), jnp.float32, 0.7, 1.4)
    return jnp.exp(math.log(3.0) * position) * roughness


def draw_slow_input(key, part):
    key = jax.random.fold_in(key, 11)
    key_scale, key_value = jax.random.split(key, 2)
    frame_scale = rising(key_scale, FRAMES)[:, None, None]
    values = jax.random.truncated_normal(key_value, -4.0, 4.0, (FRAMES, PIXELS, SLOW_WIDTH), jnp.float32)
    return values * frame_scale


def draw_fast_input(key, part):
    key = jax.random.fold_in(key, 13)
    key_scale, key_value = jax.random.split(key, 2)
    frame_scale = rising(key_scale, FAST_FRAMES)[:, None, None]
    values = jax.random.truncated_normal(key_value, -4.0, 4.0, (FAST_FRAMES, PIXELS, FAST_WIDTH), jnp.float32)
    return values * frame_scale


def draw_slow_cotangent(key, part):
    key = jax.random.fold_in(key, 19)
    key_scale, key_value = jax.random.split(key, 2)
    frame_scale = rising(key_scale, FRAMES)[:, None, None]
    values = jax.random.truncated_normal(key_value, -4.0, 4.0, (FRAMES, PIXELS, SLOW_WIDTH), jnp.float32)
    return values * frame_scale


def draw_fast_cotangent(key, part):
    key = jax.random.fold_in(key, 23)
    key_scale, key_value = jax.random.split(key, 2)
    frame_scale = rising(key_scale, FAST_FRAMES)[:, None, None]
    values = jax.random.truncated_normal(key_value, -4.0, 4.0, (FAST_FRAMES, PIXELS, FAST_WIDTH), jnp.float32)
    return values * frame_scale


def draw_clip_starts(key, part):
    key = jax.random.fold_in(key, 17)
    offsets = jax.random.randint(key, (CLIPS,), 1, CLIP, dtype=jnp.int32)
    number = jnp.arange(CLIPS, dtype=jnp.int32)
    offsets = jnp.where(number == CLIPS - 1, CLIP - 1, offsets)
    return number * CLIP + jnp.where(number == 0, 0, offsets)


def levels(rng, extent, cuts, least, top_value):
    factor_of, own = 1.0, jax.random.fold_in(rng, 6)
    for dim, blocks in cuts:
        heights = jnp.exp(jax.random.uniform(jax.random.fold_in(own, dim), (blocks,), jnp.float32, least / len(cuts), top_value / len(cuts)))
        factor_of = factor_of * jnp.repeat(heights, extent[dim] // blocks).reshape([-1 if axis == dim else 1 for axis in range(len(extent))])
    return factor_of


def normal_values(own_key, shape, width, most, cuts=(), kind=jnp.bfloat16):
    values = width * jax.random.normal(own_key, shape, jnp.float32)
    if cuts:
        values = values * levels(own_key, shape, cuts, -0.22, 0.18)
    return jnp.clip(values, -most, most).astype(kind)


def setup_inputs(seed: int = 0) -> dict:
    streams_of = jax.random.split(jax.random.key(seed), 30)
    return {
        "slow_input": draw_slow_input(jax.random.fold_in(streams_of[29], 71), 0),
        "fast_input": draw_fast_input(jax.random.fold_in(streams_of[29], 71), 0),
        "clip_starts": draw_clip_starts(jax.random.fold_in(streams_of[29], 71), 0),
        "fast_reduce": normal_values(streams_of[3], (FAST_WIDTH, FAST_INNER), FAST_WIDTH ** -0.5, 0.5, (), jnp.float32),
        "fast_reduce_gain": jnp.clip(1.0 + 0.18 * jax.random.normal(streams_of[4], (FAST_INNER,), jnp.float32), 0.1, 1.9),
        "fast_reduce_bias": normal_values(streams_of[5], (FAST_INNER,), 0.3, 1.5, (), jnp.float32),
        "fast_temporal": normal_values(streams_of[6], (3, FAST_INNER, FAST_INNER), (3 * FAST_INNER) ** -0.5, 0.625, (), jnp.float32),
        "fast_temporal_gain": jnp.clip(1.0 + 0.18 * jax.random.normal(streams_of[7], (FAST_INNER,), jnp.float32), 0.1, 1.9),
        "fast_temporal_bias": normal_values(streams_of[8], (FAST_INNER,), 0.3, 1.5, (), jnp.float32),
        "fast_expand": normal_values(streams_of[9], (FAST_INNER, FAST_WIDTH), FAST_INNER ** -0.5, 1.0, (), jnp.float32),
        "fast_expand_gain": jnp.clip(1.0 + 0.18 * jax.random.normal(streams_of[10], (FAST_WIDTH,), jnp.float32), 0.1, 1.9),
        "fast_expand_bias": normal_values(streams_of[11], (FAST_WIDTH,), 0.3, 1.5, (), jnp.float32),
        "lateral_conv": normal_values(streams_of[12], (5, FAST_WIDTH, LATERAL_WIDTH), (5 * FAST_WIDTH) ** -0.5, 0.25, ((2, 4),), jnp.float32),
        "lateral_gain": jnp.clip(1.0 + 0.18 * jax.random.normal(streams_of[13], (LATERAL_WIDTH,), jnp.float32), 0.1, 1.9),
        "lateral_bias": normal_values(streams_of[14], (LATERAL_WIDTH,), 0.3, 1.5, ((0, 4),), jnp.float32),
        "slow_reduce": normal_values(streams_of[15], (SLOW_IN, SLOW_INNER), SLOW_IN ** -0.5, 0.15625, ((1, 4),), jnp.float32),
        "slow_reduce_gain": jnp.clip(1.0 + 0.18 * jax.random.normal(streams_of[16], (SLOW_INNER,), jnp.float32), 0.1, 1.9),
        "slow_reduce_bias": normal_values(streams_of[17], (SLOW_INNER,), 0.3, 1.5, ((0, 4),), jnp.float32),
        "slow_temporal": normal_values(streams_of[18], (3, SLOW_INNER, SLOW_INNER), (3 * SLOW_INNER) ** -0.5, 0.21875, ((2, 4),), jnp.float32),
        "slow_temporal_gain": jnp.clip(1.0 + 0.18 * jax.random.normal(streams_of[19], (SLOW_INNER,), jnp.float32), 0.1, 1.9),
        "slow_temporal_bias": normal_values(streams_of[20], (SLOW_INNER,), 0.3, 1.5, ((0, 4),), jnp.float32),
        "slow_expand": normal_values(streams_of[21], (SLOW_INNER, SLOW_WIDTH), SLOW_INNER ** -0.5, 0.375, ((0, 4),), jnp.float32),
        "slow_expand_gain": jnp.clip(1.0 + 0.18 * jax.random.normal(streams_of[22], (SLOW_WIDTH,), jnp.float32), 0.1, 1.9),
        "slow_expand_bias": normal_values(streams_of[23], (SLOW_WIDTH,), 0.3, 1.5, ((0, 4),), jnp.float32),
        "shortcut_conv": normal_values(streams_of[24], (SLOW_IN, SLOW_WIDTH), SLOW_IN ** -0.5, 0.15625, ((1, 4),), jnp.float32),
        "shortcut_gain": jnp.clip(1.0 + 0.18 * jax.random.normal(streams_of[25], (SLOW_WIDTH,), jnp.float32), 0.1, 1.9),
        "shortcut_bias": normal_values(streams_of[26], (SLOW_WIDTH,), 0.3, 1.5, ((0, 4),), jnp.float32),
        "slow_cotangent": draw_slow_cotangent(jax.random.fold_in(streams_of[29], 71), 0),
        "fast_cotangent": draw_fast_cotangent(jax.random.fold_in(streams_of[29], 71), 0),
    }


EPSILON = 1e-05
PRECISE = lax.Precision.HIGHEST

@jax.custom_vjp
def low(v):
    return lax.optimization_barrier(v.astype(jnp.bfloat16)).astype(jnp.float32)

@jax.custom_vjp
def low_back(v):
    return v

def low_keep(v):
    return (low(v), None)

def low_pass(kept, grad):
    return (grad,)

def back_keep(v):
    return (v, None)

def back_low(kept, grad):
    return (low(grad),)
low.defvjp(low_keep, low_pass)
low_back.defvjp(back_keep, back_low)

def product(former, latter):
    return jnp.dot(former, latter, precision=PRECISE, preferred_element_type=jnp.float32)

def frame_clips(length, starts):
    frame_at = jnp.arange(length, dtype=jnp.int32)
    return lax.optimization_barrier(jnp.sum((starts[None, :] <= frame_at[:, None]).astype(jnp.int32), axis=1)) - 1

def shifted(tensor, offset):
    length = tensor.shape[0]
    padded = jnp.pad(tensor, ((2, 2), (0, 0), (0, 0)))
    return padded[2 + offset:2 + offset + length]

def shifted_ids(clip_of, offset):
    length = clip_of.shape[0]
    padded = jnp.pad(clip_of, (2, 2), constant_values=-5)
    return padded[2 + offset:2 + offset + length]

def batch_norm(tensor, gain_vector, bias_vector):
    average = lax.optimization_barrier(jnp.mean(tensor, axis=(0, 1)))
    spread = lax.optimization_barrier(jnp.mean(tensor * tensor, axis=(0, 1))) - average * average
    return (tensor - average) * lax.rsqrt(spread + EPSILON) * gain_vector + bias_vector

def temporal(tensor, weight, clip_of):
    summed = jnp.zeros(tensor.shape[:2] + (weight.shape[2],), jnp.float32)
    for column in range(3):
        allowed = (shifted_ids(clip_of, column - 1) == clip_of).astype(jnp.float32)
        summed = summed + allowed[:, None, None] * product(shifted(tensor, column - 1), weight[column])
    return summed

def lateral(fast_frames, weight, clip_of):
    own_clips = clip_of[::ALPHA]
    summed = jnp.zeros((fast_frames.shape[0] // ALPHA, fast_frames.shape[1], weight.shape[2]), jnp.float32)
    for column in range(5):
        allowed = (shifted_ids(clip_of, column - 2)[::ALPHA] == own_clips).astype(jnp.float32)
        summed = summed + allowed[:, None, None] * product(shifted(fast_frames, column - 2)[::ALPHA], weight[column])
    return summed

def forward(slow_value, fast_value, weights, slow_ids, fast_ids):
    fast_reduce, fast_reduce_gain, fast_reduce_bias, fast_temporal, fast_temporal_gain, fast_temporal_bias, fast_expand, fast_expand_gain, fast_expand_bias, lateral_conv, lateral_gain, lateral_bias, slow_reduce, slow_reduce_gain, slow_reduce_bias, slow_temporal, slow_temporal_gain, slow_temporal_bias, slow_expand, slow_expand_gain, slow_expand_bias, shortcut_conv, shortcut_gain, shortcut_bias = weights
    fast_first = jax.nn.silu(batch_norm(product(fast_value, fast_reduce), fast_reduce_gain, fast_reduce_bias))
    fast_middle = jax.nn.silu(batch_norm(temporal(fast_first, fast_temporal, fast_ids), fast_temporal_gain, fast_temporal_bias))
    fast_last = batch_norm(product(fast_middle, fast_expand), fast_expand_gain, fast_expand_bias)
    fast_output = jax.nn.silu(fast_last + fast_value)
    side = jax.nn.silu(batch_norm(lateral(fast_value, lateral_conv, fast_ids), lateral_gain, lateral_bias))
    joined = jnp.concatenate([slow_value, side], axis=2)
    slow_first = jax.nn.silu(batch_norm(product(joined, slow_reduce), slow_reduce_gain, slow_reduce_bias))
    slow_middle = jax.nn.silu(batch_norm(temporal(slow_first, slow_temporal, slow_ids), slow_temporal_gain, slow_temporal_bias))
    slow_last = batch_norm(product(slow_middle, slow_expand), slow_expand_gain, slow_expand_bias)
    short_path = batch_norm(product(joined, shortcut_conv), shortcut_gain, shortcut_bias)
    slow_output = jax.nn.silu(slow_last + short_path)
    return (slow_output, fast_output)

def reference(slow_input, fast_input, clip_starts, fast_reduce, fast_reduce_gain, fast_reduce_bias, fast_temporal, fast_temporal_gain, fast_temporal_bias, fast_expand, fast_expand_gain, fast_expand_bias, lateral_conv, lateral_gain, lateral_bias, slow_reduce, slow_reduce_gain, slow_reduce_bias, slow_temporal, slow_temporal_gain, slow_temporal_bias, slow_expand, slow_expand_gain, slow_expand_bias, shortcut_conv, shortcut_gain, shortcut_bias, slow_cotangent, fast_cotangent):
    slow_ids = frame_clips(slow_input.shape[0], clip_starts)
    fast_ids = frame_clips(fast_input.shape[0], clip_starts * ALPHA)
    weights = (fast_reduce, fast_reduce_gain, fast_reduce_bias, fast_temporal, fast_temporal_gain, fast_temporal_bias, fast_expand, fast_expand_gain, fast_expand_bias, lateral_conv, lateral_gain, lateral_bias, slow_reduce, slow_reduce_gain, slow_reduce_bias, slow_temporal, slow_temporal_gain, slow_temporal_bias, slow_expand, slow_expand_gain, slow_expand_bias, shortcut_conv, shortcut_gain, shortcut_bias)

    def whole(slow_value, fast_value, weight_set):
        return forward(slow_value, fast_value, weight_set, slow_ids, fast_ids)
    outputs, pullback = jax.vjp(whole, slow_input, fast_input, weights)
    slow_output, fast_output = outputs
    slow_input_gradient, fast_input_gradient, changes = pullback((slow_cotangent, fast_cotangent))
    fast_reduce_gradient, fast_reduce_gain_gradient, fast_reduce_bias_gradient, fast_temporal_gradient, fast_temporal_gain_gradient, fast_temporal_bias_gradient, fast_expand_gradient, fast_expand_gain_gradient, fast_expand_bias_gradient, lateral_conv_gradient, lateral_gain_gradient, lateral_bias_gradient, slow_reduce_gradient, slow_reduce_gain_gradient, slow_reduce_bias_gradient, slow_temporal_gradient, slow_temporal_gain_gradient, slow_temporal_bias_gradient, slow_expand_gradient, slow_expand_gain_gradient, slow_expand_bias_gradient, shortcut_conv_gradient, shortcut_gain_gradient, shortcut_bias_gradient = changes
    return (slow_output, fast_output, slow_input_gradient, fast_input_gradient, fast_reduce_gradient, fast_reduce_gain_gradient, fast_reduce_bias_gradient, fast_temporal_gradient, fast_temporal_gain_gradient, fast_temporal_bias_gradient, fast_expand_gradient, fast_expand_gain_gradient, fast_expand_bias_gradient, lateral_conv_gradient, lateral_gain_gradient, lateral_bias_gradient, slow_reduce_gradient, slow_reduce_gain_gradient, slow_reduce_bias_gradient, slow_temporal_gradient, slow_temporal_gain_gradient, slow_temporal_bias_gradient, slow_expand_gradient, slow_expand_gain_gradient, slow_expand_bias_gradient, shortcut_conv_gradient, shortcut_gain_gradient, shortcut_bias_gradient)
```

```python
import functools

import jax
import jax.numpy as jnp
from jax import lax
from jax.experimental import pallas as pl
from jax.experimental.pallas import tpu as pltpu
from jax.sharding import Mesh, PartitionSpec as P

EPSILON = 1e-05
F32 = jnp.float32
BF16 = jnp.bfloat16
MESH = pl.DeviceIdType.MESH
LIMIT = 58 * 1024 * 1024
ROLE = ("yy", "hh")
ALL = ("dp", "yy", "hh")


def split(v):
    high = v.astype(BF16)
    return high, (v - high.astype(F32)).astype(BF16)


def dot(a, b, ca, cb):
    return lax.dot_general(a, b, (((ca,), (cb,)), ((), ())), preferred_element_type=F32)


def dot3(a, b, ca=1, cb=0):
    (ah, al), (bh, bl) = a, b
    return dot(ah, bh, ca, cb) + dot(ah, bl, ca, cb) + dot(al, bh, ca, cb)


def sigmoid(v):
    return 0.5 * jnp.tanh(0.5 * v) + 0.5


def silu(v):
    return v * sigmoid(v)


def slope(v):
    s = sigmoid(v)
    return s * (1.0 + v * (1.0 - s))


def colsum(v):
    return jnp.sum(v, axis=0, keepdims=True)


def moments(total, squares, number):
    mean = total * (1.0 / number)
    return mean, lax.rsqrt(squares * (1.0 / number) - mean * mean + EPSILON)


def back_terms(gain, mean, inverse, up, upz, number):
    alpha = gain * inverse
    beta = -alpha * inverse * (upz * inverse) * (1.0 / number)
    return alpha, beta, -alpha * up * (1.0 / number) - beta * mean


def fold32(v):
    return v + pltpu.roll(v, 32, 1) + pltpu.roll(v, 64, 1) + pltpu.roll(v, 96, 1)


def fold128(v):
    return v[:, 0:128] + v[:, 128:256] + v[:, 256:384] + v[:, 384:512]


def four(v):
    return jnp.concatenate([v, v, v, v], axis=1)


def rows_of(ref, g):
    pixels, count, lanes = ref.shape
    return ref[:, pl.ds(g, count // 4, stride=4), :].reshape(pixels * (count // 4), lanes)


def frames_of(ref):
    return jnp.concatenate([rows_of(ref, g) for g in range(4)], axis=1)


def masked(v, mask):
    frames = mask.shape[0]
    lanes = v.shape[1] // mask.shape[1]
    wide = mask[...] if lanes == 1 else jnp.concatenate([mask[...]] * lanes, axis=1)
    return (v.reshape(-1, frames, v.shape[1]) * wide[None]).reshape(v.shape)


def edge(ref, v, at, frames):
    rows = v.shape[0]
    parts = []
    for k in range(v.shape[1] // 128):
        ref[k] = v[:, 128 * k : 128 * (k + 1)]
        parts.append(ref[k, pl.ds(at, rows // frames, stride=frames), :])
    return jnp.concatenate(parts, axis=1)


def edges(ref, v, frames):
    rows = v.shape[0]
    first, last = [], []
    for k in range(v.shape[1] // 128):
        ref[k] = v[:, 128 * k : 128 * (k + 1)]
        first.append(ref[k, pl.ds(0, rows // frames, stride=frames), :])
        last.append(ref[k, pl.ds(frames - 1, rows // frames, stride=frames), :])
    return jnp.concatenate(first, axis=1), jnp.concatenate(last, axis=1)


def shifted(ref, v, step, frames, beyond):
    rows = v.shape[0]
    at = 0 if step == 1 else frames - 1
    parts = []
    for k in range(v.shape[1] // 128):
        lanes = slice(128 * k, 128 * (k + 1))
        ref[k] = pltpu.roll(v[:, lanes], 1 if step == 1 else rows - 1, 0)
        ref[k, pl.ds(at, rows // frames, stride=frames), :] = beyond[:, lanes]
        parts.append(ref[k])
    return jnp.concatenate(parts, axis=1)


def add_rows(ref, *rows):
    @pl.when(pl.program_id(0) == 0)
    def _():
        ref[...] = jnp.zeros_like(ref)

    for k, row in enumerate(rows):
        ref[k : k + 1, :] += row


def add_whole(ref, value):
    @pl.when(pl.program_id(0) == 0)
    def _():
        ref[...] = jnp.zeros_like(ref)

    ref[...] += value


def vmem():
    return pl.BlockSpec(memory_space=pltpu.VMEM)


def shape(*dims, dtype=F32):
    return jax.ShapeDtypeStruct(dims, dtype)


def cost(flops, nbytes):
    return pl.CostEstimate(flops=int(2 * flops), bytes_accessed=int(2 * nbytes), transcendentals=0)


def whole(x):
    rank = len(x.shape)
    return pl.BlockSpec(tuple(x.shape), lambda i, *s: (0,) * rank)


def part(x, rows, at=None):
    tail = (0,) * (len(x.shape) - 1)
    where = at or (lambda i, *s: i)
    return pl.BlockSpec((rows,) + tuple(x.shape[1:]), lambda i, *s: (where(i, *s),) + tail)


def stepped(body, name, steps, scalars, ins, outs, scratch=(), est=None):
    return pl.pallas_call(
        body,
        name=name,
        out_shape=[o for o, _ in outs],
        grid_spec=pltpu.PrefetchScalarGridSpec(
            num_scalar_prefetch=len(scalars),
            grid=(steps,),
            in_specs=[s for _, s in ins],
            out_specs=[s for _, s in outs],
            scratch_shapes=list(scratch),
        ),
        compiler_params=pltpu.CompilerParams(vmem_limit_bytes=LIMIT),
        cost_estimate=est,
    )(*scalars, *[a for a, _ in ins])


def sum_kernel(sizes, axes, widths, edges, *refs):
    dps, ys, hs = sizes
    roles = ys * hs if axes == ROLE else hs
    parts = len(widths)
    xs, refs = refs[:parts], refs[parts:]
    edge_in, refs = refs[:edges], refs[edges:]
    outs, refs = refs[:parts], refs[parts:]
    edge_out, refs = refs[:edges], refs[edges:]
    one_src, two_src, b1, b2, s1, r1, s2, r2 = refs[:8]
    d = lax.axis_index("dp")
    y = lax.axis_index("yy")
    h = lax.axis_index("hh")
    m = y * hs + h

    def role(i):
        if axes != ROLE:
            return {"hh": lax.rem(h + i, hs)}
        p = lax.rem(m + i, roles)
        return {"yy": p // hs, "hh": lax.rem(p, hs)}

    def along(i):
        return {"dp": lax.rem(d + i, dps)}

    def send(src, dst, ssem, rsem, to):
        c = pltpu.make_async_remote_copy(
            src_ref=src, dst_ref=dst, send_sem=ssem, recv_sem=rsem, device_id=to, device_id_type=MESH
        )
        c.start()
        return c

    bar = pltpu.get_barrier_semaphore()
    for i in range(1, roles):
        pl.semaphore_signal(bar, inc=1, device_id=role(i), device_id_type=MESH)
    for i in range(1, dps):
        pl.semaphore_signal(bar, inc=1, device_id=along(i), device_id_type=MESH)
    one_src[...] = jnp.zeros_like(one_src)
    start = 0
    for x, width in zip(xs, widths):
        one_src[start : start + x.shape[0], 0:width] = x[...]
        start += x.shape[0]
    pl.semaphore_wait(bar, roles + dps - 2)
    one = [send(one_src, b1.at[i - 1], s1.at[i - 1], r1.at[i - 1], role(i)) for i in range(1, roles)]
    rim = []
    if edges:
        s3, r3 = refs[8:]
        rim = [
            send(edge_in[k], edge_out[k], s3.at[k], r3.at[k], along(1 if k == 0 else dps - 1))
            for k in range(edges)
        ]
    acc = one_src[...]
    for i, c in enumerate(one):
        c.wait_recv()
        acc = acc + b1[i]
    two_src[...] = acc
    two = [send(two_src, b2.at[i - 1], s2.at[i - 1], r2.at[i - 1], along(i)) for i in range(1, dps)]
    for i, c in enumerate(two):
        c.wait_recv()
        acc = acc + b2[i]
    start = 0
    for o, width in zip(outs, widths):
        o[...] = acc[start : start + o.shape[0], 0:width]
        start += o.shape[0]
    for c in rim:
        c.wait_recv()
    for c in one + rim + two:
        c.wait_send()


def total(xs, cid, sizes, axes, rims=()):
    dps, ys, hs = sizes
    roles = ys * hs if axes == ROLE else hs
    widths = [x.shape[1] for x in xs]
    packed = (sum(x.shape[0] for x in xs), max(widths))
    dma = pltpu.SemaphoreType.DMA
    return pl.pallas_call(
        functools.partial(sum_kernel, sizes, axes, widths, len(rims)),
        name="sum%d" % cid,
        out_shape=[shape(*x.shape) for x in xs] + [shape(*r.shape) for r in rims],
        in_specs=[vmem()] * (len(xs) + len(rims)),
        out_specs=[vmem()] * (len(xs) + len(rims)),
        scratch_shapes=[
            pltpu.VMEM(packed, F32),
            pltpu.VMEM(packed, F32),
            pltpu.VMEM((roles - 1,) + packed, F32),
            pltpu.VMEM((dps - 1,) + packed, F32),
            dma((roles - 1,)), dma((roles - 1,)), dma((dps - 1,)), dma((dps - 1,)),
        ] + ([dma((2,)), dma((2,))] if rims else []),
        compiler_params=pltpu.CompilerParams(collective_id=cid, has_side_effects=True),
    )(*xs, *rims)


def fast1_kernel(frames, idx, x_ref, rh, rl, p_ref, e0, e1, st, tmp):
    p = dot3(split(frames_of(x_ref)), (rh[...], rl[...]))
    p_ref[...] = p
    e0[0], e1[0] = edges(tmp, p, frames)
    add_rows(st, colsum(p), colsum(p * p))


def lateral_taps(frames, mask, x_ref, halo, bz):
    x = [rows_of(x_ref, g) for g in range(4)]
    beyond = jnp.concatenate([halo[:, 6, :], halo[:, 7, :]], axis=1)
    early = shifted(bz, jnp.concatenate([x[2], x[3]], axis=1), 1, frames, beyond)
    return jnp.concatenate([masked(early, mask), x[0], x[1], x[2]], axis=1)


def lateral_kernel(frames, idx, mask, x_ref, halo, wh, wl, s_ref, e0, st, bz):
    p = dot3(split(lateral_taps(frames, mask, x_ref, halo, bz)), (wh[...], wl[...]), 1, 1)
    s_ref[...] = p
    e0[0] = edge(bz, p, 0, frames)
    add_rows(st, colsum(p), colsum(p * p))


def fast_norm(tot, number):
    return moments(fold32(tot[0:1, :]), fold32(tot[1:2, :]), number)


def wide_norm(tot, number):
    return moments(fold128(tot[0:1, :]), fold128(tot[1:2, :]), number)


def rims_of(v, prev, nxt):
    lane = lax.broadcasted_iota(jnp.int32, v.shape, 1)
    return jnp.where(lane >= 96, prev, jnp.where(lane < 32, nxt, 0.0))


def fast2_kernel(
    number, frames, mp, mn, tot, gain, bias, p1, before, after, wh, wl, a_ref, z_ref, p2, st, zp, zn
):
    mean, inverse = fast_norm(tot, number)
    scale = gain[...] * inverse
    shift = bias[...] - mean * scale
    a = silu(p1[...] * scale + shift)
    a_ref[...] = a
    prev = shifted(zp, a, 1, frames, silu(before[0] * scale + shift))
    nxt = shifted(zn, a, -1, frames, silu(after[0] * scale + shift))
    z = rims_of(a, masked(prev, mp), masked(nxt, mn))
    z_ref[...] = z
    p = dot3(split(jnp.concatenate([a, z], axis=1)), (wh[...], wl[...]))
    p2[...] = p
    add_rows(st, colsum(p), colsum(p * p))


def fast3_kernel(number, tot, gain, bias, p2, eh, el, b_ref, st):
    mean, inverse = fast_norm(tot, number)
    scale = gain[...] * inverse
    b = silu(p2[...] * scale + (bias[...] - mean * scale))
    b_ref[...] = b
    p = dot3(split(b), (eh[...], el[...]))
    add_rows(st, colsum(p), colsum(p * p))


def put_frames(ref, v):
    pixels, count, lanes = ref.shape
    for g in range(4):
        ref[:, pl.ds(g, count // 4, stride=4), :] = v[:, lanes * g : lanes * (g + 1)].reshape(
            pixels, count // 4, lanes
        )


def fast4_kernel(number, share, idx, tot, gain, bias, x_ref, c_ref, b_ref, eh, el, o_ref, f_ref, u_ref, st):
    mean, inverse = wide_norm(tot, number)
    scale = gain[...] * inverse
    shift = bias[...] - mean * scale
    p = dot3(split(b_ref[...]), (eh[...], el[...]))
    j = p * four(scale) + four(shift) + frames_of(x_ref)
    s = sigmoid(j)
    out = j * s
    put_frames(o_ref, out)
    put_frames(f_ref, out)
    u = frames_of(c_ref) * (s * (1.0 + j * (1.0 - s)))
    u_ref[...] = u
    add_rows(st, share * colsum(u), share * colsum(u * (p - four(mean))))


def fast5_kernel(
    number, frames, tot, back, gain, tot2, gain2, bias2, u_ref, b_ref, p2, eh, el, u2, eg, e0, e1, st, tmp
):
    mean, inverse = wide_norm(tot, number)
    alpha, beta, gamma = back_terms(
        gain[...], mean, inverse, fold128(back[0:1, :]), fold128(back[1:2, :]), number
    )
    bs = split(b_ref[...])
    e = (eh[...], el[...])
    g = split(four(alpha) * u_ref[...] + four(beta) * dot3(bs, e) + four(gamma))
    add_whole(eg, dot3(bs, g, 0, 0))
    v = dot3(g, e, 1, 1)
    mean2, inverse2 = fast_norm(tot2, number)
    z = p2[...] - mean2
    u = v * slope(z * (inverse2 * gain2[...]) + bias2[...])
    u2[...] = u
    e0[0, 0], e1[0, 0] = edges(tmp, u, frames)
    e0[0, 1], e1[0, 1] = edges(tmp, p2[...], frames)
    add_rows(st, colsum(u), colsum(u * z))


def fast6_kernel(
    number, frames, mp, mn, tot2, back2, gain2, tot1, gain1, bias1, u2, p2, before, after, a, z, p1,
    wh, wl, u1, tg, st, zp, zn
):
    mean2, inverse2 = fast_norm(tot2, number)
    alpha, beta, gamma = back_terms(
        gain2[...], mean2, inverse2, fold32(back2[0:1, :]), fold32(back2[1:2, :]), number
    )
    g = alpha * u2[...] + beta * p2[...] + gamma
    prev = shifted(zp, g, 1, frames, alpha * before[0, 0] + beta * before[0, 1] + gamma)
    nxt = shifted(zn, g, -1, frames, alpha * after[0, 0] + beta * after[0, 1] + gamma)
    gz = rims_of(g, masked(prev, mp), masked(nxt, mn))
    add_whole(tg, dot3(split(jnp.concatenate([a[...], z[...]], axis=1)), split(g), 0, 0))
    v = dot3(split(jnp.concatenate([g, gz], axis=1)), (wh[...], wl[...]), 1, 1)
    mean1, inverse1 = fast_norm(tot1, number)
    c = p1[...] - mean1
    u = v * slope(c * (gain1[...] * inverse1) + bias1[...])
    u1[...] = u
    add_rows(st, colsum(u), colsum(u * c))


def fast7_kernel(number, idx, tot1, back1, gain1, x_ref, u1, p1, g1, rg):
    mean, inverse = fast_norm(tot1, number)
    alpha, beta, gamma = back_terms(
        gain1[...], mean, inverse, fold32(back1[0:1, :]), fold32(back1[1:2, :]), number
    )
    g = alpha * u1[...] + beta * p1[...] + gamma
    g1[...] = g
    add_whole(rg, dot3(split(frames_of(x_ref)), split(g), 0, 0))


def slow1_kernel(
    number, frames, idx, tot, gain, bias, x0, x1, x2, x3, side, rh, rl, sh, sl,
    first, short, jh, jl, e0, e1, st, wide, tmp
):
    lanes = x0.shape[1]
    for r, x in enumerate((x0, x1, x2, x3)):
        at = pl.multiple_of(idx[3 + r] * lanes, lanes)
        wide[:, pl.ds(at, lanes)] = x[...]
    mean, inverse = moments(tot[0:1, :], tot[1:2, :], number)
    scale = gain[...] * inverse
    top = sh.shape[0] * lanes
    wide[:, top:] = silu(side[...] * scale + (bias[...] - mean * scale))
    joined = split(wide[...])
    jh[0], jl[0] = joined
    p = dot3(joined, (rh[...], rl[...]), 1, 1)
    first[...] = p
    e0[0], e1[0] = edges(tmp, p, frames)
    sums = [colsum(p)]
    squares = [colsum(p * p)]
    for n in range(sh.shape[0]):
        p = dot3(joined, (sh[n], sl[n]))
        short[:, n * lanes : (n + 1) * lanes] = p
        sums.append(colsum(p))
        squares.append(colsum(p * p))
    add_rows(st, jnp.concatenate(sums, axis=1), jnp.concatenate(squares, axis=1))


def slow2_kernel(
    number, frames, mp, mn, tot, gain, bias, first, before, after, wh, wl, th, tl, pm, st, zp, zn
):
    width = gain.shape[1]
    mean, inverse = moments(tot[0:1, 0:width], tot[1:2, 0:width], number)
    scale = gain[...] * inverse
    shift = bias[...] - mean * scale
    a = silu(first[...] * scale + shift)
    prev = shifted(zp, a, 1, frames, silu(before[0] * scale + shift))
    nxt = shifted(zn, a, -1, frames, silu(after[0] * scale + shift))
    taps = split(jnp.concatenate([masked(prev, mp), a, masked(nxt, mn)], axis=1))
    th[0], tl[0] = taps
    p = dot3(taps, (wh[...], wl[...]), 1, 1)
    pm[...] = p
    add_rows(st, colsum(p), colsum(p * p))


def slow3_kernel(number, tot, gain, bias, pm, eh, el, bh, bl, st):
    mean, inverse = moments(tot[0:1, :], tot[1:2, :], number)
    scale = gain[...] * inverse
    b = split(silu(pm[...] * scale + (bias[...] - mean * scale)))
    bh[0], bl[0] = b
    p = dot3(b, (eh[...], el[...]))
    add_rows(st, colsum(p), colsum(p * p))


def slow4_kernel(
    number, idx, tot_l, tot_s, gain_l, bias_l, gain_s, bias_s, bh, bl, short, c0, c1, c2, c3, eh, el,
    o0, o1, o2, o3, u_ref, st, wide
):
    lanes = c0.shape[1]
    for r, c in enumerate((c0, c1, c2, c3)):
        at = pl.multiple_of(idx[3 + r] * lanes, lanes)
        wide[:, pl.ds(at, lanes)] = c[...]
    off = tot_s.shape[1] - short.shape[1]
    bs = (bh[0], bl[0])
    sums = []
    for n in range(short.shape[1] // lanes):
        at = slice(n * lanes, (n + 1) * lanes)
        mean_l, inv_l = moments(tot_l[0:1, at], tot_l[1:2, at], number)
        far = slice(off + n * lanes, off + (n + 1) * lanes)
        mean_s, inv_s = moments(tot_s[0:1, far], tot_s[1:2, far], number)
        zl = dot3(bs, (eh[:, at], el[:, at])) - mean_l
        zs = short[:, at] - mean_s
        j = zl * (inv_l * gain_l[:, at]) + zs * (inv_s * gain_s[:, at]) + (bias_l[:, at] + bias_s[:, at])
        s = sigmoid(j)
        u = wide[:, at] * (s * (1.0 + j * (1.0 - s)))
        u_ref[:, at] = u
        sums.append((colsum(u), colsum(u * zl), colsum(u * zs)))
        wide[:, at] = j * s
    for r, o in enumerate((o0, o1, o2, o3)):
        at = pl.multiple_of(idx[3 + r] * lanes, lanes)
        o[...] = wide[:, pl.ds(at, lanes)]
    add_rows(st, *[jnp.concatenate(rows, axis=1) for rows in zip(*sums)])


def slow5_kernel(
    number, frames, tot_l, back, gain_l, tot_m, gain_m, bias_m, u_ref, bh, bl, pm, eh, el,
    um, eg, e0, e1, st, tmp
):
    mean, inverse = moments(tot_l[0:1, :], tot_l[1:2, :], number)
    alpha, beta, gamma = back_terms(gain_l[...], mean, inverse, back[0:1, :], back[1:2, :], number)
    bs = (bh[0], bl[0])
    e = (eh[...], el[...])
    g = split(alpha * u_ref[...] + beta * dot3(bs, e) + gamma)
    add_whole(eg, dot3(bs, g, 0, 0))
    v = dot3(g, e, 1, 1)
    mean_m, inv_m = moments(tot_m[0:1, :], tot_m[1:2, :], number)
    z = pm[...] - mean_m
    u = v * slope(z * (inv_m * gain_m[...]) + bias_m[...])
    um[...] = u
    e0[0, 0], e1[0, 0] = edges(tmp, u, frames)
    e0[0, 1], e1[0, 1] = edges(tmp, pm[...], frames)
    add_rows(st, colsum(u), colsum(u * z))


def slow6_kernel(number, tot_s, back, gain_s, u_ref, short, jh, jl, sh, sl, dx, grads):
    off = tot_s.shape[1] - short.shape[1]
    mean, inverse = moments(tot_s[0:1, off:], tot_s[1:2, off:], number)
    alpha, beta, gamma = back_terms(gain_s[...], mean, inverse, back[0:1, :], back[2:3, :], number)
    lanes = sh.shape[2]
    joined = (jh[0], jl[0])

    @pl.when(pl.program_id(0) == 0)
    def _():
        grads[...] = jnp.zeros_like(grads)

    out = None
    for n in range(sh.shape[0]):
        at = slice(n * lanes, (n + 1) * lanes)
        g = split(alpha[:, at] * u_ref[:, at] + beta[:, at] * short[:, at] + gamma[:, at])
        grads[n] += dot3(joined, g, 0, 0)
        part = dot3(g, (sh[n], sl[n]), 1, 1)
        out = part if out is None else out + part
    dx[...] = out


def slow7_kernel(
    number, frames, mp, mn, tot_m, back, gain_m, tot_f, gain_f, bias_f, um, pm, before, after, th, tl,
    first, wh, wl, uf, tg, st, zp, zn
):
    mean, inverse = moments(tot_m[0:1, :], tot_m[1:2, :], number)
    alpha, beta, gamma = back_terms(gain_m[...], mean, inverse, back[0:1, :], back[1:2, :], number)
    g = alpha * um[...] + beta * pm[...] + gamma
    prev = shifted(zp, g, 1, frames, alpha * before[0, 0] + beta * before[0, 1] + gamma)
    nxt = shifted(zn, g, -1, frames, alpha * after[0, 0] + beta * after[0, 1] + gamma)
    gs = split(g)
    add_whole(tg, dot3(gs, (th[0], tl[0]), 0, 0))
    width = gain_f.shape[1]
    v = dot3(split(masked(nxt, mn)), (wh[:, 0:width], wl[:, 0:width]))
    v += dot3(gs, (wh[:, width : 2 * width], wl[:, width : 2 * width]))
    v += dot3(split(masked(prev, mp)), (wh[:, 2 * width :], wl[:, 2 * width :]))
    mean_f, inv_f = moments(tot_f[0:1, 0:width], tot_f[1:2, 0:width], number)
    z = first[...] - mean_f
    u = v * slope(z * (gain_f[...] * inv_f) + bias_f[...])
    uf[...] = u
    add_rows(st, colsum(u), colsum(u * z))


def slow8_kernel(
    number, frames, idx, tot_f, back, gain_f, tot_a, gain_a, bias_a, uf, first, jh, jl, dx, side,
    rh, rl, o0, o1, o2, o3, us, rg, e0, st, wide, tmp
):
    width = gain_f.shape[1]
    mean, inverse = moments(tot_f[0:1, 0:width], tot_f[1:2, 0:width], number)
    alpha, beta, gamma = back_terms(gain_f[...], mean, inverse, back[0:1, :], back[1:2, :], number)
    g = split(alpha * uf[...] + beta * first[...] + gamma)
    add_whole(rg, dot3(g, (jh[0], jl[0]), 0, 0))
    lanes = o0.shape[1]
    wide[...] = dx[...] + dot3(g, (rh[...], rl[...]))
    for r, o in enumerate((o0, o1, o2, o3)):
        at = pl.multiple_of(idx[3 + r] * lanes, lanes)
        o[...] = wide[:, pl.ds(at, lanes)]
    mean_a, inv_a = moments(tot_a[0:1, :], tot_a[1:2, :], number)
    z = side[...] - mean_a
    top = wide.shape[1] - width
    u = wide[:, top:] * slope(z * (inv_a * gain_a[...]) + bias_a[...])
    us[...] = u
    e0[0] = edge(tmp, u, 0, frames)
    add_rows(st, colsum(u), colsum(u * z))


def side_terms(number, tot_a, back, gain_a):
    mean, inverse = moments(tot_a[0:1, :], tot_a[1:2, :], number)
    return back_terms(gain_a[...], mean, inverse, back[0:1, :], back[1:2, :], number)


def slow9_kernel(number, frames, idx, mask, tot_a, back, gain_a, us, side, x_ref, halo, lg, bz):
    alpha, beta, gamma = side_terms(number, tot_a, back, gain_a)
    g = split(alpha * us[...] + beta * side[...] + gamma)
    add_whole(lg, dot3(g, split(lateral_taps(frames, mask, x_ref, halo, bz)), 0, 0))


def last_kernel(
    number, frames, idx, mask, tot_a, back, gain_a, us, side, us_edge, side_edge, u3, g1, wh, wl,
    rh, rl, o_ref, f_ref, zn
):
    alpha, beta, gamma = side_terms(number, tot_a, back, gain_a)
    here = alpha * us[...] + beta * side[...] + gamma
    after = shifted(zn, here, -1, frames, alpha * us_edge[0] + beta * side_edge[0] + gamma)
    base = u3[...] + dot3(split(g1[...]), (rh[...], rl[...]), 1, 1)
    near = dot3(split(here), (wh[:, 256:], wl[:, 256:]))
    far = dot3(split(masked(after, mask)), (wh[:, 0:256], wl[:, 0:256]))
    both = jnp.concatenate(
        [near[:, 0:256], near[:, 256:384] + far[:, 0:128], far[:, 128:256]], axis=1
    )
    out = base + both
    put_frames(o_ref, out)
    put_frames(f_ref, out)


def weight_split(w):
    high = lax.reduce_precision(w, 8, 7)
    return high.astype(BF16), (w - high).astype(BF16)


def row(v):
    return v.reshape(1, -1)


def tiled_row(v):
    return jnp.tile(v.reshape(1, -1), (1, 4))


def by_pixel(v):
    return v.transpose(1, 0, 2)


def after(value, *events):
    return lax.optimization_barrier((value,) + events)[0]


def local(sizes, *args):
    (
        slow_input, fast_input, clip_starts,
        fast_reduce, fast_reduce_gain, fast_reduce_bias,
        fast_temporal, fast_temporal_gain, fast_temporal_bias,
        fast_expand, fast_expand_gain, fast_expand_bias,
        lateral_conv, lateral_gain, lateral_bias,
        slow_reduce, slow_reduce_gain, slow_reduce_bias,
        slow_temporal, slow_temporal_gain, slow_temporal_bias,
        slow_expand, slow_expand_gain, slow_expand_bias,
        shortcut_conv, shortcut_gain, shortcut_bias,
        slow_cotangent, fast_cotangent,
    ) = args
    dps, ys, hs = sizes
    roles = ys * hs
    d, y, h = (lax.axis_index(a) for a in ALL)
    m = y * hs + h
    frames, pixels, lanes = slow_input.shape
    shard_rows = slow_reduce.shape[1]
    inner = shard_rows * roles
    joined_width = slow_reduce.shape[0]
    wide = lanes * roles
    number = frames * dps * pixels
    fast_number = number * 4
    half = pixels // hs
    own = pixels // roles
    steps = 7
    half_block, own_block = half // steps, own // steps
    fast_rows, slow_rows = half_block * frames, own_block * frames

    slow_x = by_pixel(slow_input).reshape(pixels * frames, lanes)
    slow_c = by_pixel(slow_cotangent).reshape(pixels * frames, lanes)
    fast_x = by_pixel(fast_input)
    fast_c = by_pixel(fast_cotangent)

    def block_of(p):
        return (p % hs) * ys + p // hs

    def role_xor(r):
        return (y ^ (r // hs)) * hs + (h ^ (r % hs))

    peers = [role_xor(r) for r in range(roles)]
    q = block_of(m)
    idx = jnp.stack([h, q, y] + peers).astype(jnp.int32)
    own_rows = own * frames
    row_at = [own_rows * block_of(p) for p in peers]

    times = d * frames + jnp.arange(0, frames + 1, dtype=jnp.int32)

    def clip_of(t):
        return jnp.sum((clip_starts[None, :] <= t[:, None]).astype(jnp.int32), axis=1) - 1

    same = jnp.logical_and(
        clip_of(times) == clip_of(times - 1), jnp.logical_and(times >= 1, times < frames * dps)
    ).astype(F32)
    mask_prev = jnp.broadcast_to(same[:frames, None], (frames, 128))
    mask_next = jnp.broadcast_to(same[1:, None], (frames, 128))

    def role_pairs(r):
        return [(i, i ^ r) for i in range(roles)]

    def placed(out, got):
        for r in range(1, roles):
            out = lax.dynamic_update_slice_in_dim(out, got[r - 1], row_at[r], axis=0)
        return by_pixel(out.reshape(pixels, frames, lanes))

    swap = [(0, 1), (1, 0)]
    half_rows = half * frames

    def from_core(array):
        return lax.ppermute(
            lax.dynamic_slice_in_dim(array, half_rows * (1 - h), half_rows, axis=0), "hh", swap
        )

    def for_partner(array, here):
        return [
            lax.dynamic_slice_in_dim(array, half_rows * h + own_rows * (1 - y), own_rows, axis=0),
            lax.dynamic_slice_in_dim(here, own_rows * (1 - y), own_rows, axis=0),
        ]

    sho_y = lax.ppermute(shortcut_conv, "yy", swap)
    in_core = from_core(slow_x)
    in_send = jnp.concatenate(for_partner(slow_x, in_core), axis=0)
    in_y = lax.ppermute(in_send, "yy", swap)
    sho_core = jnp.stack([shortcut_conv, sho_y])
    sho_other = lax.ppermute(sho_core, "hh", swap)
    sho_all = jnp.stack([sho_core[0], sho_other[0], sho_core[1], sho_other[1]])
    sho_h, sho_l = weight_split(
        jnp.stack([lax.dynamic_index_in_dim(sho_all, p, 0, keepdims=False) for p in peers])
    )

    vectors = [
        lateral_gain, lateral_bias, slow_reduce_gain, slow_reduce_bias, slow_temporal_gain,
        slow_temporal_bias, slow_expand_gain, slow_expand_bias, shortcut_gain, shortcut_bias,
    ]
    vector = jnp.concatenate(vectors)
    across = -(-vector.shape[0] // (shard_rows * 128)) * 128
    vector = jnp.pad(vector, (0, shard_rows * across - vector.shape[0])).reshape(shard_rows, across)
    piece = jnp.concatenate([lateral_conv.transpose(2, 0, 1).reshape(shard_rows, -1), vector], axis=1)
    column = jnp.stack([piece, lax.ppermute(piece, "yy", swap)])
    other = lax.ppermute(column, "hh", swap)
    table = jnp.stack([column[0], other[0], column[1], other[1]])
    table = jnp.stack([lax.dynamic_index_in_dim(table, p, 0, keepdims=False) for p in peers])
    taps = lateral_conv.shape[0] * lateral_conv.shape[1]
    lat_h, lat_l = weight_split(table[:, :, 0:taps].reshape(inner, taps))
    vector = table[:, :, taps:].reshape(roles, -1)
    share = shard_rows // dps
    piece = jnp.concatenate(
        [slow_reduce.T, slow_temporal.transpose(2, 0, 1).reshape(shard_rows, -1), slow_expand], axis=1
    )
    piece = lax.dynamic_slice_in_dim(piece, d * share, share, axis=0)
    got = lax.all_gather(piece, ALL, axis=0, tiled=False).reshape((dps, roles) + piece.shape)
    matrix = got.transpose(1, 0, 2, 3).reshape(inner, -1)
    bounds = [0, joined_width, joined_width + 3 * inner, joined_width + 3 * inner + wide]
    (red_h, red_l), (tem_h, tem_l), (exp_h, exp_l) = [
        weight_split(matrix[:, bounds[k] : bounds[k + 1]]) for k in range(3)
    ]
    full = []
    start = 0
    for v in vectors:
        full.append(vector[:, start : start + v.shape[0]].reshape(1, -1))
        start += v.shape[0]
    (
        lat_gain, lat_bias, red_gain, red_bias, tem_gain, tem_bias, exp_gain, exp_bias, sho_gain, sho_bias
    ) = full

    eye = jnp.eye(4, dtype=F32)
    up = jnp.eye(4, k=1, dtype=F32)
    down = jnp.eye(4, k=-1, dtype=F32)
    far_next = jnp.eye(4, k=3, dtype=F32)
    far_prev = jnp.eye(4, k=-3, dtype=F32)
    fr_h, fr_l = weight_split(after(jnp.kron(eye, fast_reduce), in_send))
    fe_h, fe_l = weight_split(jnp.kron(eye, fast_expand))
    centre = jnp.kron(eye, fast_temporal[1]) + jnp.kron(up, fast_temporal[0]) + jnp.kron(down, fast_temporal[2])
    outer = jnp.kron(far_next, fast_temporal[2]) + jnp.kron(far_prev, fast_temporal[0])
    ft_h, ft_l = weight_split(jnp.concatenate([centre, outer], axis=0))
    fb_h, fb_l = weight_split(jnp.concatenate([centre, outer], axis=1))
    fr_gain, fr_bias = tiled_row(fast_reduce_gain), tiled_row(fast_reduce_bias)
    ft_gain, ft_bias = tiled_row(fast_temporal_gain), tiled_row(fast_temporal_bias)
    fe_gain, fe_bias = row(fast_expand_gain), row(fast_expand_bias)

    forth = [(i, i + 1) for i in range(dps - 1)]
    backw = [(i + 1, i) for i in range(dps - 1)]
    halo = lax.dynamic_slice(fast_x, (half * h, frames * 4 - 8, 0), (half, 8, 128))
    halo = lax.ppermute(halo, "dp", forth)

    in_half = lambda i, s, *_: s[0] * steps + i
    in_own = lambda i, s, *_: s[1] * steps + i
    own_in_half = lambda i, s, *_: s[2] * steps + i

    def all_of(*arrays):
        return [(x, whole(x)) for x in arrays]

    def const(*dims):
        o = shape(*dims)
        return (o, whole(o))

    def by_block(x, at=None):
        return (x, part(x, x.shape[0] // steps, at))

    def out_rows(rows, width):
        return by_block(shape(rows * steps, width))

    def out_blocks(*dims, dtype=F32):
        return by_block(shape(steps, *dims, dtype=dtype))

    def tmp(*dims):
        return pltpu.VMEM(dims, F32)

    def cut(rows, width):
        return tmp(width // 128, rows, 128)

    other_y = lambda i, s, *_: (1 - s[2]) * steps + i

    fr, sr = fast_rows, slow_rows
    nf, ns = fr * steps, sr * steps
    fx = (fast_x, part(fast_x, half_block, in_half))
    fc = (fast_c, part(fast_c, half_block, in_half))
    masks = all_of(mask_prev, mask_next)
    core = ("hh",)

    p1, e0, e1, st = stepped(
        functools.partial(fast1_kernel, frames), "fast1", steps, [idx], [fx] + all_of(fr_h, fr_l),
        [out_rows(fr, 128), out_blocks(half_block, 128), out_blocks(half_block, 128), const(2, 128)],
        scratch=[cut(fr, 128)],
        est=cost(2 * 3 * nf * 512 * 256, nf * 640 * 4),
    )
    tot_f1, before, beyond = total([st], 1, sizes, core, (e1, e0))
    a1, z1, p2, st = stepped(
        functools.partial(fast2_kernel, fast_number, frames), "fast2", steps, [],
        masks + all_of(tot_f1, fr_gain, fr_bias)
        + [by_block(p1), by_block(before), by_block(beyond)] + all_of(ft_h, ft_l),
        [out_rows(fr, 128)] * 3 + [const(2, 128)],
        scratch=[cut(fr, 128)] * 2,
        est=cost(2 * 3 * nf * 256 * 256, 4 * nf * 128 * 4),
    )
    (tot_f2,) = total([st], 2, sizes, core)
    cot_core = from_core(after(slow_c, tot_f1))
    slow_cot = [cot_core] + [
        lax.all_gather(after(v, matrix), "yy", axis=0, tiled=True) for v in for_partner(slow_c, cot_core)
    ]
    side, side_edge, st_a = stepped(
        functools.partial(lateral_kernel, frames), "lateral", steps, [idx],
        all_of(mask_prev) + [fx, by_block(halo)] + all_of(after(lat_h, st), lat_l),
        [out_rows(fr, inner), out_blocks(half_block, inner), const(2, inner)],
        scratch=[cut(fr, 256)],
        est=cost(2 * 3 * nf * 768 * 256, nf * 768 * 4),
    )
    side_edge = lax.ppermute(side_edge, "dp", backw)
    b1, st = stepped(
        functools.partial(fast3_kernel, fast_number), "fast3", steps, [],
        all_of(tot_f2, ft_gain, ft_bias) + [by_block(p2)] + all_of(fe_h, fe_l),
        [out_rows(fr, 128), const(2, 512)],
        est=cost(2 * 3 * nf * 256 * 512, 2 * nf * 128 * 4),
    )
    tot_f3, tot_a = total([st, st_a], 3, sizes, core)
    half_out = shape(half, frames * 4, 128)
    full_out = shape(pixels, frames * 4, 128)
    fast_half, fast_full, u3, st_f4 = stepped(
        functools.partial(fast4_kernel, fast_number, 1.0 / ys), "fast4", steps, [idx],
        all_of(tot_f3, fe_gain, fe_bias) + [fx, fc, by_block(b1)] + all_of(fe_h, fe_l),
        [by_block(half_out), (full_out, part(full_out, half_block, in_half)), out_rows(fr, 512), const(2, 512)],
        est=cost(2 * 3 * nf * 256 * 512, nf * 5 * 512 * 4),
    )

    side_own = (side, part(side, slow_rows, own_in_half))
    sx = (slow_x, part(slow_x, slow_rows, in_own))
    sc = (slow_c, part(slow_c, slow_rows, in_own))
    bf_joined = out_blocks(sr, joined_width, dtype=BF16)
    first, short, jh, jl, e0, e1, st = stepped(
        functools.partial(slow1_kernel, number, frames), "slow1", steps, [idx],
        all_of(after(tot_a, st_f4), lat_gain, lat_bias) + [sx, (in_core, part(in_core, slow_rows, own_in_half))]
        + [(in_y, part(in_y, slow_rows, at)) for at in (lambda i, *s: i, lambda i, *s: steps + i)]
        + [side_own]
        + all_of(red_h, red_l, sho_h, sho_l),
        [
            out_rows(sr, inner), out_rows(sr, wide), bf_joined, bf_joined,
            out_blocks(own_block, inner), out_blocks(own_block, inner), const(2, inner + wide),
        ],
        scratch=[tmp(sr, joined_width), cut(sr, inner)],
        est=cost(2 * 3 * ns * 1280 * 1280, ns * 4 * 3840 + 7e6),
    )
    tot_s, back_f3, before, beyond = total([st, st_f4], 8, sizes, ROLE, (e1, e0))
    bf_taps = out_blocks(sr, 3 * inner, dtype=BF16)
    wide_masks = all_of(*[jnp.concatenate([v, v], axis=1) for v in (mask_prev, mask_next)])
    th, tl, pm, st = stepped(
        functools.partial(slow2_kernel, number, frames), "slow2", steps, [],
        wide_masks + all_of(tot_s, red_gain, red_bias) + [by_block(x) for x in (first, before, beyond)]
        + all_of(tem_h, tem_l),
        [bf_taps, bf_taps, out_rows(sr, inner), const(2, inner)],
        scratch=[cut(sr, inner)] * 2,
        est=cost(2 * 3 * ns * 768 * 256, ns * 4 * 1500),
    )
    (tot_m,) = total([st], 9, sizes, ROLE)
    bf_mid = out_blocks(sr, inner, dtype=BF16)
    bh, bl, st = stepped(
        functools.partial(slow3_kernel, number), "slow3", steps, [],
        all_of(tot_m, tem_gain, tem_bias) + [by_block(pm)] + all_of(exp_h, exp_l),
        [bf_mid, bf_mid, const(2, wide)],
        est=cost(2 * 3 * ns * 1024 * 256, ns * 4 * 512),
    )
    (tot_l,) = total([st], 10, sizes, ROLE)
    slow_full = shape(pixels * frames, lanes)
    own_out = (slow_full, part(slow_full, slow_rows, in_own))
    *outs, u, st = stepped(
        functools.partial(slow4_kernel, number), "slow4", steps, [idx],
        all_of(tot_l, tot_s, exp_gain, exp_bias, sho_gain, sho_bias)
        + [by_block(x) for x in (bh, bl, short)] + [sc]
        + [(slow_cot[0], part(slow_cot[0], slow_rows, own_in_half))]
        + [(x, part(x, slow_rows, other_y)) for x in slow_cot[1:]]
        + all_of(exp_h, exp_l),
        [own_out] + [out_rows(sr, lanes)] * (roles - 1) + [out_rows(sr, wide), const(4, wide)],
        scratch=[tmp(sr, wide)],
        est=cost(2 * 3 * ns * 1024 * 256, ns * 4 * 4352),
    )
    (back_ls,) = total([st], 11, sizes, ROLE)
    sent = [lax.ppermute(after(outs[r], back_ls), ROLE, role_pairs(r)) for r in range(1, roles)]

    dx, short_grads = stepped(
        functools.partial(slow6_kernel, number), "slow6", steps, [],
        all_of(tot_s, back_ls, sho_gain) + [by_block(x) for x in (u, short, jh, jl)] + all_of(sho_h, sho_l),
        [out_rows(sr, joined_width), const(roles, joined_width, lanes)],
        est=cost(2 * 6 * ns * 1280 * 1024, ns * 4 * 4600 + 12e6),
    )
    um, expand_grad, e0, e1, st = stepped(
        functools.partial(slow5_kernel, number, frames), "slow5", steps, [],
        all_of(tot_l, after(back_ls, dx), exp_gain, tot_m, tem_gain, tem_bias)
        + [by_block(x) for x in (u, bh, bl, pm)] + all_of(exp_h, exp_l),
        [
            out_rows(sr, inner), const(inner, wide), out_blocks(2, own_block, inner),
            out_blocks(2, own_block, inner), const(2, inner),
        ],
        scratch=[cut(sr, inner)],
        est=cost(2 * 9 * ns * 1024 * 256, ns * 4 * 1800),
    )
    slow_output = placed(outs[0], sent)
    back_m, before, beyond = total([after(st, *sent)], 12, sizes, ROLE, (e1, e0))
    def by_peer(g):
        rows = g.shape[0] // roles
        parts = [lax.dynamic_slice_in_dim(g, p * rows, rows, axis=0) for p in peers]
        return jnp.stack([parts[0], parts[2]]), jnp.stack([parts[1], parts[3]])

    def chip_sum(near, far):
        return near + lax.ppermute(far, "hh", swap)

    near, far = by_peer(short_grads.reshape(roles * joined_width, lanes))
    short_both = chip_sum(near, after(far, back_m))
    short_got = lax.all_gather(short_both[1], "yy", axis=0, tiled=False)
    uf, temporal_grad, st = stepped(
        functools.partial(slow7_kernel, number, frames), "slow7", steps, [],
        wide_masks + all_of(tot_m, back_m, tem_gain, tot_s, red_gain, red_bias)
        + [by_block(x) for x in (um, pm, before, beyond, th, tl, first)] + all_of(tem_h, tem_l),
        [out_rows(sr, inner), const(inner, 3 * inner), const(2, inner)],
        scratch=[cut(sr, inner)] * 2,
        est=cost(2 * 6 * ns * 768 * 256, ns * 4 * 1500),
    )
    (back_f,) = total([st], 13, sizes, ROLE)
    *outs, us, reduce_grad, us_edge, st = stepped(
        functools.partial(slow8_kernel, number, frames), "slow8", steps, [idx],
        all_of(tot_s, back_f, red_gain, tot_a, lat_gain, lat_bias)
        + [by_block(x) for x in (uf, first, jh, jl, dx)] + [side_own] + all_of(red_h, red_l),
        [own_out] + [out_rows(sr, lanes)] * (roles - 1)
        + [out_rows(sr, inner), const(inner, joined_width), out_blocks(own_block, inner), const(2, inner)],
        scratch=[tmp(sr, joined_width), cut(sr, inner)],
        est=cost(2 * 6 * ns * 1280 * 256, ns * 4 * 5000),
    )
    (back_a,) = total([after(st, short_got)], 14, sizes, ROLE)
    shortcut_sum = lax.psum(
        short_both[0] + lax.dynamic_index_in_dim(short_got, 1 - y, 0, keepdims=False), "dp"
    )
    us_sent = after(us, back_a)
    us_other = lax.ppermute(us_sent, "yy", swap)
    edge_sent = after(us_edge, back_a)
    edge_same = lax.ppermute(edge_sent, "dp", backw)
    edge_cross = lax.ppermute(
        edge_sent, ("dp", "yy"), [(i * ys + j, (i - 1) * ys + 1 - j) for i in range(1, dps) for j in range(ys)]
    )

    own_halo = (halo, part(halo, own_block, own_in_half))
    (lateral_grad,) = stepped(
        functools.partial(slow9_kernel, number, frames), "slow9", steps, [idx],
        all_of(mask_prev, tot_a, back_a, lat_gain)
        + [by_block(us), side_own, (fast_x, part(fast_x, own_block, in_own)), own_halo],
        [const(inner, 640)],
        scratch=[cut(sr, 256)],
        est=cost(2 * 3 * ns * 640 * 256, ns * 4 * 1500),
    )

    both = chip_sum(*by_peer(jnp.concatenate([reduce_grad, temporal_grad, expand_grad, lateral_grad], axis=1)))
    rest = both[0] + lax.ppermute(both[1], "yy", swap)
    grads_sent = [
        lax.ppermute(after(outs[r], back_a if r == 1 else both), ROLE, role_pairs(r))
        for r in range(1, roles)
    ]
    slow_input_gradient = placed(outs[0], grads_sent)

    u2, expand_packed, e0, e1, st = stepped(
        functools.partial(fast5_kernel, fast_number, frames), "fast5", steps, [],
        all_of(tot_f3, after(back_f3, back_a, lateral_grad), fe_gain, tot_f2, ft_gain, ft_bias)
        + [by_block(u3), by_block(b1), by_block(p2)] + all_of(fe_h, fe_l),
        [
            out_rows(fr, 128), const(128, 512), out_blocks(2, half_block, 128),
            out_blocks(2, half_block, 128), const(2, 128),
        ],
        scratch=[cut(fr, 128)],
        est=cost(2 * 9 * nf * 256 * 512, nf * 900 * 4),
    )
    back_f2, before, beyond = total([after(st, us_other)], 5, sizes, core, (e1, e0))
    u1, temporal_packed, st = stepped(
        functools.partial(fast6_kernel, fast_number, frames), "fast6", steps, [],
        masks + all_of(tot_f2, back_f2, ft_gain, tot_f1, fr_gain, fr_bias)
        + [by_block(x) for x in (u2, p2, before, beyond, a1, z1, p1)] + all_of(fb_h, fb_l),
        [out_rows(fr, 128), const(256, 128), const(2, 128)],
        scratch=[cut(fr, 128)] * 2,
        est=cost(2 * 6 * nf * 256 * 256, 6 * nf * 128 * 4),
    )
    (back_f1,) = total([st], 6, sizes, core)
    g1, reduce_packed = stepped(
        functools.partial(fast7_kernel, fast_number), "fast7", steps, [idx],
        all_of(tot_f1, back_f1, fr_gain) + [fx, by_block(u1), by_block(p1)],
        [out_rows(fr, 128), const(512, 128)],
        est=cost(2 * 3 * nf * 512 * 256, nf * 900 * 4),
    )

    def in_order(mine, other):
        return jnp.concatenate([jnp.where(y == 0, mine, other), jnp.where(y == 0, other, mine)], axis=0)

    us_half = in_order(us, us_other)
    rim = in_order(edge_same.reshape(own, inner), edge_cross.reshape(own, inner))
    grad_half, grad_full = stepped(
        functools.partial(last_kernel, number, frames), "last", steps, [idx],
        all_of(mask_next, tot_a, after(back_a, rest, grads_sent[1], shortcut_sum), lat_gain)
        + [by_block(x) for x in (us_half, side, rim.reshape(steps, half_block, inner), side_edge, u3, g1)]
        + all_of(lat_h, lat_l, fr_h, fr_l),
        [by_block(half_out), (full_out, part(full_out, half_block, in_half))],
        scratch=[cut(fr, inner)],
        est=cost(2 * 3 * nf * 1024 * 256, nf * 4 * 2000),
    )

    def fast_whole(mine, full):
        got = lax.ppermute(mine, "hh", swap)
        return by_pixel(lax.dynamic_update_slice_in_dim(full, got, half * (1 - h), axis=0))

    fast_output = fast_whole(fast_half, fast_full)
    fast_input_gradient = fast_whole(grad_half, grad_full)

    rest = lax.psum(after(rest, shortcut_sum), "dp")
    reduce_sum = rest[:, 0:joined_width].T
    expand_sum = rest[:, joined_width + 3 * inner : joined_width + 3 * inner + wide]
    lateral_sum = rest[:, joined_width + 3 * inner + wide :].reshape(shard_rows, -1, 128).transpose(1, 2, 0)
    temporal_sum = rest[:, joined_width : joined_width + 3 * inner].reshape(shard_rows, 3, inner).transpose(1, 2, 0)

    eb = expand_packed.reshape(4, 32, 4, 128)
    expand_small = eb[0, :, 0] + eb[1, :, 1] + eb[2, :, 2] + eb[3, :, 3]
    rb = reduce_packed.reshape(4, 128, 4, 32)
    reduce_small = rb[0, :, 0] + rb[1, :, 1] + rb[2, :, 2] + rb[3, :, 3]
    tb = temporal_packed.reshape(8, 32, 4, 32)
    tap0 = tb[0, :, 1] + tb[1, :, 2] + tb[2, :, 3] + tb[7, :, 0]
    tap1 = tb[0, :, 0] + tb[1, :, 1] + tb[2, :, 2] + tb[3, :, 3]
    tap2 = tb[1, :, 0] + tb[2, :, 1] + tb[3, :, 2] + tb[4, :, 3]
    small = jnp.concatenate(
        [expand_small, reduce_small.reshape(32, 128), jnp.stack([tap0, tap1, tap2]).reshape(24, 128)], axis=0
    )
    (small,) = total([small], 15, sizes, core)

    def fold(v):
        return jnp.sum(v.reshape(4, -1), axis=0)

    def zhat(back, tot, n, row_at=1, off=0):
        mean = tot[0, off:] / n
        return back[row_at] * lax.rsqrt(tot[1, off:] / n - mean * mean + EPSILON)

    def fast_pair(back, tot):
        sums = jnp.sum(tot.reshape(2, 4, -1), axis=1)
        bias = fold(back[0])
        mean = sums[0] / fast_number
        return fold(back[1]) * lax.rsqrt(sums[1] / fast_number - mean * mean + EPSILON), bias

    def shard(v):
        size = v.shape[0] // roles
        return lax.dynamic_slice_in_dim(v, m * size, size, axis=0)

    def slow_pair(back, tot, n=number, row_at=1, off=0, width=None):
        tot = tot[:, : width] if width else tot
        return shard(zhat(back, tot, n, row_at, off)), shard(back[0])

    fr_gg, fr_bg = fast_pair(back_f1, tot_f1)
    ft_gg, ft_bg = fast_pair(back_f2, tot_f2)
    fe_gg, fe_bg = fast_pair(back_f3, tot_f3)
    la_gg, la_bg = slow_pair(back_a, tot_a, number)
    re_gg, re_bg = slow_pair(back_f, tot_s, width=inner)
    te_gg, te_bg = slow_pair(back_m, tot_m)
    ex_gg, ex_bg = slow_pair(back_ls, tot_l)
    sh_gg, sh_bg = slow_pair(back_ls, tot_s, row_at=2, off=inner)
    return (
        slow_output, fast_output, slow_input_gradient, fast_input_gradient,
        small[32:64].reshape(128, 32), fr_gg, fr_bg,
        small[64:88].reshape(3, 32, 32), ft_gg, ft_bg,
        small[0:32], fe_gg, fe_bg,
        lateral_sum, la_gg, la_bg,
        reduce_sum, re_gg, re_bg,
        temporal_sum, te_gg, te_bg,
        expand_sum, ex_gg, ex_bg,
        shortcut_sum, sh_gg, sh_bg,
    )


def solution(mesh):
    dps, roles = mesh.shape["dp"], mesh.shape["mp"]
    sizes = (dps, roles // 2, 2)
    fine = Mesh(mesh.devices.reshape(sizes), ALL)
    mp = ROLE
    frames3 = P("dp", None, mp)
    fast3 = P("dp", None, None)
    none = P()
    in_specs = (
        (frames3, fast3) + (none,) * 10
        + (P(None, None, mp), P(mp), P(mp), P(None, mp), P(mp), P(mp), P(None, None, mp), P(mp), P(mp),
           P(mp, None), P(mp), P(mp), P(None, mp), P(mp), P(mp), frames3, fast3)
    )
    out_specs = (
        (frames3, fast3, frames3, fast3) + (none,) * 9
        + (P(None, None, mp), P(mp), P(mp), P(None, mp), P(mp), P(mp), P(None, None, mp), P(mp), P(mp),
           P(mp, None), P(mp), P(mp), P(None, mp), P(mp), P(mp))
    )
    return jax.shard_map(
        functools.partial(local, sizes), mesh=fine, in_specs=in_specs, out_specs=out_specs, check_vma=False
    )
```

```python
import functools

import jax
import jax.numpy as jnp
from jax import lax
from jax.experimental import pallas as pl
from jax.experimental.pallas import tpu as pltpu
from jax.sharding import Mesh, PartitionSpec as P

EPSILON = 1e-05
F32 = jnp.float32
BF16 = jnp.bfloat16
MESH = pl.DeviceIdType.MESH
LIMIT = 58 * 1024 * 1024
ROLE = ("yy", "hh")
ALL = ("dp", "yy", "hh")


def split(v):
    high = v.astype(BF16)
    return high, (v - high.astype(F32)).astype(BF16)


def dot(a, b, ca, cb):
    return lax.dot_general(a, b, (((ca,), (cb,)), ((), ())), preferred_element_type=F32)


def dot3(a, b, ca=1, cb=0):
    (ah, al), (bh, bl) = a, b
    return dot(ah, bh, ca, cb) + dot(ah, bl, ca, cb) + dot(al, bh, ca, cb)


def sigmoid(v):
    return 0.5 * jnp.tanh(0.5 * v) + 0.5


def silu(v):
    return v * sigmoid(v)


def slope(v):
    s = sigmoid(v)
    return s * (1.0 + v * (1.0 - s))


def colsum(v):
    return jnp.sum(v, axis=0, keepdims=True)


def moments(total, squares, number):
    mean = total * (1.0 / number)
    return mean, lax.rsqrt(squares * (1.0 / number) - mean * mean + EPSILON)


def back_terms(gain, mean, inverse, up, upz, number):
    alpha = gain * inverse
    beta = -alpha * inverse * (upz * inverse) * (1.0 / number)
    return alpha, beta, -alpha * up * (1.0 / number) - beta * mean


def fold32(v):
    return v + pltpu.roll(v, 32, 1) + pltpu.roll(v, 64, 1) + pltpu.roll(v, 96, 1)


def fold128(v):
    return v[:, 0:128] + v[:, 128:256] + v[:, 256:384] + v[:, 384:512]


def four(v):
    return jnp.concatenate([v, v, v, v], axis=1)


def rows_of(ref, g):
    pixels, count, lanes = ref.shape
    return ref[:, pl.ds(g, count // 4, stride=4), :].reshape(pixels * (count // 4), lanes)


def frames_of(ref):
    return jnp.concatenate([rows_of(ref, g) for g in range(4)], axis=1)


def masked(v, mask):
    frames = mask.shape[0]
    lanes = v.shape[1] // mask.shape[1]
    wide = mask[...] if lanes == 1 else jnp.concatenate([mask[...]] * lanes, axis=1)
    return (v.reshape(-1, frames, v.shape[1]) * wide[None]).reshape(v.shape)


def edge(ref, v, at, frames):
    rows = v.shape[0]
    parts = []
    for k in range(v.shape[1] // 128):
        ref[k] = v[:, 128 * k : 128 * (k + 1)]
        parts.append(ref[k, pl.ds(at, rows // frames, stride=frames), :])
    return jnp.concatenate(parts, axis=1)


def edges(ref, v, frames):
    rows = v.shape[0]
    first, last = [], []
    for k in range(v.shape[1] // 128):
        ref[k] = v[:, 128 * k : 128 * (k + 1)]
        first.append(ref[k, pl.ds(0, rows // frames, stride=frames), :])
        last.append(ref[k, pl.ds(frames - 1, rows // frames, stride=frames), :])
    return jnp.concatenate(first, axis=1), jnp.concatenate(last, axis=1)


def shifted(ref, v, step, frames, beyond):
    rows = v.shape[0]
    at = 0 if step == 1 else frames - 1
    parts = []
    for k in range(v.shape[1] // 128):
        lanes = slice(128 * k, 128 * (k + 1))
        ref[k] = pltpu.roll(v[:, lanes], 1 if step == 1 else rows - 1, 0)
        ref[k, pl.ds(at, rows // frames, stride=frames), :] = beyond[:, lanes]
        parts.append(ref[k])
    return jnp.concatenate(parts, axis=1)


def add_rows(ref, *rows):
    @pl.when(pl.program_id(0) == 0)
    def _():
        ref[...] = jnp.zeros_like(ref)

    for k, row in enumerate(rows):
        ref[k : k + 1, :] += row


def add_whole(ref, value):
    @pl.when(pl.program_id(0) == 0)
    def _():
        ref[...] = jnp.zeros_like(ref)

    ref[...] += value


def vmem():
    return pl.BlockSpec(memory_space=pltpu.VMEM)


def shape(*dims, dtype=F32):
    return jax.ShapeDtypeStruct(dims, dtype)


def cost(flops, nbytes):
    return pl.CostEstimate(flops=int(flops / 2), bytes_accessed=int(nbytes / 2), transcendentals=0)


def whole(x):
    rank = len(x.shape)
    return pl.BlockSpec(tuple(x.shape), lambda i, *s: (0,) * rank)


def part(x, rows, at=None):
    tail = (0,) * (len(x.shape) - 1)
    where = at or (lambda i, *s: i)
    return pl.BlockSpec((rows,) + tuple(x.shape[1:]), lambda i, *s: (where(i, *s),) + tail)


def stepped(body, name, steps, scalars, ins, outs, scratch=(), est=None):
    return pl.pallas_call(
        body,
        name=name,
        out_shape=[o for o, _ in outs],
        grid_spec=pltpu.PrefetchScalarGridSpec(
            num_scalar_prefetch=len(scalars),
            grid=(steps,),
            in_specs=[s for _, s in ins],
            out_specs=[s for _, s in outs],
            scratch_shapes=list(scratch),
        ),
        compiler_params=pltpu.CompilerParams(vmem_limit_bytes=LIMIT),
        cost_estimate=est,
    )(*scalars, *[a for a, _ in ins])


def sum_kernel(sizes, axes, widths, edges, *refs):
    dps, ys, hs = sizes
    roles = ys * hs if axes == ROLE else hs
    parts = len(widths)
    xs, refs = refs[:parts], refs[parts:]
    edge_in, refs = refs[:edges], refs[edges:]
    outs, refs = refs[:parts], refs[parts:]
    edge_out, refs = refs[:edges], refs[edges:]
    one_src, two_src, b1, b2, s1, r1, s2, r2 = refs[:8]
    d = lax.axis_index("dp")
    y = lax.axis_index("yy")
    h = lax.axis_index("hh")
    m = y * hs + h

    def role(i):
        if axes != ROLE:
            return {"hh": lax.rem(h + i, hs)}
        p = lax.rem(m + i, roles)
        return {"yy": p // hs, "hh": lax.rem(p, hs)}

    def along(i):
        return {"dp": lax.rem(d + i, dps)}

    def send(src, dst, ssem, rsem, to):
        c = pltpu.make_async_remote_copy(
            src_ref=src, dst_ref=dst, send_sem=ssem, recv_sem=rsem, device_id=to, device_id_type=MESH
        )
        c.start()
        return c

    bar = pltpu.get_barrier_semaphore()
    for i in range(1, roles):
        pl.semaphore_signal(bar, inc=1, device_id=role(i), device_id_type=MESH)
    for i in range(1, dps):
        pl.semaphore_signal(bar, inc=1, device_id=along(i), device_id_type=MESH)
    one_src[...] = jnp.zeros_like(one_src)
    start = 0
    for x, width in zip(xs, widths):
        one_src[start : start + x.shape[0], 0:width] = x[...]
        start += x.shape[0]
    pl.semaphore_wait(bar, roles + dps - 2)
    one = [send(one_src, b1.at[i - 1], s1.at[i - 1], r1.at[i - 1], role(i)) for i in range(1, roles)]
    rim = []
    if edges:
        s3, r3 = refs[8:]
        rim = [
            send(edge_in[k], edge_out[k], s3.at[k], r3.at[k], along(1 if k == 0 else dps - 1))
            for k in range(edges)
        ]
    acc = one_src[...]
    for i, c in enumerate(one):
        c.wait_recv()
        acc = acc + b1[i]
    two_src[...] = acc
    two = [send(two_src, b2.at[i - 1], s2.at[i - 1], r2.at[i - 1], along(i)) for i in range(1, dps)]
    for i, c in enumerate(two):
        c.wait_recv()
        acc = acc + b2[i]
    start = 0
    for o, width in zip(outs, widths):
        o[...] = acc[start : start + o.shape[0], 0:width]
        start += o.shape[0]
    for c in rim:
        c.wait_recv()
    for c in one + rim + two:
        c.wait_send()


def total(xs, cid, sizes, axes, rims=()):
    dps, ys, hs = sizes
    roles = ys * hs if axes == ROLE else hs
    widths = [x.shape[1] for x in xs]
    packed = (sum(x.shape[0] for x in xs), max(widths))
    dma = pltpu.SemaphoreType.DMA
    return pl.pallas_call(
        functools.partial(sum_kernel, sizes, axes, widths, len(rims)),
        name="sum%d" % cid,
        out_shape=[shape(*x.shape) for x in xs] + [shape(*r.shape) for r in rims],
        in_specs=[vmem()] * (len(xs) + len(rims)),
        out_specs=[vmem()] * (len(xs) + len(rims)),
        scratch_shapes=[
            pltpu.VMEM(packed, F32),
            pltpu.VMEM(packed, F32),
            pltpu.VMEM((roles - 1,) + packed, F32),
            pltpu.VMEM((dps - 1,) + packed, F32),
            dma((roles - 1,)), dma((roles - 1,)), dma((dps - 1,)), dma((dps - 1,)),
        ] + ([dma((2,)), dma((2,))] if rims else []),
        compiler_params=pltpu.CompilerParams(collective_id=cid, has_side_effects=True),
    )(*xs, *rims)


def last_sum_kernel(sizes, x_ref, v_ref, o_ref, w_ref, two_src, b1, b2, vb, s1, r1, s2, r2, s3, r3, s4, r4):
    dps, ys, hs = sizes
    d = lax.axis_index("dp")
    h = lax.axis_index("hh")

    def along(i):
        return lax.rem(d + i, dps)

    def send(src, dst, ssem, rsem, to):
        c = pltpu.make_async_remote_copy(
            src_ref=src, dst_ref=dst, send_sem=ssem, recv_sem=rsem, device_id=to, device_id_type=MESH
        )
        c.start()
        return c

    bar = pltpu.get_barrier_semaphore()
    other = {"hh": lax.rem(h + 1, hs)}
    pl.semaphore_signal(bar, inc=1, device_id=other, device_id_type=MESH)
    for i in range(1, dps):
        pl.semaphore_signal(bar, inc=1, device_id={"dp": along(i)}, device_id_type=MESH)
    pl.semaphore_wait(bar, dps)
    one = send(x_ref, b1, s1, r1, other)
    out = [
        send(v_ref.at[along(i)], vb.at[i - 1], s3.at[i - 1], r3.at[i - 1], {"dp": along(i)})
        for i in range(1, dps)
    ]
    one.wait_recv()
    acc = x_ref[...] + b1[...]
    two_src[...] = acc
    two = [send(two_src, b2.at[i - 1], s2.at[i - 1], r2.at[i - 1], {"dp": along(i)}) for i in range(1, dps)]
    piece = v_ref[d]
    for i, c in enumerate(out):
        c.wait_recv()
        piece = piece + vb[i]
    w_ref[d] = piece
    back = [
        send(w_ref.at[d], w_ref.at[d], s4.at[i - 1], r4.at[i - 1], {"dp": along(i)}) for i in range(1, dps)
    ]
    for i, c in enumerate(two):
        c.wait_recv()
        acc = acc + b2[i]
    o_ref[...] = acc
    for c in back:
        c.wait_recv()
    one.wait_send()
    for c in out + two + back:
        c.wait_send()


def last_total(x, v, cid, sizes):
    dps, ys, hs = sizes
    dma = pltpu.SemaphoreType.DMA
    return pl.pallas_call(
        functools.partial(last_sum_kernel, sizes),
        name="sum%d" % cid,
        out_shape=[shape(*x.shape), shape(*v.shape)],
        in_specs=[vmem()] * 2,
        out_specs=[vmem()] * 2,
        scratch_shapes=[
            pltpu.VMEM(x.shape, F32),
            pltpu.VMEM(x.shape, F32),
            pltpu.VMEM((dps - 1,) + x.shape, F32),
            pltpu.VMEM((dps - 1,) + v.shape[1:], F32),
            dma, dma,
        ] + [dma((dps - 1,))] * 6,
        compiler_params=pltpu.CompilerParams(collective_id=cid, has_side_effects=True),
    )(x, v)


def fast1_kernel(frames, idx, x_ref, rh, rl, p_ref, e0, e1, st, tmp):
    p = dot3(split(frames_of(x_ref)), (rh[...], rl[...]))
    p_ref[...] = p
    e0[0], e1[0] = edges(tmp, p, frames)
    add_rows(st, colsum(p), colsum(p * p))


def lateral_taps(frames, mask, x_ref, halo, bz):
    x = [rows_of(x_ref, g) for g in range(4)]
    beyond = jnp.concatenate([halo[:, 6, :], halo[:, 7, :]], axis=1)
    early = shifted(bz, jnp.concatenate([x[2], x[3]], axis=1), 1, frames, beyond)
    return jnp.concatenate([masked(early, mask), x[0], x[1], x[2]], axis=1)


def lateral_kernel(frames, idx, mask, x_ref, halo, wh, wl, s_ref, e0, st, bz):
    p = dot3(split(lateral_taps(frames, mask, x_ref, halo, bz)), (wh[...], wl[...]), 1, 1)
    s_ref[...] = p
    e0[0] = edge(bz, p, 0, frames)
    add_rows(st, colsum(p), colsum(p * p))


def fast_norm(tot, number):
    return moments(fold32(tot[0:1, :]), fold32(tot[1:2, :]), number)


def wide_norm(tot, number):
    return moments(fold128(tot[0:1, :]), fold128(tot[1:2, :]), number)


def rims_of(v, prev, nxt):
    lane = lax.broadcasted_iota(jnp.int32, v.shape, 1)
    return jnp.where(lane >= 96, prev, jnp.where(lane < 32, nxt, 0.0))


def fast2_kernel(
    number, frames, mp, mn, tot, gain, bias, p1, before, after, wh, wl, a_ref, z_ref, p2, st, zp, zn
):
    mean, inverse = fast_norm(tot, number)
    scale = gain[...] * inverse
    shift = bias[...] - mean * scale
    a = silu(p1[...] * scale + shift)
    a_ref[...] = a
    prev = shifted(zp, a, 1, frames, silu(before[0] * scale + shift))
    nxt = shifted(zn, a, -1, frames, silu(after[0] * scale + shift))
    z = rims_of(a, masked(prev, mp), masked(nxt, mn))
    z_ref[...] = z
    p = dot3(split(jnp.concatenate([a, z], axis=1)), (wh[...], wl[...]))
    p2[...] = p
    add_rows(st, colsum(p), colsum(p * p))


def fast3_kernel(number, tot, gain, bias, p2, eh, el, b_ref, st):
    mean, inverse = fast_norm(tot, number)
    scale = gain[...] * inverse
    b = silu(p2[...] * scale + (bias[...] - mean * scale))
    b_ref[...] = b
    p = dot3(split(b), (eh[...], el[...]))
    add_rows(st, colsum(p), colsum(p * p))


def put_frames(ref, v):
    pixels, count, lanes = ref.shape
    for g in range(4):
        ref[:, pl.ds(g, count // 4, stride=4), :] = v[:, lanes * g : lanes * (g + 1)].reshape(
            pixels, count // 4, lanes
        )


def fast4_kernel(number, share, idx, tot, gain, bias, x_ref, c_ref, b_ref, eh, el, o_ref, f_ref, u_ref, st):
    mean, inverse = wide_norm(tot, number)
    scale = gain[...] * inverse
    shift = bias[...] - mean * scale
    p = dot3(split(b_ref[...]), (eh[...], el[...]))
    j = p * four(scale) + four(shift) + frames_of(x_ref)
    s = sigmoid(j)
    out = j * s
    put_frames(o_ref, out)
    put_frames(f_ref, out)
    u = frames_of(c_ref) * (s * (1.0 + j * (1.0 - s)))
    u_ref[...] = u
    add_rows(st, share * colsum(u), share * colsum(u * (p - four(mean))))


def fast5_kernel(
    number, frames, tot, back, gain, tot2, gain2, bias2, u_ref, b_ref, p2, eh, el, u2, eg, e0, e1, st, tmp
):
    mean, inverse = wide_norm(tot, number)
    alpha, beta, gamma = back_terms(
        gain[...], mean, inverse, fold128(back[0:1, :]), fold128(back[1:2, :]), number
    )
    bs = split(b_ref[...])
    e = (eh[...], el[...])
    g = split(four(alpha) * u_ref[...] + four(beta) * dot3(bs, e) + four(gamma))
    add_whole(eg, dot3(bs, g, 0, 0))
    v = dot3(g, e, 1, 1)
    mean2, inverse2 = fast_norm(tot2, number)
    z = p2[...] - mean2
    u = v * slope(z * (inverse2 * gain2[...]) + bias2[...])
    u2[...] = u
    e0[0, 0], e1[0, 0] = edges(tmp, u, frames)
    e0[0, 1], e1[0, 1] = edges(tmp, p2[...], frames)
    add_rows(st, colsum(u), colsum(u * z))


def fast6_kernel(
    number, frames, mp, mn, tot2, back2, gain2, tot1, gain1, bias1, u2, p2, before, after, a, z, p1,
    wh, wl, u1, tg, st, zp, zn
):
    mean2, inverse2 = fast_norm(tot2, number)
    alpha, beta, gamma = back_terms(
        gain2[...], mean2, inverse2, fold32(back2[0:1, :]), fold32(back2[1:2, :]), number
    )
    g = alpha * u2[...] + beta * p2[...] + gamma
    prev = shifted(zp, g, 1, frames, alpha * before[0, 0] + beta * before[0, 1] + gamma)
    nxt = shifted(zn, g, -1, frames, alpha * after[0, 0] + beta * after[0, 1] + gamma)
    gz = rims_of(g, masked(prev, mp), masked(nxt, mn))
    add_whole(tg, dot3(split(jnp.concatenate([a[...], z[...]], axis=1)), split(g), 0, 0))
    v = dot3(split(jnp.concatenate([g, gz], axis=1)), (wh[...], wl[...]), 1, 1)
    mean1, inverse1 = fast_norm(tot1, number)
    c = p1[...] - mean1
    u = v * slope(c * (gain1[...] * inverse1) + bias1[...])
    u1[...] = u
    add_rows(st, colsum(u), colsum(u * c))


def fast7_kernel(number, idx, tot1, back1, gain1, x_ref, u1, p1, g1, rg):
    mean, inverse = fast_norm(tot1, number)
    alpha, beta, gamma = back_terms(
        gain1[...], mean, inverse, fold32(back1[0:1, :]), fold32(back1[1:2, :]), number
    )
    g = alpha * u1[...] + beta * p1[...] + gamma
    g1[...] = g
    add_whole(rg, dot3(split(frames_of(x_ref)), split(g), 0, 0))


def slow1_kernel(
    number, frames, idx, tot, gain, bias, x0, x1, x2, x3, side, rh, rl, sh, sl,
    first, short, jh, jl, e0, e1, st, wide, tmp
):
    lanes = x0.shape[1]
    for r, x in enumerate((x0, x1, x2, x3)):
        at = pl.multiple_of(idx[3 + r] * lanes, lanes)
        wide[:, pl.ds(at, lanes)] = x[...]
    mean, inverse = moments(tot[0:1, :], tot[1:2, :], number)
    scale = gain[...] * inverse
    top = sh.shape[0] * lanes
    wide[:, top:] = silu(side[...] * scale + (bias[...] - mean * scale))
    joined = split(wide[...])
    jh[0], jl[0] = joined
    p = dot3(joined, (rh[...], rl[...]), 1, 1)
    first[...] = p
    e0[0], e1[0] = edges(tmp, p, frames)
    sums = [colsum(p)]
    squares = [colsum(p * p)]
    for n in range(sh.shape[0]):
        p = dot3(joined, (sh[n], sl[n]))
        short[:, n * lanes : (n + 1) * lanes] = p
        sums.append(colsum(p))
        squares.append(colsum(p * p))
    add_rows(st, jnp.concatenate(sums, axis=1), jnp.concatenate(squares, axis=1))


def slow2_kernel(
    number, frames, mp, mn, tot, gain, bias, first, before, after, wh, wl, th, tl, pm, st, zp, zn
):
    width = gain.shape[1]
    mean, inverse = moments(tot[0:1, 0:width], tot[1:2, 0:width], number)
    scale = gain[...] * inverse
    shift = bias[...] - mean * scale
    a = silu(first[...] * scale + shift)
    prev = shifted(zp, a, 1, frames, silu(before[0] * scale + shift))
    nxt = shifted(zn, a, -1, frames, silu(after[0] * scale + shift))
    taps = split(jnp.concatenate([masked(prev, mp), a, masked(nxt, mn)], axis=1))
    th[0], tl[0] = taps
    p = dot3(taps, (wh[...], wl[...]), 1, 1)
    pm[...] = p
    add_rows(st, colsum(p), colsum(p * p))


def slow3_kernel(number, tot, gain, bias, pm, eh, el, bh, bl, st):
    mean, inverse = moments(tot[0:1, :], tot[1:2, :], number)
    scale = gain[...] * inverse
    b = split(silu(pm[...] * scale + (bias[...] - mean * scale)))
    bh[0], bl[0] = b
    p = dot3(b, (eh[...], el[...]))
    add_rows(st, colsum(p), colsum(p * p))


def slow4_kernel(
    number, idx, tot_l, tot_s, gain_l, bias_l, gain_s, bias_s, bh, bl, short, c0, c1, c2, c3, eh, el,
    o0, o1, o2, o3, u_ref, st, wide
):
    lanes = c0.shape[1]
    for r, c in enumerate((c0, c1, c2, c3)):
        at = pl.multiple_of(idx[3 + r] * lanes, lanes)
        wide[:, pl.ds(at, lanes)] = c[...]
    off = tot_s.shape[1] - short.shape[1]
    bs = (bh[0], bl[0])
    sums = []
    for n in range(short.shape[1] // lanes):
        at = slice(n * lanes, (n + 1) * lanes)
        mean_l, inv_l = moments(tot_l[0:1, at], tot_l[1:2, at], number)
        far = slice(off + n * lanes, off + (n + 1) * lanes)
        mean_s, inv_s = moments(tot_s[0:1, far], tot_s[1:2, far], number)
        zl = dot3(bs, (eh[:, at], el[:, at])) - mean_l
        zs = short[:, at] - mean_s
        j = zl * (inv_l * gain_l[:, at]) + zs * (inv_s * gain_s[:, at]) + (bias_l[:, at] + bias_s[:, at])
        s = sigmoid(j)
        u = wide[:, at] * (s * (1.0 + j * (1.0 - s)))
        u_ref[:, at] = u
        sums.append((colsum(u), colsum(u * zl), colsum(u * zs)))
        wide[:, at] = j * s
    for r, o in enumerate((o0, o1, o2, o3)):
        at = pl.multiple_of(idx[3 + r] * lanes, lanes)
        o[...] = wide[:, pl.ds(at, lanes)]
    add_rows(st, *[jnp.concatenate(rows, axis=1) for rows in zip(*sums)])


def slow5_kernel(
    number, frames, tot_l, back, gain_l, tot_m, gain_m, bias_m, u_ref, bh, bl, pm, eh, el,
    um, eg, e0, e1, st, tmp
):
    mean, inverse = moments(tot_l[0:1, :], tot_l[1:2, :], number)
    alpha, beta, gamma = back_terms(gain_l[...], mean, inverse, back[0:1, :], back[1:2, :], number)
    bs = (bh[0], bl[0])
    e = (eh[...], el[...])
    g = split(alpha * u_ref[...] + beta * dot3(bs, e) + gamma)
    add_whole(eg, dot3(bs, g, 0, 0))
    v = dot3(g, e, 1, 1)
    mean_m, inv_m = moments(tot_m[0:1, :], tot_m[1:2, :], number)
    z = pm[...] - mean_m
    u = v * slope(z * (inv_m * gain_m[...]) + bias_m[...])
    um[...] = u
    e0[0, 0], e1[0, 0] = edges(tmp, u, frames)
    e0[0, 1], e1[0, 1] = edges(tmp, pm[...], frames)
    add_rows(st, colsum(u), colsum(u * z))


def slow6_kernel(number, tot_s, back, gain_s, u_ref, short, jh, jl, sh, sl, dx, grads):
    off = tot_s.shape[1] - short.shape[1]
    mean, inverse = moments(tot_s[0:1, off:], tot_s[1:2, off:], number)
    alpha, beta, gamma = back_terms(gain_s[...], mean, inverse, back[0:1, :], back[2:3, :], number)
    lanes = sh.shape[2]
    joined = (jh[0], jl[0])

    @pl.when(pl.program_id(0) == 0)
    def _():
        grads[...] = jnp.zeros_like(grads)

    out = None
    for n in range(sh.shape[0]):
        at = slice(n * lanes, (n + 1) * lanes)
        g = split(alpha[:, at] * u_ref[:, at] + beta[:, at] * short[:, at] + gamma[:, at])
        grads[n] += dot3(joined, g, 0, 0)
        part = dot3(g, (sh[n], sl[n]), 1, 1)
        out = part if out is None else out + part
    dx[...] = out


def slow7_kernel(
    number, frames, mp, mn, tot_m, back, gain_m, tot_f, gain_f, bias_f, um, pm, before, after, th, tl,
    first, wh, wl, uf, tg, st, zp, zn
):
    mean, inverse = moments(tot_m[0:1, :], tot_m[1:2, :], number)
    alpha, beta, gamma = back_terms(gain_m[...], mean, inverse, back[0:1, :], back[1:2, :], number)
    g = alpha * um[...] + beta * pm[...] + gamma
    prev = shifted(zp, g, 1, frames, alpha * before[0, 0] + beta * before[0, 1] + gamma)
    nxt = shifted(zn, g, -1, frames, alpha * after[0, 0] + beta * after[0, 1] + gamma)
    gs = split(g)
    add_whole(tg, dot3(gs, (th[0], tl[0]), 0, 0))
    width = gain_f.shape[1]
    v = dot3(split(masked(nxt, mn)), (wh[:, 0:width], wl[:, 0:width]))
    v += dot3(gs, (wh[:, width : 2 * width], wl[:, width : 2 * width]))
    v += dot3(split(masked(prev, mp)), (wh[:, 2 * width :], wl[:, 2 * width :]))
    mean_f, inv_f = moments(tot_f[0:1, 0:width], tot_f[1:2, 0:width], number)
    z = first[...] - mean_f
    u = v * slope(z * (gain_f[...] * inv_f) + bias_f[...])
    uf[...] = u
    add_rows(st, colsum(u), colsum(u * z))


def slow8_kernel(
    number, frames, idx, tot_f, back, gain_f, tot_a, gain_a, bias_a, uf, first, jh, jl, dx, side,
    rh, rl, o0, o1, o2, o3, us, rg, e0, st, wide, tmp
):
    width = gain_f.shape[1]
    mean, inverse = moments(tot_f[0:1, 0:width], tot_f[1:2, 0:width], number)
    alpha, beta, gamma = back_terms(gain_f[...], mean, inverse, back[0:1, :], back[1:2, :], number)
    g = split(alpha * uf[...] + beta * first[...] + gamma)
    add_whole(rg, dot3(g, (jh[0], jl[0]), 0, 0))
    lanes = o0.shape[1]
    wide[...] = dx[...] + dot3(g, (rh[...], rl[...]))
    for r, o in enumerate((o0, o1, o2, o3)):
        at = pl.multiple_of(idx[3 + r] * lanes, lanes)
        o[...] = wide[:, pl.ds(at, lanes)]
    mean_a, inv_a = moments(tot_a[0:1, :], tot_a[1:2, :], number)
    z = side[...] - mean_a
    top = wide.shape[1] - width
    u = wide[:, top:] * slope(z * (inv_a * gain_a[...]) + bias_a[...])
    us[...] = u
    e0[0] = edge(tmp, u, 0, frames)
    add_rows(st, colsum(u), colsum(u * z))


def side_terms(number, tot_a, back, gain_a):
    mean, inverse = moments(tot_a[0:1, :], tot_a[1:2, :], number)
    return back_terms(gain_a[...], mean, inverse, back[0:1, :], back[1:2, :], number)


def slow9_kernel(number, frames, idx, mask, tot_a, back, gain_a, us, side, x_ref, halo, lg, bz):
    alpha, beta, gamma = side_terms(number, tot_a, back, gain_a)
    g = split(alpha * us[...] + beta * side[...] + gamma)
    add_whole(lg, dot3(g, split(lateral_taps(frames, mask, x_ref, halo, bz)), 0, 0))


def last_kernel(
    number, frames, idx, mask, tot_a, back, gain_a, us, side, us_edge, side_edge, u3, g1, wh, wl,
    rh, rl, o_ref, f_ref, zn
):
    alpha, beta, gamma = side_terms(number, tot_a, back, gain_a)
    here = alpha * us[...] + beta * side[...] + gamma
    after = shifted(zn, here, -1, frames, alpha * us_edge[0] + beta * side_edge[0] + gamma)
    base = u3[...] + dot3(split(g1[...]), (rh[...], rl[...]), 1, 1)
    near = dot3(split(here), (wh[:, 256:], wl[:, 256:]))
    far = dot3(split(masked(after, mask)), (wh[:, 0:256], wl[:, 0:256]))
    both = jnp.concatenate(
        [near[:, 0:256], near[:, 256:384] + far[:, 0:128], far[:, 128:256]], axis=1
    )
    out = base + both
    put_frames(o_ref, out)
    put_frames(f_ref, out)


def weight_split(w):
    high = lax.reduce_precision(w, 8, 7)
    return high.astype(BF16), (w - high).astype(BF16)


def row(v):
    return v.reshape(1, -1)


def tiled_row(v):
    return jnp.tile(v.reshape(1, -1), (1, 4))


def by_pixel(v):
    return v.transpose(1, 0, 2)


def after(value, *events):
    return lax.optimization_barrier((value,) + events)[0]


def local(sizes, *args):
    (
        slow_input, fast_input, clip_starts,
        fast_reduce, fast_reduce_gain, fast_reduce_bias,
        fast_temporal, fast_temporal_gain, fast_temporal_bias,
        fast_expand, fast_expand_gain, fast_expand_bias,
        lateral_conv, lateral_gain, lateral_bias,
        slow_reduce, slow_reduce_gain, slow_reduce_bias,
        slow_temporal, slow_temporal_gain, slow_temporal_bias,
        slow_expand, slow_expand_gain, slow_expand_bias,
        shortcut_conv, shortcut_gain, shortcut_bias,
        slow_cotangent, fast_cotangent,
    ) = args
    dps, ys, hs = sizes
    roles = ys * hs
    d, y, h = (lax.axis_index(a) for a in ALL)
    m = y * hs + h
    frames, pixels, lanes = slow_input.shape
    shard_rows = slow_reduce.shape[1]
    inner = shard_rows * roles
    joined_width = slow_reduce.shape[0]
    wide = lanes * roles
    number = frames * dps * pixels
    fast_number = number * 4
    half = pixels // hs
    own = pixels // roles
    steps = 7
    half_block, own_block = half // steps, own // steps
    fast_rows, slow_rows = half_block * frames, own_block * frames

    slow_x = by_pixel(slow_input).reshape(pixels * frames, lanes)
    slow_c = by_pixel(slow_cotangent).reshape(pixels * frames, lanes)
    fast_x = by_pixel(fast_input)
    fast_c = by_pixel(fast_cotangent)

    def block_of(p):
        return (p % hs) * ys + p // hs

    def role_xor(r):
        return (y ^ (r // hs)) * hs + (h ^ (r % hs))

    peers = [role_xor(r) for r in range(roles)]
    q = block_of(m)
    idx = jnp.stack([h, q, y] + peers).astype(jnp.int32)
    own_rows = own * frames
    row_at = [own_rows * block_of(p) for p in peers]

    times = d * frames + jnp.arange(0, frames + 1, dtype=jnp.int32)

    def clip_of(t):
        return jnp.sum((clip_starts[None, :] <= t[:, None]).astype(jnp.int32), axis=1) - 1

    same = jnp.logical_and(
        clip_of(times) == clip_of(times - 1), jnp.logical_and(times >= 1, times < frames * dps)
    ).astype(F32)
    mask_prev = jnp.broadcast_to(same[:frames, None], (frames, 128))
    mask_next = jnp.broadcast_to(same[1:, None], (frames, 128))

    def role_pairs(r):
        return [(i, i ^ r) for i in range(roles)]

    def placed(out, got):
        for r in range(1, roles):
            out = lax.dynamic_update_slice_in_dim(out, got[r - 1], row_at[r], axis=0)
        return by_pixel(out.reshape(pixels, frames, lanes))

    swap = [(0, 1), (1, 0)]
    half_rows = half * frames

    def from_core(array):
        return lax.ppermute(
            lax.dynamic_slice_in_dim(array, half_rows * (1 - h), half_rows, axis=0), "hh", swap
        )

    def for_partner(array, here):
        return [
            lax.dynamic_slice_in_dim(array, half_rows * h + own_rows * (1 - y), own_rows, axis=0),
            lax.dynamic_slice_in_dim(here, own_rows * (1 - y), own_rows, axis=0),
        ]

    sho_y = lax.ppermute(shortcut_conv, "yy", swap)
    in_core = from_core(slow_x)
    in_send = jnp.concatenate(for_partner(slow_x, in_core), axis=0)
    in_y = lax.ppermute(in_send, "yy", swap)

    vectors = [
        lateral_gain, lateral_bias, slow_reduce_gain, slow_reduce_bias, slow_temporal_gain,
        slow_temporal_bias, slow_expand_gain, slow_expand_bias, shortcut_gain, shortcut_bias,
    ]
    vector = jnp.concatenate(vectors)
    share = shard_rows // dps
    across = -(-vector.shape[0] // (share * 128)) * 128
    vector = jnp.pad(vector, (0, share * across - vector.shape[0])).reshape(share, across)
    piece = jnp.concatenate(
        [
            lateral_conv.transpose(2, 0, 1).reshape(shard_rows, -1),
            slow_reduce.T,
            slow_temporal.transpose(2, 0, 1).reshape(shard_rows, -1),
            slow_expand,
        ],
        axis=1,
    )
    piece = jnp.concatenate([lax.dynamic_slice_in_dim(piece, d * share, share, axis=0), vector], axis=1)
    got = lax.all_gather(piece, ALL, axis=0, tiled=False).reshape((dps, roles) + piece.shape)
    matrix = got[:, :, :, : piece.shape[1] - across].transpose(1, 0, 2, 3).reshape(inner, -1)
    taps = lateral_conv.shape[0] * lateral_conv.shape[1]
    bounds = [0, taps, taps + joined_width, taps + joined_width + 3 * inner]
    bounds.append(bounds[-1] + wide)
    (lat_h, lat_l), (red_h, red_l), (tem_h, tem_l), (exp_h, exp_l) = [
        weight_split(matrix[:, bounds[k] : bounds[k + 1]]) for k in range(4)
    ]
    vector = got[0, :, :, piece.shape[1] - across :].reshape(roles, -1)
    full = []
    start = 0
    for v in vectors:
        full.append(vector[:, start : start + v.shape[0]].reshape(1, -1))
        start += v.shape[0]
    (
        lat_gain, lat_bias, red_gain, red_bias, tem_gain, tem_bias, exp_gain, exp_bias, sho_gain, sho_bias
    ) = full

    eye = jnp.eye(4, dtype=F32)
    up = jnp.eye(4, k=1, dtype=F32)
    down = jnp.eye(4, k=-1, dtype=F32)
    far_next = jnp.eye(4, k=3, dtype=F32)
    far_prev = jnp.eye(4, k=-3, dtype=F32)
    fr_h, fr_l = weight_split(after(jnp.kron(eye, fast_reduce), in_send))
    fe_h, fe_l = weight_split(jnp.kron(eye, fast_expand))
    centre = jnp.kron(eye, fast_temporal[1]) + jnp.kron(up, fast_temporal[0]) + jnp.kron(down, fast_temporal[2])
    outer = jnp.kron(far_next, fast_temporal[2]) + jnp.kron(far_prev, fast_temporal[0])
    ft_h, ft_l = weight_split(jnp.concatenate([centre, outer], axis=0))
    fb_h, fb_l = weight_split(jnp.concatenate([centre, outer], axis=1))
    fr_gain, fr_bias = tiled_row(fast_reduce_gain), tiled_row(fast_reduce_bias)
    ft_gain, ft_bias = tiled_row(fast_temporal_gain), tiled_row(fast_temporal_bias)
    fe_gain, fe_bias = row(fast_expand_gain), row(fast_expand_bias)

    forth = [(i, i + 1) for i in range(dps - 1)]
    backw = [(i + 1, i) for i in range(dps - 1)]
    halo = lax.dynamic_slice(fast_x, (half * h, frames * 4 - 8, 0), (half, 8, 128))
    halo = lax.ppermute(halo, "dp", forth)

    in_half = lambda i, s, *_: s[0] * steps + i
    in_own = lambda i, s, *_: s[1] * steps + i
    own_in_half = lambda i, s, *_: s[2] * steps + i

    def all_of(*arrays):
        return [(x, whole(x)) for x in arrays]

    def const(*dims):
        o = shape(*dims)
        return (o, whole(o))

    def by_block(x, at=None):
        return (x, part(x, x.shape[0] // steps, at))

    def out_rows(rows, width):
        return by_block(shape(rows * steps, width))

    def out_blocks(*dims, dtype=F32):
        return by_block(shape(steps, *dims, dtype=dtype))

    def tmp(*dims):
        return pltpu.VMEM(dims, F32)

    def cut(rows, width):
        return tmp(width // 128, rows, 128)

    other_y = lambda i, s, *_: (1 - s[2]) * steps + i

    fr, sr = fast_rows, slow_rows
    nf, ns = fr * steps, sr * steps
    fx = (fast_x, part(fast_x, half_block, in_half))
    fc = (fast_c, part(fast_c, half_block, in_half))
    masks = all_of(mask_prev, mask_next)
    core = ("hh",)

    p1, e0, e1, st = stepped(
        functools.partial(fast1_kernel, frames), "fast1", steps, [idx], [fx] + all_of(fr_h, fr_l),
        [out_rows(fr, 128), out_blocks(half_block, 128), out_blocks(half_block, 128), const(2, 128)],
        scratch=[cut(fr, 128)],
        est=cost(2 * 3 * nf * 512 * 256, nf * 640 * 4),
    )
    st_f1 = st
    tot_f1, before, beyond = total([st], 1, sizes, core, (e1, e0))
    a1, z1, p2, st = stepped(
        functools.partial(fast2_kernel, fast_number, frames), "fast2", steps, [],
        masks + all_of(tot_f1, fr_gain, fr_bias)
        + [by_block(p1), by_block(before), by_block(beyond)] + all_of(ft_h, ft_l),
        [out_rows(fr, 128)] * 3 + [const(2, 128)],
        scratch=[cut(fr, 128)] * 2,
        est=cost(2 * 3 * nf * 256 * 256, 4 * nf * 128 * 4),
    )
    (tot_f2,) = total([st], 2, sizes, core)

    def role_table(mine, from_y, event):
        column = jnp.stack([after(mine, event), from_y])
        other = lax.ppermute(column, "hh", swap)
        table = jnp.stack([column[0], other[0], column[1], other[1]])
        return jnp.stack([lax.dynamic_index_in_dim(table, p, 0, keepdims=False) for p in peers])

    sho_h, sho_l = weight_split(role_table(shortcut_conv, sho_y, tot_f1))
    cot_core = from_core(after(slow_c, tot_f1))
    slow_cot = [cot_core] + [
        lax.all_gather(after(v, matrix), "yy", axis=0, tiled=True) for v in for_partner(slow_c, cot_core)
    ]
    side, side_edge, st_a = stepped(
        functools.partial(lateral_kernel, frames), "lateral", steps, [idx],
        all_of(mask_prev) + [fx, by_block(halo)] + all_of(after(lat_h, st), lat_l),
        [out_rows(fr, inner), out_blocks(half_block, inner), const(2, inner)],
        scratch=[cut(fr, 256)],
        est=cost(2 * 3 * nf * 768 * 256, nf * 768 * 4),
    )
    side_edge = lax.ppermute(side_edge, "dp", backw)
    b1, st = stepped(
        functools.partial(fast3_kernel, fast_number), "fast3", steps, [],
        all_of(tot_f2, ft_gain, ft_bias) + [by_block(p2)] + all_of(fe_h, fe_l),
        [out_rows(fr, 128), const(2, 512)],
        est=cost(2 * 3 * nf * 256 * 512, 2 * nf * 128 * 4),
    )
    tot_f3, tot_a = total([st, st_a], 3, sizes, core)
    half_out = shape(half, frames * 4, 128)
    full_out = shape(pixels, frames * 4, 128)
    fast_half, fast_full, u3, st_f4 = stepped(
        functools.partial(fast4_kernel, fast_number, 1.0 / ys), "fast4", steps, [idx],
        all_of(tot_f3, fe_gain, fe_bias) + [fx, fc, by_block(b1)] + all_of(fe_h, fe_l),
        [by_block(half_out), (full_out, part(full_out, half_block, in_half)), out_rows(fr, 512), const(2, 512)],
        est=cost(2 * 3 * nf * 256 * 512, nf * 5 * 512 * 4),
    )

    side_own = (side, part(side, slow_rows, own_in_half))
    sx = (slow_x, part(slow_x, slow_rows, in_own))
    sc = (slow_c, part(slow_c, slow_rows, in_own))
    bf_joined = out_blocks(sr, joined_width, dtype=BF16)
    first, short, jh, jl, e0, e1, st = stepped(
        functools.partial(slow1_kernel, number, frames), "slow1", steps, [idx],
        all_of(after(tot_a, st_f4), lat_gain, lat_bias) + [sx, (in_core, part(in_core, slow_rows, own_in_half))]
        + [(in_y, part(in_y, slow_rows, at)) for at in (lambda i, *s: i, lambda i, *s: steps + i)]
        + [side_own]
        + all_of(red_h, red_l, sho_h, sho_l),
        [
            out_rows(sr, inner), out_rows(sr, wide), bf_joined, bf_joined,
            out_blocks(own_block, inner), out_blocks(own_block, inner), const(2, inner + wide),
        ],
        scratch=[tmp(sr, joined_width), cut(sr, inner)],
        est=cost(2 * 3 * ns * 1280 * 1280, ns * 4 * 3840 + 7e6),
    )
    tot_s, back_f3, before, beyond = total([st, st_f4], 8, sizes, ROLE, (e1, e0))
    bf_taps = out_blocks(sr, 3 * inner, dtype=BF16)
    wide_masks = all_of(*[jnp.concatenate([v, v], axis=1) for v in (mask_prev, mask_next)])
    th, tl, pm, st = stepped(
        functools.partial(slow2_kernel, number, frames), "slow2", steps, [],
        wide_masks + all_of(tot_s, red_gain, red_bias) + [by_block(x) for x in (first, before, beyond)]
        + all_of(tem_h, tem_l),
        [bf_taps, bf_taps, out_rows(sr, inner), const(2, inner)],
        scratch=[cut(sr, inner)] * 2,
        est=cost(2 * 3 * ns * 768 * 256, ns * 4 * 1500),
    )
    (tot_m,) = total([st], 9, sizes, ROLE)
    bf_mid = out_blocks(sr, inner, dtype=BF16)
    bh, bl, st = stepped(
        functools.partial(slow3_kernel, number), "slow3", steps, [],
        all_of(tot_m, tem_gain, tem_bias) + [by_block(pm)] + all_of(exp_h, exp_l),
        [bf_mid, bf_mid, const(2, wide)],
        est=cost(2 * 3 * ns * 1024 * 256, ns * 4 * 512),
    )
    (tot_l,) = total([st], 10, sizes, ROLE)
    slow_full = shape(pixels * frames, lanes)
    own_out = (slow_full, part(slow_full, slow_rows, in_own))
    *outs, u, st = stepped(
        functools.partial(slow4_kernel, number), "slow4", steps, [idx],
        all_of(tot_l, tot_s, exp_gain, exp_bias, sho_gain, sho_bias)
        + [by_block(x) for x in (bh, bl, short)] + [sc]
        + [(slow_cot[0], part(slow_cot[0], slow_rows, own_in_half))]
        + [(x, part(x, slow_rows, other_y)) for x in slow_cot[1:]]
        + all_of(exp_h, exp_l),
        [own_out] + [out_rows(sr, lanes)] * (roles - 1) + [out_rows(sr, wide), const(4, wide)],
        scratch=[tmp(sr, wide)],
        est=cost(2 * 3 * ns * 1024 * 256, ns * 4 * 4352),
    )
    (back_ls,) = total([st], 11, sizes, ROLE)
    near_rows = lax.ppermute(outs[1], "hh", swap)
    far_rows = lax.ppermute(outs[3], "hh", swap)
    from_y = [lax.all_gather(v, "yy", axis=0, tiled=False) for v in (outs[2], far_rows)]

    dx, short_grads = stepped(
        functools.partial(slow6_kernel, number), "slow6", steps, [],
        all_of(tot_s, back_ls, sho_gain) + [by_block(x) for x in (u, short, jh, jl)] + all_of(sho_h, sho_l),
        [out_rows(sr, joined_width), const(roles, joined_width, lanes)],
        est=cost(2 * 6 * ns * 1280 * 1024, ns * 4 * 4600 + 12e6),
    )
    um, expand_grad, e0, e1, st = stepped(
        functools.partial(slow5_kernel, number, frames), "slow5", steps, [],
        all_of(tot_l, after(back_ls, dx), exp_gain, tot_m, tem_gain, tem_bias)
        + [by_block(x) for x in (u, bh, bl, pm)] + all_of(exp_h, exp_l),
        [
            out_rows(sr, inner), const(inner, wide), out_blocks(2, own_block, inner),
            out_blocks(2, own_block, inner), const(2, inner),
        ],
        scratch=[cut(sr, inner)],
        est=cost(2 * 9 * ns * 1024 * 256, ns * 4 * 1800),
    )
    slow_out = outs[0]
    back_m, before, beyond = total([st], 12, sizes, ROLE, (e1, e0))
    def by_peer(g):
        rows = g.shape[0] // roles
        parts = [lax.dynamic_slice_in_dim(g, p * rows, rows, axis=0) for p in peers]
        return jnp.stack([parts[0], parts[2]]), jnp.stack([parts[1], parts[3]])

    def chip_sum(near, far):
        return near + lax.ppermute(far, "hh", swap)

    expand_pair = lax.psum_scatter(
        after(expand_grad, *from_y).reshape(roles, shard_rows, wide), ROLE, scatter_dimension=0, tiled=False
    )
    short_pair = lax.psum_scatter(after(short_grads, *from_y), ROLE, scatter_dimension=0, tiled=False)
    uf, temporal_grad, st = stepped(
        functools.partial(slow7_kernel, number, frames), "slow7", steps, [],
        wide_masks + all_of(tot_m, back_m, tem_gain, tot_s, red_gain, red_bias)
        + [by_block(x) for x in (um, pm, before, beyond, th, tl, first)] + all_of(tem_h, tem_l),
        [out_rows(sr, inner), const(inner, 3 * inner), const(2, inner)],
        scratch=[cut(sr, inner)] * 2,
        est=cost(2 * 6 * ns * 768 * 256, ns * 4 * 1500),
    )
    (back_f,) = total([st], 13, sizes, ROLE)
    *outs, us, reduce_grad, us_edge, st = stepped(
        functools.partial(slow8_kernel, number, frames), "slow8", steps, [idx],
        all_of(tot_s, back_f, red_gain, tot_a, lat_gain, lat_bias)
        + [by_block(x) for x in (uf, first, jh, jl, dx)] + [side_own] + all_of(red_h, red_l),
        [own_out] + [out_rows(sr, lanes)] * (roles - 1)
        + [out_rows(sr, inner), const(inner, joined_width), out_blocks(own_block, inner), const(2, inner)],
        scratch=[tmp(sr, joined_width), cut(sr, inner)],
        est=cost(2 * 6 * ns * 1280 * 256, ns * 4 * 5000),
    )
    (back_a,) = total([st], 14, sizes, ROLE)
    shortcut_sum, expand_sum = lax.psum((short_pair, expand_pair), "dp")
    us_sent = after(us, back_a)
    us_other = lax.ppermute(us_sent, "yy", swap)
    edge_sent = after(us_edge, back_a)
    edge_same = lax.ppermute(edge_sent, "dp", backw)
    edge_cross = lax.ppermute(
        edge_sent, ("dp", "yy"), [(i * ys + j, (i - 1) * ys + 1 - j) for i in range(1, dps) for j in range(ys)]
    )

    own_halo = (halo, part(halo, own_block, own_in_half))
    (lateral_grad,) = stepped(
        functools.partial(slow9_kernel, number, frames), "slow9", steps, [idx],
        all_of(mask_prev, tot_a, back_a, lat_gain)
        + [by_block(us), side_own, (fast_x, part(fast_x, own_block, in_own)), own_halo],
        [const(inner, 640)],
        scratch=[cut(sr, 256)],
        est=cost(2 * 3 * ns * 640 * 256, ns * 4 * 1500),
    )

    both = chip_sum(*by_peer(jnp.concatenate([lateral_grad, reduce_grad, temporal_grad], axis=1)))
    rest_y = lax.ppermute(both[1], "yy", swap)
    u2, expand_packed, e0, e1, st = stepped(
        functools.partial(fast5_kernel, fast_number, frames), "fast5", steps, [],
        all_of(tot_f3, after(back_f3, back_a, both, short_pair, expand_pair), fe_gain, tot_f2, ft_gain, ft_bias)
        + [by_block(u3), by_block(b1), by_block(p2)] + all_of(fe_h, fe_l),
        [
            out_rows(fr, 128), const(128, 512), out_blocks(2, half_block, 128),
            out_blocks(2, half_block, 128), const(2, 128),
        ],
        scratch=[cut(fr, 128)],
        est=cost(2 * 9 * nf * 256 * 512, nf * 900 * 4),
    )
    rest = both[0] + after(rest_y, u2)
    back_f2, before, beyond = total([st], 5, sizes, core, (e1, e0))
    grads_sent = [
        lax.ppermute(after(outs[r], back_a if r == 1 else rest), ROLE, role_pairs(r))
        for r in range(1, roles)
    ]
    slow_input_gradient = placed(outs[0], grads_sent)

    u1, temporal_packed, st = stepped(
        functools.partial(fast6_kernel, fast_number, frames), "fast6", steps, [],
        masks + all_of(tot_f2, after(back_f2, rest), ft_gain, tot_f1, fr_gain, fr_bias)
        + [by_block(x) for x in (u2, p2, before, beyond, a1, z1, p1)] + all_of(fb_h, fb_l),
        [out_rows(fr, 128), const(256, 128), const(2, 128)],
        scratch=[cut(fr, 128)] * 2,
        est=cost(2 * 6 * nf * 256 * 256, 6 * nf * 128 * 4),
    )
    (back_f1,) = total([st], 6, sizes, core)
    g1, reduce_packed = stepped(
        functools.partial(fast7_kernel, fast_number), "fast7", steps, [idx],
        all_of(tot_f1, after(back_f1, us_other), fr_gain) + [fx, by_block(u1), by_block(p1)],
        [out_rows(fr, 128), const(512, 128)],
        est=cost(2 * 3 * nf * 512 * 256, nf * 900 * 4),
    )

    def in_order(mine, other):
        return jnp.concatenate([jnp.where(y == 0, mine, other), jnp.where(y == 0, other, mine)], axis=0)

    eb = expand_packed.reshape(4, 32, 4, 128)
    expand_small = eb[0, :, 0] + eb[1, :, 1] + eb[2, :, 2] + eb[3, :, 3]
    rb = reduce_packed.reshape(4, 128, 4, 32)
    reduce_small = rb[0, :, 0] + rb[1, :, 1] + rb[2, :, 2] + rb[3, :, 3]
    tb = temporal_packed.reshape(8, 32, 4, 32)
    tap0 = tb[0, :, 1] + tb[1, :, 2] + tb[2, :, 3] + tb[7, :, 0]
    tap1 = tb[0, :, 0] + tb[1, :, 1] + tb[2, :, 2] + tb[3, :, 3]
    tap2 = tb[1, :, 0] + tb[2, :, 1] + tb[3, :, 2] + tb[4, :, 3]
    small = jnp.concatenate(
        [expand_small, reduce_small.reshape(32, 128), jnp.stack([tap0, tap1, tap2]).reshape(24, 128)], axis=0
    )
    small, rest = last_total(small, rest.reshape(dps, -1, rest.shape[1]), 15, sizes)
    rest = rest.reshape(shard_rows, -1)
    lateral_sum = rest[:, 0:taps].reshape(shard_rows, -1, 128).transpose(1, 2, 0)
    reduce_sum = rest[:, taps : taps + joined_width].T
    temporal_sum = rest[:, taps + joined_width :].reshape(shard_rows, 3, inner).transpose(1, 2, 0)
    us_half = in_order(us, after(us_other, g1))
    rim = in_order(edge_same.reshape(own, inner), edge_cross.reshape(own, inner))
    grad_half, grad_full = stepped(
        functools.partial(last_kernel, number, frames), "last", steps, [idx],
        all_of(mask_next, tot_a, after(back_a, grads_sent[1], grads_sent[2], shortcut_sum, small), lat_gain)
        + [by_block(x) for x in (us_half, side, rim.reshape(steps, half_block, inner), side_edge, u3, g1)]
        + all_of(lat_h, lat_l, fr_h, fr_l),
        [by_block(half_out), (full_out, part(full_out, half_block, in_half))],
        scratch=[cut(fr, inner)],
        est=cost(2 * 3 * nf * 1024 * 256, nf * 4 * 2000),
    )

    def fast_whole(mine, full):
        got = lax.ppermute(mine, "hh", swap)
        return by_pixel(lax.dynamic_update_slice_in_dim(full, got, half * (1 - h), axis=0))

    from_y = [lax.dynamic_index_in_dim(v, 1 - y, 0, keepdims=False) for v in from_y]
    slow_output = placed(after(slow_out, small), [near_rows] + from_y)
    fast_output = fast_whole(fast_half, after(fast_full, grad_half))
    fast_input_gradient = fast_whole(grad_half, grad_full)

    def fold(v):
        return jnp.sum(v.reshape(4, -1), axis=0)

    def zhat(back, tot, n, row_at=1, off=0):
        mean = tot[0, off:] / n
        return back[row_at] * lax.rsqrt(tot[1, off:] / n - mean * mean + EPSILON)

    def fast_pair(back, tot):
        sums = jnp.sum(tot.reshape(2, 4, -1), axis=1)
        bias = fold(back[0])
        mean = sums[0] / fast_number
        return fold(back[1]) * lax.rsqrt(sums[1] / fast_number - mean * mean + EPSILON), bias

    def shard(v):
        size = v.shape[0] // roles
        return lax.dynamic_slice_in_dim(v, m * size, size, axis=0)

    def slow_pair(back, tot, n=number, row_at=1, off=0, width=None):
        tot = tot[:, : width] if width else tot
        return shard(zhat(back, tot, n, row_at, off)), shard(back[0])

    fr_gg, fr_bg = fast_pair(back_f1, tot_f1)
    ft_gg, ft_bg = fast_pair(back_f2, tot_f2)
    fe_gg, fe_bg = fast_pair(back_f3, tot_f3)
    la_gg, la_bg = slow_pair(back_a, tot_a, number)
    re_gg, re_bg = slow_pair(back_f, tot_s, width=inner)
    te_gg, te_bg = slow_pair(back_m, tot_m)
    ex_gg, ex_bg = slow_pair(back_ls, tot_l)
    sh_gg, sh_bg = slow_pair(back_ls, tot_s, row_at=2, off=inner)
    return (
        slow_output, fast_output, slow_input_gradient, fast_input_gradient,
        small[32:64].reshape(128, 32), fr_gg, fr_bg,
        small[64:88].reshape(3, 32, 32), ft_gg, ft_bg,
        small[0:32], fe_gg, fe_bg,
        lateral_sum, la_gg, la_bg,
        reduce_sum, re_gg, re_bg,
        temporal_sum, te_gg, te_bg,
        expand_sum, ex_gg, ex_bg,
        shortcut_sum, sh_gg, sh_bg,
    )


def solution(mesh):
    dps, roles = mesh.shape["dp"], mesh.shape["mp"]
    sizes = (dps, roles // 2, 2)
    fine = Mesh(mesh.devices.reshape(sizes), ALL)
    mp = ROLE
    frames3 = P("dp", None, mp)
    fast3 = P("dp", None, None)
    none = P()
    in_specs = (
        (frames3, fast3) + (none,) * 10
        + (P(None, None, mp), P(mp), P(mp), P(None, mp), P(mp), P(mp), P(None, None, mp), P(mp), P(mp),
           P(mp, None), P(mp), P(mp), P(None, mp), P(mp), P(mp), frames3, fast3)
    )
    out_specs = (
        (frames3, fast3, frames3, fast3) + (none,) * 9
        + (P(None, None, mp), P(mp), P(mp), P(None, mp), P(mp), P(mp), P(None, None, mp), P(mp), P(mp),
           P(mp, None), P(mp), P(mp), P(None, mp), P(mp), P(mp))
    )
    return jax.shard_map(
        functools.partial(local, sizes), mesh=fine, in_specs=in_specs, out_specs=out_specs, check_vma=False
    )
```

```python
import functools

import jax
import jax.numpy as jnp
from jax import lax
from jax.experimental import pallas as pl
from jax.experimental.pallas import tpu as pltpu
from jax.sharding import Mesh, PartitionSpec as P

EPSILON = 1e-05
F32 = jnp.float32
BF16 = jnp.bfloat16
MESH = pl.DeviceIdType.MESH
LIMIT = 58 * 1024 * 1024
ROLE = ("yy", "hh")
ALL = ("dp", "yy", "hh")


def split(v):
    high = v.astype(BF16)
    return high, (v - high.astype(F32)).astype(BF16)


def dot(a, b, ca, cb):
    return lax.dot_general(a, b, (((ca,), (cb,)), ((), ())), preferred_element_type=F32)


def dot3(a, b, ca=1, cb=0):
    (ah, al), (bh, bl) = a, b
    return dot(ah, bh, ca, cb) + dot(ah, bl, ca, cb) + dot(al, bh, ca, cb)


def sigmoid(v):
    return 0.5 * jnp.tanh(0.5 * v) + 0.5


def silu(v):
    return v * sigmoid(v)


def slope(v):
    s = sigmoid(v)
    return s * (1.0 + v * (1.0 - s))


def colsum(v):
    return jnp.sum(v, axis=0, keepdims=True)


def moments(total, squares, number):
    mean = total * (1.0 / number)
    return mean, lax.rsqrt(squares * (1.0 / number) - mean * mean + EPSILON)


def back_terms(gain, mean, inverse, up, upz, number):
    alpha = gain * inverse
    beta = -alpha * inverse * (upz * inverse) * (1.0 / number)
    return alpha, beta, -alpha * up * (1.0 / number) - beta * mean


def fold32(v):
    return v + pltpu.roll(v, 32, 1) + pltpu.roll(v, 64, 1) + pltpu.roll(v, 96, 1)


def fold128(v):
    return v[:, 0:128] + v[:, 128:256] + v[:, 256:384] + v[:, 384:512]


def four(v):
    return jnp.concatenate([v, v, v, v], axis=1)


def rows_of(ref, g):
    pixels, count, lanes = ref.shape
    return ref[:, pl.ds(g, count // 4, stride=4), :].reshape(pixels * (count // 4), lanes)


def frames_of(ref):
    return jnp.concatenate([rows_of(ref, g) for g in range(4)], axis=1)


def masked(v, mask):
    frames = mask.shape[0]
    lanes = v.shape[1] // mask.shape[1]
    wide = mask[...] if lanes == 1 else jnp.concatenate([mask[...]] * lanes, axis=1)
    return (v.reshape(-1, frames, v.shape[1]) * wide[None]).reshape(v.shape)


def edge(ref, v, at, frames):
    rows = v.shape[0]
    parts = []
    for k in range(v.shape[1] // 128):
        ref[k] = v[:, 128 * k : 128 * (k + 1)]
        parts.append(ref[k, pl.ds(at, rows // frames, stride=frames), :])
    return jnp.concatenate(parts, axis=1)


def edges(ref, v, frames):
    rows = v.shape[0]
    first, last = [], []
    for k in range(v.shape[1] // 128):
        ref[k] = v[:, 128 * k : 128 * (k + 1)]
        first.append(ref[k, pl.ds(0, rows // frames, stride=frames), :])
        last.append(ref[k, pl.ds(frames - 1, rows // frames, stride=frames), :])
    return jnp.concatenate(first, axis=1), jnp.concatenate(last, axis=1)


def shifted(ref, v, step, frames, beyond):
    rows = v.shape[0]
    at = 0 if step == 1 else frames - 1
    parts = []
    for k in range(v.shape[1] // 128):
        lanes = slice(128 * k, 128 * (k + 1))
        ref[k] = pltpu.roll(v[:, lanes], 1 if step == 1 else rows - 1, 0)
        ref[k, pl.ds(at, rows // frames, stride=frames), :] = beyond[:, lanes]
        parts.append(ref[k])
    return jnp.concatenate(parts, axis=1)


def add_rows(ref, *rows):
    @pl.when(pl.program_id(0) == 0)
    def _():
        ref[...] = jnp.zeros_like(ref)

    for k, row in enumerate(rows):
        ref[k : k + 1, :] += row


def add_whole(ref, value):
    @pl.when(pl.program_id(0) == 0)
    def _():
        ref[...] = jnp.zeros_like(ref)

    ref[...] += value


def vmem():
    return pl.BlockSpec(memory_space=pltpu.VMEM)


def shape(*dims, dtype=F32):
    return jax.ShapeDtypeStruct(dims, dtype)


def cost(flops, nbytes):
    return pl.CostEstimate(flops=int(flops / 2), bytes_accessed=int(nbytes / 2), transcendentals=0)


def whole(x):
    rank = len(x.shape)
    return pl.BlockSpec(tuple(x.shape), lambda i, *s: (0,) * rank)


def part(x, rows, at=None):
    tail = (0,) * (len(x.shape) - 1)
    where = at or (lambda i, *s: i)
    return pl.BlockSpec((rows,) + tuple(x.shape[1:]), lambda i, *s: (where(i, *s),) + tail)


def stepped(body, name, steps, scalars, ins, outs, scratch=(), est=None):
    return pl.pallas_call(
        body,
        name=name,
        out_shape=[o for o, _ in outs],
        grid_spec=pltpu.PrefetchScalarGridSpec(
            num_scalar_prefetch=len(scalars),
            grid=(steps,),
            in_specs=[s for _, s in ins],
            out_specs=[s for _, s in outs],
            scratch_shapes=list(scratch),
        ),
        compiler_params=pltpu.CompilerParams(vmem_limit_bytes=LIMIT),
        cost_estimate=est,
    )(*scalars, *[a for a, _ in ins])


def sum_kernel(sizes, axes, widths, edges, *refs):
    dps, ys, hs = sizes
    roles = ys * hs if axes == ROLE else hs
    parts = len(widths)
    xs, refs = refs[:parts], refs[parts:]
    edge_in, refs = refs[:edges], refs[edges:]
    outs, refs = refs[:parts], refs[parts:]
    edge_out, refs = refs[:edges], refs[edges:]
    one_src, two_src, b1, b2, s1, r1, s2, r2 = refs[:8]
    d = lax.axis_index("dp")
    y = lax.axis_index("yy")
    h = lax.axis_index("hh")
    m = y * hs + h

    def role(i):
        if axes != ROLE:
            return {"hh": lax.rem(h + i, hs)}
        p = lax.rem(m + i, roles)
        return {"yy": p // hs, "hh": lax.rem(p, hs)}

    def along(i):
        return {"dp": lax.rem(d + i, dps)}

    def send(src, dst, ssem, rsem, to):
        c = pltpu.make_async_remote_copy(
            src_ref=src, dst_ref=dst, send_sem=ssem, recv_sem=rsem, device_id=to, device_id_type=MESH
        )
        c.start()
        return c

    bar = pltpu.get_barrier_semaphore()
    for i in range(1, roles):
        pl.semaphore_signal(bar, inc=1, device_id=role(i), device_id_type=MESH)
    for i in range(1, dps):
        pl.semaphore_signal(bar, inc=1, device_id=along(i), device_id_type=MESH)
    one_src[...] = jnp.zeros_like(one_src)
    start = 0
    for x, width in zip(xs, widths):
        one_src[start : start + x.shape[0], 0:width] = x[...]
        start += x.shape[0]
    pl.semaphore_wait(bar, roles + dps - 2)
    one = [send(one_src, b1.at[i - 1], s1.at[i - 1], r1.at[i - 1], role(i)) for i in range(1, roles)]
    rim = []
    if edges:
        s3, r3 = refs[8:]
        rim = [
            send(edge_in[k], edge_out[k], s3.at[k], r3.at[k], along(1 if k == 0 else dps - 1))
            for k in range(edges)
        ]
    acc = one_src[...]
    for i, c in enumerate(one):
        c.wait_recv()
        acc = acc + b1[i]
    two_src[...] = acc
    two = [send(two_src, b2.at[i - 1], s2.at[i - 1], r2.at[i - 1], along(i)) for i in range(1, dps)]
    for i, c in enumerate(two):
        c.wait_recv()
        acc = acc + b2[i]
    start = 0
    for o, width in zip(outs, widths):
        o[...] = acc[start : start + o.shape[0], 0:width]
        start += o.shape[0]
    for c in rim:
        c.wait_recv()
    for c in one + rim + two:
        c.wait_send()


def total(xs, cid, sizes, axes, rims=()):
    dps, ys, hs = sizes
    roles = ys * hs if axes == ROLE else hs
    widths = [x.shape[1] for x in xs]
    packed = (sum(x.shape[0] for x in xs), max(widths))
    dma = pltpu.SemaphoreType.DMA
    return pl.pallas_call(
        functools.partial(sum_kernel, sizes, axes, widths, len(rims)),
        name="sum%d" % cid,
        out_shape=[shape(*x.shape) for x in xs] + [shape(*r.shape) for r in rims],
        in_specs=[vmem()] * (len(xs) + len(rims)),
        out_specs=[vmem()] * (len(xs) + len(rims)),
        scratch_shapes=[
            pltpu.VMEM(packed, F32),
            pltpu.VMEM(packed, F32),
            pltpu.VMEM((roles - 1,) + packed, F32),
            pltpu.VMEM((dps - 1,) + packed, F32),
            dma((roles - 1,)), dma((roles - 1,)), dma((dps - 1,)), dma((dps - 1,)),
        ] + ([dma((2,)), dma((2,))] if rims else []),
        compiler_params=pltpu.CompilerParams(collective_id=cid, has_side_effects=True),
    )(*xs, *rims)


def last_sum_kernel(sizes, x_ref, v_ref, o_ref, w_ref, two_src, b1, b2, vb, s1, r1, s2, r2, s3, r3, s4, r4):
    dps, ys, hs = sizes
    d = lax.axis_index("dp")
    h = lax.axis_index("hh")

    def along(i):
        return lax.rem(d + i, dps)

    def send(src, dst, ssem, rsem, to):
        c = pltpu.make_async_remote_copy(
            src_ref=src, dst_ref=dst, send_sem=ssem, recv_sem=rsem, device_id=to, device_id_type=MESH
        )
        c.start()
        return c

    bar = pltpu.get_barrier_semaphore()
    other = {"hh": lax.rem(h + 1, hs)}
    pl.semaphore_signal(bar, inc=1, device_id=other, device_id_type=MESH)
    for i in range(1, dps):
        pl.semaphore_signal(bar, inc=1, device_id={"dp": along(i)}, device_id_type=MESH)
    pl.semaphore_wait(bar, dps)
    one = send(x_ref, b1, s1, r1, other)
    out = [
        send(v_ref.at[along(i)], vb.at[i - 1], s3.at[i - 1], r3.at[i - 1], {"dp": along(i)})
        for i in range(1, dps)
    ]
    one.wait_recv()
    acc = x_ref[...] + b1[...]
    two_src[...] = acc
    two = [send(two_src, b2.at[i - 1], s2.at[i - 1], r2.at[i - 1], {"dp": along(i)}) for i in range(1, dps)]
    piece = v_ref[d]
    for i, c in enumerate(out):
        c.wait_recv()
        piece = piece + vb[i]
    w_ref[d] = piece
    back = [
        send(w_ref.at[d], w_ref.at[d], s4.at[i - 1], r4.at[i - 1], {"dp": along(i)}) for i in range(1, dps)
    ]
    for i, c in enumerate(two):
        c.wait_recv()
        acc = acc + b2[i]
    o_ref[...] = acc
    for c in back:
        c.wait_recv()
    one.wait_send()
    for c in out + two + back:
        c.wait_send()


def last_total(x, v, cid, sizes):
    dps, ys, hs = sizes
    dma = pltpu.SemaphoreType.DMA
    return pl.pallas_call(
        functools.partial(last_sum_kernel, sizes),
        name="sum%d" % cid,
        out_shape=[shape(*x.shape), shape(*v.shape)],
        in_specs=[vmem()] * 2,
        out_specs=[vmem()] * 2,
        scratch_shapes=[
            pltpu.VMEM(x.shape, F32),
            pltpu.VMEM(x.shape, F32),
            pltpu.VMEM((dps - 1,) + x.shape, F32),
            pltpu.VMEM((dps - 1,) + v.shape[1:], F32),
            dma, dma,
        ] + [dma((dps - 1,))] * 6,
        compiler_params=pltpu.CompilerParams(collective_id=cid, has_side_effects=True),
    )(x, v)


def fast1_kernel(frames, idx, x_ref, rh, rl, p_ref, e0, e1, st, tmp):
    p = dot3(split(frames_of(x_ref)), (rh[...], rl[...]))
    p_ref[...] = p
    e0[0], e1[0] = edges(tmp, p, frames)
    add_rows(st, colsum(p), colsum(p * p))


def lateral_taps(frames, mask, x_ref, halo, bz):
    x = [rows_of(x_ref, g) for g in range(4)]
    beyond = jnp.concatenate([halo[:, 6, :], halo[:, 7, :]], axis=1)
    early = shifted(bz, jnp.concatenate([x[2], x[3]], axis=1), 1, frames, beyond)
    return jnp.concatenate([masked(early, mask), x[0], x[1], x[2]], axis=1)


def lateral_kernel(frames, idx, mask, x_ref, halo, wh, wl, s_ref, e0, st, bz):
    p = dot3(split(lateral_taps(frames, mask, x_ref, halo, bz)), (wh[...], wl[...]), 1, 1)
    s_ref[...] = p
    e0[0] = edge(bz, p, 0, frames)
    add_rows(st, colsum(p), colsum(p * p))


def fast_norm(tot, number):
    return moments(fold32(tot[0:1, :]), fold32(tot[1:2, :]), number)


def wide_norm(tot, number):
    return moments(fold128(tot[0:1, :]), fold128(tot[1:2, :]), number)


def rims_of(v, prev, nxt):
    lane = lax.broadcasted_iota(jnp.int32, v.shape, 1)
    return jnp.where(lane >= 96, prev, jnp.where(lane < 32, nxt, 0.0))


def fast2_kernel(
    number, frames, mp, mn, tot, gain, bias, p1, before, after, wh, wl, a_ref, z_ref, p2, st, zp, zn
):
    mean, inverse = fast_norm(tot, number)
    scale = gain[...] * inverse
    shift = bias[...] - mean * scale
    a = silu(p1[...] * scale + shift)
    a_ref[...] = a
    prev = shifted(zp, a, 1, frames, silu(before[0] * scale + shift))
    nxt = shifted(zn, a, -1, frames, silu(after[0] * scale + shift))
    z = rims_of(a, masked(prev, mp), masked(nxt, mn))
    z_ref[...] = z
    p = dot3(split(jnp.concatenate([a, z], axis=1)), (wh[...], wl[...]))
    p2[...] = p
    add_rows(st, colsum(p), colsum(p * p))


def fast3_kernel(number, tot, gain, bias, p2, eh, el, b_ref, st):
    mean, inverse = fast_norm(tot, number)
    scale = gain[...] * inverse
    b = silu(p2[...] * scale + (bias[...] - mean * scale))
    b_ref[...] = b
    p = dot3(split(b), (eh[...], el[...]))
    add_rows(st, colsum(p), colsum(p * p))


def put_frames(ref, v):
    pixels, count, lanes = ref.shape
    for g in range(4):
        ref[:, pl.ds(g, count // 4, stride=4), :] = v[:, lanes * g : lanes * (g + 1)].reshape(
            pixels, count // 4, lanes
        )


def fast4_kernel(number, share, idx, tot, gain, bias, x_ref, c_ref, b_ref, eh, el, o_ref, f_ref, u_ref, st):
    mean, inverse = wide_norm(tot, number)
    scale = gain[...] * inverse
    shift = bias[...] - mean * scale
    p = dot3(split(b_ref[...]), (eh[...], el[...]))
    j = p * four(scale) + four(shift) + frames_of(x_ref)
    s = sigmoid(j)
    out = j * s
    put_frames(o_ref, out)
    put_frames(f_ref, out)
    u = frames_of(c_ref) * (s * (1.0 + j * (1.0 - s)))
    u_ref[...] = u
    add_rows(st, share * colsum(u), share * colsum(u * (p - four(mean))))


def fast5_kernel(
    number, frames, tot, back, gain, tot2, gain2, bias2, u_ref, b_ref, p2, eh, el, u2, eg, e0, e1, st, tmp
):
    mean, inverse = wide_norm(tot, number)
    alpha, beta, gamma = back_terms(
        gain[...], mean, inverse, fold128(back[0:1, :]), fold128(back[1:2, :]), number
    )
    bs = split(b_ref[...])
    e = (eh[...], el[...])
    g = split(four(alpha) * u_ref[...] + four(beta) * dot3(bs, e) + four(gamma))
    add_whole(eg, dot3(bs, g, 0, 0))
    v = dot3(g, e, 1, 1)
    mean2, inverse2 = fast_norm(tot2, number)
    z = p2[...] - mean2
    u = v * slope(z * (inverse2 * gain2[...]) + bias2[...])
    u2[...] = u
    e0[0, 0], e1[0, 0] = edges(tmp, u, frames)
    e0[0, 1], e1[0, 1] = edges(tmp, p2[...], frames)
    add_rows(st, colsum(u), colsum(u * z))


def fast6_kernel(
    number, frames, mp, mn, tot2, back2, gain2, tot1, gain1, bias1, u2, p2, before, after, a, z, p1,
    wh, wl, u1, tg, st, zp, zn
):
    mean2, inverse2 = fast_norm(tot2, number)
    alpha, beta, gamma = back_terms(
        gain2[...], mean2, inverse2, fold32(back2[0:1, :]), fold32(back2[1:2, :]), number
    )
    g = alpha * u2[...] + beta * p2[...] + gamma
    prev = shifted(zp, g, 1, frames, alpha * before[0, 0] + beta * before[0, 1] + gamma)
    nxt = shifted(zn, g, -1, frames, alpha * after[0, 0] + beta * after[0, 1] + gamma)
    gz = rims_of(g, masked(prev, mp), masked(nxt, mn))
    add_whole(tg, dot3(split(jnp.concatenate([a[...], z[...]], axis=1)), split(g), 0, 0))
    v = dot3(split(jnp.concatenate([g, gz], axis=1)), (wh[...], wl[...]), 1, 1)
    mean1, inverse1 = fast_norm(tot1, number)
    c = p1[...] - mean1
    u = v * slope(c * (gain1[...] * inverse1) + bias1[...])
    u1[...] = u
    add_rows(st, colsum(u), colsum(u * c))


def fast7_kernel(number, idx, tot1, back1, gain1, x_ref, u1, p1, g1, rg):
    mean, inverse = fast_norm(tot1, number)
    alpha, beta, gamma = back_terms(
        gain1[...], mean, inverse, fold32(back1[0:1, :]), fold32(back1[1:2, :]), number
    )
    g = alpha * u1[...] + beta * p1[...] + gamma
    g1[...] = g
    add_whole(rg, dot3(split(frames_of(x_ref)), split(g), 0, 0))


def slow1_kernel(
    number, frames, idx, tot, gain, bias, x0, x1, x2, x3, side, rh, rl, sh, sl,
    first, short, jh, jl, e0, e1, st, wide, tmp
):
    lanes = x0.shape[1]
    for r, x in enumerate((x0, x1, x2, x3)):
        at = pl.multiple_of(idx[3 + r] * lanes, lanes)
        wide[:, pl.ds(at, lanes)] = x[...]
    mean, inverse = moments(tot[0:1, :], tot[1:2, :], number)
    scale = gain[...] * inverse
    top = sh.shape[0] * lanes
    wide[:, top:] = silu(side[...] * scale + (bias[...] - mean * scale))
    joined = split(wide[...])
    jh[0], jl[0] = joined
    p = dot3(joined, (rh[...], rl[...]), 1, 1)
    first[...] = p
    e0[0], e1[0] = edges(tmp, p, frames)
    sums = [colsum(p)]
    squares = [colsum(p * p)]
    for n in range(sh.shape[0]):
        p = dot3(joined, (sh[n], sl[n]))
        short[:, n * lanes : (n + 1) * lanes] = p
        sums.append(colsum(p))
        squares.append(colsum(p * p))
    add_rows(st, jnp.concatenate(sums, axis=1), jnp.concatenate(squares, axis=1))


def slow2_kernel(
    number, frames, mp, mn, tot, gain, bias, first, before, after, wh, wl, th, tl, pm, st, zp, zn
):
    width = gain.shape[1]
    mean, inverse = moments(tot[0:1, 0:width], tot[1:2, 0:width], number)
    scale = gain[...] * inverse
    shift = bias[...] - mean * scale
    a = silu(first[...] * scale + shift)
    prev = shifted(zp, a, 1, frames, silu(before[0] * scale + shift))
    nxt = shifted(zn, a, -1, frames, silu(after[0] * scale + shift))
    taps = split(jnp.concatenate([masked(prev, mp), a, masked(nxt, mn)], axis=1))
    th[0], tl[0] = taps
    p = dot3(taps, (wh[...], wl[...]), 1, 1)
    pm[...] = p
    add_rows(st, colsum(p), colsum(p * p))


def slow3_kernel(number, tot, gain, bias, pm, eh, el, bh, bl, st):
    mean, inverse = moments(tot[0:1, :], tot[1:2, :], number)
    scale = gain[...] * inverse
    b = split(silu(pm[...] * scale + (bias[...] - mean * scale)))
    bh[0], bl[0] = b
    p = dot3(b, (eh[...], el[...]))
    add_rows(st, colsum(p), colsum(p * p))


def slow4_kernel(
    number, idx, tot_l, tot_s, gain_l, bias_l, gain_s, bias_s, bh, bl, short, c0, c1, c2, c3, eh, el,
    o0, o1, o2, o3, u_ref, st, wide
):
    lanes = c0.shape[1]
    for r, c in enumerate((c0, c1, c2, c3)):
        at = pl.multiple_of(idx[3 + r] * lanes, lanes)
        wide[:, pl.ds(at, lanes)] = c[...]
    off = tot_s.shape[1] - short.shape[1]
    bs = (bh[0], bl[0])
    sums = []
    for n in range(short.shape[1] // lanes):
        at = slice(n * lanes, (n + 1) * lanes)
        mean_l, inv_l = moments(tot_l[0:1, at], tot_l[1:2, at], number)
        far = slice(off + n * lanes, off + (n + 1) * lanes)
        mean_s, inv_s = moments(tot_s[0:1, far], tot_s[1:2, far], number)
        zl = dot3(bs, (eh[:, at], el[:, at])) - mean_l
        zs = short[:, at] - mean_s
        j = zl * (inv_l * gain_l[:, at]) + zs * (inv_s * gain_s[:, at]) + (bias_l[:, at] + bias_s[:, at])
        s = sigmoid(j)
        u = wide[:, at] * (s * (1.0 + j * (1.0 - s)))
        u_ref[:, at] = u
        sums.append((colsum(u), colsum(u * zl), colsum(u * zs)))
        wide[:, at] = j * s
    for r, o in enumerate((o0, o1, o2, o3)):
        at = pl.multiple_of(idx[3 + r] * lanes, lanes)
        o[...] = wide[:, pl.ds(at, lanes)]
    add_rows(st, *[jnp.concatenate(rows, axis=1) for rows in zip(*sums)])


def slow5_kernel(
    number, frames, tot_l, back, gain_l, tot_m, gain_m, bias_m, u_ref, bh, bl, pm, eh, el,
    um, eg, e0, e1, st, tmp
):
    mean, inverse = moments(tot_l[0:1, :], tot_l[1:2, :], number)
    alpha, beta, gamma = back_terms(gain_l[...], mean, inverse, back[0:1, :], back[1:2, :], number)
    bs = (bh[0], bl[0])
    e = (eh[...], el[...])
    g = split(alpha * u_ref[...] + beta * dot3(bs, e) + gamma)
    add_whole(eg, dot3(bs, g, 0, 0))
    v = dot3(g, e, 1, 1)
    mean_m, inv_m = moments(tot_m[0:1, :], tot_m[1:2, :], number)
    z = pm[...] - mean_m
    u = v * slope(z * (inv_m * gain_m[...]) + bias_m[...])
    um[...] = u
    e0[0, 0], e1[0, 0] = edges(tmp, u, frames)
    e0[0, 1], e1[0, 1] = edges(tmp, pm[...], frames)
    add_rows(st, colsum(u), colsum(u * z))


def slow6_kernel(number, tot_s, back, gain_s, u_ref, short, jh, jl, sh, sl, dx, grads):
    off = tot_s.shape[1] - short.shape[1]
    mean, inverse = moments(tot_s[0:1, off:], tot_s[1:2, off:], number)
    alpha, beta, gamma = back_terms(gain_s[...], mean, inverse, back[0:1, :], back[2:3, :], number)
    lanes = sh.shape[2]
    joined = (jh[0], jl[0])

    @pl.when(pl.program_id(0) == 0)
    def _():
        grads[...] = jnp.zeros_like(grads)

    out = None
    for n in range(sh.shape[0]):
        at = slice(n * lanes, (n + 1) * lanes)
        g = split(alpha[:, at] * u_ref[:, at] + beta[:, at] * short[:, at] + gamma[:, at])
        grads[n] += dot3(joined, g, 0, 0)
        part = dot3(g, (sh[n], sl[n]), 1, 1)
        out = part if out is None else out + part
    dx[...] = out


def slow7_kernel(
    number, frames, mp, mn, tot_m, back, gain_m, tot_f, gain_f, bias_f, um, pm, before, after, th, tl,
    first, wh, wl, uf, tg, st, zp, zn
):
    mean, inverse = moments(tot_m[0:1, :], tot_m[1:2, :], number)
    alpha, beta, gamma = back_terms(gain_m[...], mean, inverse, back[0:1, :], back[1:2, :], number)
    g = alpha * um[...] + beta * pm[...] + gamma
    prev = shifted(zp, g, 1, frames, alpha * before[0, 0] + beta * before[0, 1] + gamma)
    nxt = shifted(zn, g, -1, frames, alpha * after[0, 0] + beta * after[0, 1] + gamma)
    gs = split(g)
    add_whole(tg, dot3(gs, (th[0], tl[0]), 0, 0))
    width = gain_f.shape[1]
    v = dot3(split(masked(nxt, mn)), (wh[:, 0:width], wl[:, 0:width]))
    v += dot3(gs, (wh[:, width : 2 * width], wl[:, width : 2 * width]))
    v += dot3(split(masked(prev, mp)), (wh[:, 2 * width :], wl[:, 2 * width :]))
    mean_f, inv_f = moments(tot_f[0:1, 0:width], tot_f[1:2, 0:width], number)
    z = first[...] - mean_f
    u = v * slope(z * (gain_f[...] * inv_f) + bias_f[...])
    uf[...] = u
    add_rows(st, colsum(u), colsum(u * z))


def slow8_kernel(
    number, frames, idx, tot_f, back, gain_f, tot_a, gain_a, bias_a, uf, first, jh, jl, dx, side,
    rh, rl, o0, o1, o2, o3, us, rg, e0, st, wide, tmp
):
    width = gain_f.shape[1]
    mean, inverse = moments(tot_f[0:1, 0:width], tot_f[1:2, 0:width], number)
    alpha, beta, gamma = back_terms(gain_f[...], mean, inverse, back[0:1, :], back[1:2, :], number)
    g = split(alpha * uf[...] + beta * first[...] + gamma)
    add_whole(rg, dot3(g, (jh[0], jl[0]), 0, 0))
    lanes = o0.shape[1]
    wide[...] = dx[...] + dot3(g, (rh[...], rl[...]))
    for r, o in enumerate((o0, o1, o2, o3)):
        at = pl.multiple_of(idx[3 + r] * lanes, lanes)
        o[...] = wide[:, pl.ds(at, lanes)]
    mean_a, inv_a = moments(tot_a[0:1, :], tot_a[1:2, :], number)
    z = side[...] - mean_a
    top = wide.shape[1] - width
    u = wide[:, top:] * slope(z * (inv_a * gain_a[...]) + bias_a[...])
    us[...] = u
    e0[0] = edge(tmp, u, 0, frames)
    add_rows(st, colsum(u), colsum(u * z))


def side_terms(number, tot_a, back, gain_a):
    mean, inverse = moments(tot_a[0:1, :], tot_a[1:2, :], number)
    return back_terms(gain_a[...], mean, inverse, back[0:1, :], back[1:2, :], number)


def slow9_kernel(number, frames, idx, mask, tot_a, back, gain_a, us, side, x_ref, halo, lg, bz):
    alpha, beta, gamma = side_terms(number, tot_a, back, gain_a)
    g = split(alpha * us[...] + beta * side[...] + gamma)
    add_whole(lg, dot3(g, split(lateral_taps(frames, mask, x_ref, halo, bz)), 0, 0))


def last_kernel(
    number, frames, idx, mask, tot_a, back, gain_a, us, side, us_edge, side_edge, u3, g1, wh, wl,
    rh, rl, o_ref, f_ref, zn
):
    alpha, beta, gamma = side_terms(number, tot_a, back, gain_a)
    here = alpha * us[...] + beta * side[...] + gamma
    after = shifted(zn, here, -1, frames, alpha * us_edge[0] + beta * side_edge[0] + gamma)
    base = u3[...] + dot3(split(g1[...]), (rh[...], rl[...]), 1, 1)
    near = dot3(split(here), (wh[:, 256:], wl[:, 256:]))
    far = dot3(split(masked(after, mask)), (wh[:, 0:256], wl[:, 0:256]))
    both = jnp.concatenate(
        [near[:, 0:256], near[:, 256:384] + far[:, 0:128], far[:, 128:256]], axis=1
    )
    out = base + both
    put_frames(o_ref, out)
    put_frames(f_ref, out)


def weight_split(w):
    high = lax.reduce_precision(w, 8, 7)
    return high.astype(BF16), (w - high).astype(BF16)


def row(v):
    return v.reshape(1, -1)


def tiled_row(v):
    return jnp.tile(v.reshape(1, -1), (1, 4))


def by_pixel(v):
    return v.transpose(1, 0, 2)


def after(value, *events):
    return lax.optimization_barrier((value,) + events)[0]


def local(sizes, *args):
    (
        slow_input, fast_input, clip_starts,
        fast_reduce, fast_reduce_gain, fast_reduce_bias,
        fast_temporal, fast_temporal_gain, fast_temporal_bias,
        fast_expand, fast_expand_gain, fast_expand_bias,
        lateral_conv, lateral_gain, lateral_bias,
        slow_reduce, slow_reduce_gain, slow_reduce_bias,
        slow_temporal, slow_temporal_gain, slow_temporal_bias,
        slow_expand, slow_expand_gain, slow_expand_bias,
        shortcut_conv, shortcut_gain, shortcut_bias,
        slow_cotangent, fast_cotangent,
    ) = args
    dps, ys, hs = sizes
    roles = ys * hs
    d, y, h = (lax.axis_index(a) for a in ALL)
    m = y * hs + h
    frames, pixels, lanes = slow_input.shape
    shard_rows = slow_reduce.shape[1]
    inner = shard_rows * roles
    joined_width = slow_reduce.shape[0]
    wide = lanes * roles
    number = frames * dps * pixels
    fast_number = number * 4
    half = pixels // hs
    own = pixels // roles
    steps = 7
    half_block, own_block = half // steps, own // steps
    fast_rows, slow_rows = half_block * frames, own_block * frames

    slow_x = by_pixel(slow_input).reshape(pixels * frames, lanes)
    slow_c = by_pixel(slow_cotangent).reshape(pixels * frames, lanes)
    fast_x = by_pixel(fast_input)
    fast_c = by_pixel(fast_cotangent)

    def block_of(p):
        return (p % hs) * ys + p // hs

    def role_xor(r):
        return (y ^ (r // hs)) * hs + (h ^ (r % hs))

    peers = [role_xor(r) for r in range(roles)]
    q = block_of(m)
    idx = jnp.stack([h, q, y] + peers).astype(jnp.int32)
    own_rows = own * frames
    row_at = [own_rows * block_of(p) for p in peers]

    times = d * frames + jnp.arange(0, frames + 1, dtype=jnp.int32)

    def clip_of(t):
        return jnp.sum((clip_starts[None, :] <= t[:, None]).astype(jnp.int32), axis=1) - 1

    same = jnp.logical_and(
        clip_of(times) == clip_of(times - 1), jnp.logical_and(times >= 1, times < frames * dps)
    ).astype(F32)
    mask_prev = jnp.broadcast_to(same[:frames, None], (frames, 128))
    mask_next = jnp.broadcast_to(same[1:, None], (frames, 128))

    def role_pairs(r):
        return [(i, i ^ r) for i in range(roles)]

    def placed(out, got):
        for r in range(1, roles):
            out = lax.dynamic_update_slice_in_dim(out, got[r - 1], row_at[r], axis=0)
        return by_pixel(out.reshape(pixels, frames, lanes))

    swap = [(0, 1), (1, 0)]
    half_rows = half * frames

    def from_core(array):
        return lax.ppermute(
            lax.dynamic_slice_in_dim(array, half_rows * (1 - h), half_rows, axis=0), "hh", swap
        )

    def for_partner(array, here):
        return [
            lax.dynamic_slice_in_dim(array, half_rows * h + own_rows * (1 - y), own_rows, axis=0),
            lax.dynamic_slice_in_dim(here, own_rows * (1 - y), own_rows, axis=0),
        ]

    sho_y = lax.ppermute(shortcut_conv, "yy", swap)
    in_core = from_core(slow_x)
    in_send = jnp.concatenate(for_partner(slow_x, in_core), axis=0)
    in_y = lax.ppermute(in_send, "yy", swap)

    vectors = [
        lateral_gain, lateral_bias, slow_reduce_gain, slow_reduce_bias, slow_temporal_gain,
        slow_temporal_bias, slow_expand_gain, slow_expand_bias, shortcut_gain, shortcut_bias,
    ]
    vector = jnp.concatenate(vectors)
    share = shard_rows // dps
    across = -(-vector.shape[0] // (share * 128)) * 128
    vector = jnp.pad(vector, (0, share * across - vector.shape[0])).reshape(share, across)
    piece = jnp.concatenate(
        [
            lateral_conv.transpose(2, 0, 1).reshape(shard_rows, -1),
            slow_reduce.T,
            slow_temporal.transpose(2, 0, 1).reshape(shard_rows, -1),
            slow_expand,
        ],
        axis=1,
    )
    piece = jnp.concatenate([lax.dynamic_slice_in_dim(piece, d * share, share, axis=0), vector], axis=1)
    got = lax.all_gather(piece, ALL, axis=0, tiled=False).reshape((dps, roles) + piece.shape)
    matrix = got[:, :, :, : piece.shape[1] - across].transpose(1, 0, 2, 3).reshape(inner, -1)
    taps = lateral_conv.shape[0] * lateral_conv.shape[1]
    bounds = [0, taps, taps + joined_width, taps + joined_width + 3 * inner]
    bounds.append(bounds[-1] + wide)
    (lat_h, lat_l), (red_h, red_l), (tem_h, tem_l), (exp_h, exp_l) = [
        weight_split(matrix[:, bounds[k] : bounds[k + 1]]) for k in range(4)
    ]
    vector = got[0, :, :, piece.shape[1] - across :].reshape(roles, -1)
    full = []
    start = 0
    for v in vectors:
        full.append(vector[:, start : start + v.shape[0]].reshape(1, -1))
        start += v.shape[0]
    (
        lat_gain, lat_bias, red_gain, red_bias, tem_gain, tem_bias, exp_gain, exp_bias, sho_gain, sho_bias
    ) = full

    eye = jnp.eye(4, dtype=F32)
    up = jnp.eye(4, k=1, dtype=F32)
    down = jnp.eye(4, k=-1, dtype=F32)
    far_next = jnp.eye(4, k=3, dtype=F32)
    far_prev = jnp.eye(4, k=-3, dtype=F32)
    fr_h, fr_l = weight_split(after(jnp.kron(eye, fast_reduce), in_send))
    fe_h, fe_l = weight_split(jnp.kron(eye, fast_expand))
    centre = jnp.kron(eye, fast_temporal[1]) + jnp.kron(up, fast_temporal[0]) + jnp.kron(down, fast_temporal[2])
    outer = jnp.kron(far_next, fast_temporal[2]) + jnp.kron(far_prev, fast_temporal[0])
    ft_h, ft_l = weight_split(jnp.concatenate([centre, outer], axis=0))
    fb_h, fb_l = weight_split(jnp.concatenate([centre, outer], axis=1))
    fr_gain, fr_bias = tiled_row(fast_reduce_gain), tiled_row(fast_reduce_bias)
    ft_gain, ft_bias = tiled_row(fast_temporal_gain), tiled_row(fast_temporal_bias)
    fe_gain, fe_bias = row(fast_expand_gain), row(fast_expand_bias)

    forth = [(i, i + 1) for i in range(dps - 1)]
    backw = [(i + 1, i) for i in range(dps - 1)]
    halo = lax.dynamic_slice(fast_x, (half * h, frames * 4 - 8, 0), (half, 8, 128))
    halo = lax.ppermute(halo, "dp", forth)

    in_half = lambda i, s, *_: s[0] * steps + i
    in_own = lambda i, s, *_: s[1] * steps + i
    own_in_half = lambda i, s, *_: s[2] * steps + i

    def all_of(*arrays):
        return [(x, whole(x)) for x in arrays]

    def const(*dims):
        o = shape(*dims)
        return (o, whole(o))

    def by_block(x, at=None):
        return (x, part(x, x.shape[0] // steps, at))

    def out_rows(rows, width):
        return by_block(shape(rows * steps, width))

    def out_blocks(*dims, dtype=F32):
        return by_block(shape(steps, *dims, dtype=dtype))

    def tmp(*dims):
        return pltpu.VMEM(dims, F32)

    def cut(rows, width):
        return tmp(width // 128, rows, 128)

    other_y = lambda i, s, *_: (1 - s[2]) * steps + i

    fr, sr = fast_rows, slow_rows
    nf, ns = fr * steps, sr * steps
    fx = (fast_x, part(fast_x, half_block, in_half))
    fc = (fast_c, part(fast_c, half_block, in_half))
    masks = all_of(mask_prev, mask_next)
    core = ("hh",)

    p1, e0, e1, st = stepped(
        functools.partial(fast1_kernel, frames), "fast1", steps, [idx], [fx] + all_of(fr_h, fr_l),
        [out_rows(fr, 128), out_blocks(half_block, 128), out_blocks(half_block, 128), const(2, 128)],
        scratch=[cut(fr, 128)],
        est=cost(2 * 3 * nf * 512 * 256, nf * 640 * 4),
    )
    st_f1 = st
    tot_f1, before, beyond = total([st], 1, sizes, core, (e1, e0))
    a1, z1, p2, st = stepped(
        functools.partial(fast2_kernel, fast_number, frames), "fast2", steps, [],
        masks + all_of(tot_f1, fr_gain, fr_bias)
        + [by_block(p1), by_block(before), by_block(beyond)] + all_of(ft_h, ft_l),
        [out_rows(fr, 128)] * 3 + [const(2, 128)],
        scratch=[cut(fr, 128)] * 2,
        est=cost(2 * 3 * nf * 256 * 256, 4 * nf * 128 * 4),
    )
    (tot_f2,) = total([st], 2, sizes, core)

    def role_table(mine, from_y, event):
        column = jnp.stack([after(mine, event), from_y])
        other = lax.ppermute(column, "hh", swap)
        table = jnp.stack([column[0], other[0], column[1], other[1]])
        return jnp.stack([lax.dynamic_index_in_dim(table, p, 0, keepdims=False) for p in peers])

    sho_h, sho_l = weight_split(role_table(shortcut_conv, sho_y, tot_f1))
    cot_core = from_core(after(slow_c, tot_f1))
    slow_cot = [cot_core] + [
        lax.all_gather(after(v, matrix), "yy", axis=0, tiled=True) for v in for_partner(slow_c, cot_core)
    ]
    side, side_edge, st_a = stepped(
        functools.partial(lateral_kernel, frames), "lateral", steps, [idx],
        all_of(mask_prev) + [fx, by_block(halo)] + all_of(after(lat_h, st), lat_l),
        [out_rows(fr, inner), out_blocks(half_block, inner), const(2, inner)],
        scratch=[cut(fr, 256)],
        est=cost(2 * 3 * nf * 768 * 256, nf * 768 * 4),
    )
    side_edge = lax.ppermute(side_edge, "dp", backw)
    b1, st = stepped(
        functools.partial(fast3_kernel, fast_number), "fast3", steps, [],
        all_of(tot_f2, ft_gain, ft_bias) + [by_block(p2)] + all_of(fe_h, fe_l),
        [out_rows(fr, 128), const(2, 512)],
        est=cost(2 * 3 * nf * 256 * 512, 2 * nf * 128 * 4),
    )
    tot_f3, tot_a = total([st, st_a], 3, sizes, core)
    half_out = shape(half, frames * 4, 128)
    full_out = shape(pixels, frames * 4, 128)
    fast_half, fast_full, u3, st_f4 = stepped(
        functools.partial(fast4_kernel, fast_number, 1.0 / ys), "fast4", steps, [idx],
        all_of(tot_f3, fe_gain, fe_bias) + [fx, fc, by_block(b1)] + all_of(fe_h, fe_l),
        [by_block(half_out), (full_out, part(full_out, half_block, in_half)), out_rows(fr, 512), const(2, 512)],
        est=cost(2 * 3 * nf * 256 * 512, nf * 5 * 512 * 4),
    )

    side_own = (side, part(side, slow_rows, own_in_half))
    sx = (slow_x, part(slow_x, slow_rows, in_own))
    sc = (slow_c, part(slow_c, slow_rows, in_own))
    bf_joined = out_blocks(sr, joined_width, dtype=BF16)
    first, short, jh, jl, e0, e1, st = stepped(
        functools.partial(slow1_kernel, number, frames), "slow1", steps, [idx],
        all_of(after(tot_a, st_f4), lat_gain, lat_bias) + [sx, (in_core, part(in_core, slow_rows, own_in_half))]
        + [(in_y, part(in_y, slow_rows, at)) for at in (lambda i, *s: i, lambda i, *s: steps + i)]
        + [side_own]
        + all_of(red_h, red_l, sho_h, sho_l),
        [
            out_rows(sr, inner), out_rows(sr, wide), bf_joined, bf_joined,
            out_blocks(own_block, inner), out_blocks(own_block, inner), const(2, inner + wide),
        ],
        scratch=[tmp(sr, joined_width), cut(sr, inner)],
        est=cost(2 * 3 * ns * 1280 * 1280, ns * 4 * 3840 + 7e6),
    )
    tot_s, back_f3, before, beyond = total([st, st_f4], 8, sizes, ROLE, (e1, e0))
    bf_taps = out_blocks(sr, 3 * inner, dtype=BF16)
    wide_masks = all_of(*[jnp.concatenate([v, v], axis=1) for v in (mask_prev, mask_next)])
    th, tl, pm, st = stepped(
        functools.partial(slow2_kernel, number, frames), "slow2", steps, [],
        wide_masks + all_of(tot_s, red_gain, red_bias) + [by_block(x) for x in (first, before, beyond)]
        + all_of(tem_h, tem_l),
        [bf_taps, bf_taps, out_rows(sr, inner), const(2, inner)],
        scratch=[cut(sr, inner)] * 2,
        est=cost(2 * 3 * ns * 768 * 256, ns * 4 * 1500),
    )
    (tot_m,) = total([st], 9, sizes, ROLE)
    bf_mid = out_blocks(sr, inner, dtype=BF16)
    bh, bl, st = stepped(
        functools.partial(slow3_kernel, number), "slow3", steps, [],
        all_of(tot_m, tem_gain, tem_bias) + [by_block(pm)] + all_of(exp_h, exp_l),
        [bf_mid, bf_mid, const(2, wide)],
        est=cost(2 * 3 * ns * 1024 * 256, ns * 4 * 512),
    )
    (tot_l,) = total([st], 10, sizes, ROLE)
    slow_full = shape(pixels * frames, lanes)
    own_out = (slow_full, part(slow_full, slow_rows, in_own))
    *outs, u, st = stepped(
        functools.partial(slow4_kernel, number), "slow4", steps, [idx],
        all_of(tot_l, tot_s, exp_gain, exp_bias, sho_gain, sho_bias)
        + [by_block(x) for x in (bh, bl, short)] + [sc]
        + [(slow_cot[0], part(slow_cot[0], slow_rows, own_in_half))]
        + [(x, part(x, slow_rows, other_y)) for x in slow_cot[1:]]
        + all_of(exp_h, exp_l),
        [own_out] + [out_rows(sr, lanes)] * (roles - 1) + [out_rows(sr, wide), const(4, wide)],
        scratch=[tmp(sr, wide)],
        est=cost(2 * 3 * ns * 1024 * 256, ns * 4 * 4352),
    )
    (back_ls,) = total([st], 11, sizes, ROLE)
    near_rows = lax.ppermute(outs[1], "hh", swap)
    far_rows = lax.ppermute(outs[3], "hh", swap)
    from_y = [lax.all_gather(v, "yy", axis=0, tiled=False) for v in (outs[2], far_rows)]

    dx, short_grads = stepped(
        functools.partial(slow6_kernel, number), "slow6", steps, [],
        all_of(tot_s, back_ls, sho_gain) + [by_block(x) for x in (u, short, jh, jl)] + all_of(sho_h, sho_l),
        [out_rows(sr, joined_width), const(roles, joined_width, lanes)],
        est=cost(2 * 6 * ns * 1280 * 1024, ns * 4 * 4600 + 12e6),
    )
    um, expand_grad, e0, e1, st = stepped(
        functools.partial(slow5_kernel, number, frames), "slow5", steps, [],
        all_of(tot_l, after(back_ls, dx), exp_gain, tot_m, tem_gain, tem_bias)
        + [by_block(x) for x in (u, bh, bl, pm)] + all_of(exp_h, exp_l),
        [
            out_rows(sr, inner), const(inner, wide), out_blocks(2, own_block, inner),
            out_blocks(2, own_block, inner), const(2, inner),
        ],
        scratch=[cut(sr, inner)],
        est=cost(2 * 9 * ns * 1024 * 256, ns * 4 * 1800),
    )
    slow_out = outs[0]
    back_m, before, beyond = total([st], 12, sizes, ROLE, (e1, e0))
    def by_peer(g):
        rows = g.shape[0] // roles
        parts = [lax.dynamic_slice_in_dim(g, p * rows, rows, axis=0) for p in peers]
        return jnp.stack([parts[0], parts[2]]), jnp.stack([parts[1], parts[3]])

    def chip_sum(near, far):
        return near + lax.ppermute(far, "hh", swap)

    expand_pair = lax.psum_scatter(
        after(expand_grad, *from_y).reshape(roles, shard_rows, wide), ROLE, scatter_dimension=0, tiled=False
    )
    short_pair = lax.psum_scatter(after(short_grads, *from_y), ROLE, scatter_dimension=0, tiled=False)
    uf, temporal_grad, st = stepped(
        functools.partial(slow7_kernel, number, frames), "slow7", steps, [],
        wide_masks + all_of(tot_m, back_m, tem_gain, tot_s, red_gain, red_bias)
        + [by_block(x) for x in (um, pm, before, beyond, th, tl, first)] + all_of(tem_h, tem_l),
        [out_rows(sr, inner), const(inner, 3 * inner), const(2, inner)],
        scratch=[cut(sr, inner)] * 2,
        est=cost(2 * 6 * ns * 768 * 256, ns * 4 * 1500),
    )
    (back_f,) = total([st], 13, sizes, ROLE)
    *outs, us, reduce_grad, us_edge, st = stepped(
        functools.partial(slow8_kernel, number, frames), "slow8", steps, [idx],
        all_of(tot_s, back_f, red_gain, tot_a, lat_gain, lat_bias)
        + [by_block(x) for x in (uf, first, jh, jl, dx)] + [side_own] + all_of(red_h, red_l),
        [own_out] + [out_rows(sr, lanes)] * (roles - 1)
        + [out_rows(sr, inner), const(inner, joined_width), out_blocks(own_block, inner), const(2, inner)],
        scratch=[tmp(sr, joined_width), cut(sr, inner)],
        est=cost(2 * 6 * ns * 1280 * 256, ns * 4 * 5000),
    )
    (back_a,) = total([st], 14, sizes, ROLE)
    shortcut_sum, expand_sum = lax.psum((short_pair, expand_pair), "dp")
    edge_sent = after(us_edge, back_a)
    edge_same = lax.ppermute(edge_sent, "dp", backw)
    edge_cross = lax.ppermute(
        edge_sent, ("dp", "yy"), [(i * ys + j, (i - 1) * ys + 1 - j) for i in range(1, dps) for j in range(ys)]
    )

    own_halo = (halo, part(halo, own_block, own_in_half))
    (lateral_grad,) = stepped(
        functools.partial(slow9_kernel, number, frames), "slow9", steps, [idx],
        all_of(mask_prev, tot_a, back_a, lat_gain)
        + [by_block(us), side_own, (fast_x, part(fast_x, own_block, in_own)), own_halo],
        [const(inner, 640)],
        scratch=[cut(sr, 256)],
        est=cost(2 * 3 * ns * 640 * 256, ns * 4 * 1500),
    )

    both = chip_sum(*by_peer(jnp.concatenate([lateral_grad, reduce_grad, temporal_grad], axis=1)))
    rest_y = lax.ppermute(both[1], "yy", swap)
    us_other = lax.ppermute(after(us, both), "yy", swap)

    u2, expand_packed, e0, e1, st = stepped(
        functools.partial(fast5_kernel, fast_number, frames), "fast5", steps, [],
        all_of(tot_f3, after(back_f3, back_a, both, short_pair, expand_pair), fe_gain, tot_f2, ft_gain, ft_bias)
        + [by_block(u3), by_block(b1), by_block(p2)] + all_of(fe_h, fe_l),
        [
            out_rows(fr, 128), const(128, 512), out_blocks(2, half_block, 128),
            out_blocks(2, half_block, 128), const(2, 128),
        ],
        scratch=[cut(fr, 128)],
        est=cost(2 * 9 * nf * 256 * 512, nf * 900 * 4),
    )
    rest = both[0] + after(rest_y, u2)
    back_f2, before, beyond = total([st], 5, sizes, core, (e1, e0))
    grads_sent = [
        lax.ppermute(after(outs[r], back_a if r == 1 else rest), ROLE, role_pairs(r))
        for r in range(1, roles)
    ]
    slow_input_gradient = placed(outs[0], grads_sent)

    u1, temporal_packed, st = stepped(
        functools.partial(fast6_kernel, fast_number, frames), "fast6", steps, [],
        masks + all_of(tot_f2, after(back_f2, rest), ft_gain, tot_f1, fr_gain, fr_bias)
        + [by_block(x) for x in (u2, p2, before, beyond, a1, z1, p1)] + all_of(fb_h, fb_l),
        [out_rows(fr, 128), const(256, 128), const(2, 128)],
        scratch=[cut(fr, 128)] * 2,
        est=cost(2 * 6 * nf * 256 * 256, 6 * nf * 128 * 4),
    )
    (back_f1,) = total([st], 6, sizes, core)
    g1, reduce_packed = stepped(
        functools.partial(fast7_kernel, fast_number), "fast7", steps, [idx],
        all_of(tot_f1, after(back_f1, us_other), fr_gain) + [fx, by_block(u1), by_block(p1)],
        [out_rows(fr, 128), const(512, 128)],
        est=cost(2 * 3 * nf * 512 * 256, nf * 900 * 4),
    )

    def in_order(mine, other):
        return jnp.concatenate([jnp.where(y == 0, mine, other), jnp.where(y == 0, other, mine)], axis=0)

    eb = expand_packed.reshape(4, 32, 4, 128)
    expand_small = eb[0, :, 0] + eb[1, :, 1] + eb[2, :, 2] + eb[3, :, 3]
    rb = reduce_packed.reshape(4, 128, 4, 32)
    reduce_small = rb[0, :, 0] + rb[1, :, 1] + rb[2, :, 2] + rb[3, :, 3]
    tb = temporal_packed.reshape(8, 32, 4, 32)
    tap0 = tb[0, :, 1] + tb[1, :, 2] + tb[2, :, 3] + tb[7, :, 0]
    tap1 = tb[0, :, 0] + tb[1, :, 1] + tb[2, :, 2] + tb[3, :, 3]
    tap2 = tb[1, :, 0] + tb[2, :, 1] + tb[3, :, 2] + tb[4, :, 3]
    small = jnp.concatenate(
        [expand_small, reduce_small.reshape(32, 128), jnp.stack([tap0, tap1, tap2]).reshape(24, 128)], axis=0
    )
    small, rest = last_total(small, rest.reshape(dps, -1, rest.shape[1]), 15, sizes)
    rest = rest.reshape(shard_rows, -1)
    lateral_sum = rest[:, 0:taps].reshape(shard_rows, -1, 128).transpose(1, 2, 0)
    reduce_sum = rest[:, taps : taps + joined_width].T
    temporal_sum = rest[:, taps + joined_width :].reshape(shard_rows, 3, inner).transpose(1, 2, 0)
    us_half = in_order(us, after(us_other, g1))
    rim = in_order(edge_same.reshape(own, inner), edge_cross.reshape(own, inner))
    grad_half, grad_full = stepped(
        functools.partial(last_kernel, number, frames), "last", steps, [idx],
        all_of(mask_next, tot_a, after(back_a, grads_sent[1], grads_sent[2], shortcut_sum, small), lat_gain)
        + [by_block(x) for x in (us_half, side, rim.reshape(steps, half_block, inner), side_edge, u3, g1)]
        + all_of(lat_h, lat_l, fr_h, fr_l),
        [by_block(half_out), (full_out, part(full_out, half_block, in_half))],
        scratch=[cut(fr, inner)],
        est=cost(2 * 3 * nf * 1024 * 256, nf * 4 * 2000),
    )

    def fast_whole(mine, full):
        got = lax.ppermute(mine, "hh", swap)
        return by_pixel(lax.dynamic_update_slice_in_dim(full, got, half * (1 - h), axis=0))

    from_y = [lax.dynamic_index_in_dim(v, 1 - y, 0, keepdims=False) for v in from_y]
    slow_output = placed(after(slow_out, small), [near_rows] + from_y)
    fast_output = fast_whole(after(fast_half, small), after(fast_full, small))
    fast_input_gradient = fast_whole(grad_half, grad_full)

    def fold(v):
        return jnp.sum(v.reshape(4, -1), axis=0)

    def zhat(back, tot, n, row_at=1, off=0):
        mean = tot[0, off:] / n
        return back[row_at] * lax.rsqrt(tot[1, off:] / n - mean * mean + EPSILON)

    def fast_pair(back, tot):
        sums = jnp.sum(tot.reshape(2, 4, -1), axis=1)
        bias = fold(back[0])
        mean = sums[0] / fast_number
        return fold(back[1]) * lax.rsqrt(sums[1] / fast_number - mean * mean + EPSILON), bias

    def shard(v):
        size = v.shape[0] // roles
        return lax.dynamic_slice_in_dim(v, m * size, size, axis=0)

    def slow_pair(back, tot, n=number, row_at=1, off=0, width=None):
        tot = tot[:, : width] if width else tot
        return shard(zhat(back, tot, n, row_at, off)), shard(back[0])

    fr_gg, fr_bg = fast_pair(back_f1, tot_f1)
    ft_gg, ft_bg = fast_pair(back_f2, tot_f2)
    fe_gg, fe_bg = fast_pair(back_f3, tot_f3)
    la_gg, la_bg = slow_pair(back_a, tot_a, number)
    re_gg, re_bg = slow_pair(back_f, tot_s, width=inner)
    te_gg, te_bg = slow_pair(back_m, tot_m)
    ex_gg, ex_bg = slow_pair(back_ls, tot_l)
    sh_gg, sh_bg = slow_pair(back_ls, tot_s, row_at=2, off=inner)
    return (
        slow_output, fast_output, slow_input_gradient, fast_input_gradient,
        small[32:64].reshape(128, 32), fr_gg, fr_bg,
        small[64:88].reshape(3, 32, 32), ft_gg, ft_bg,
        small[0:32], fe_gg, fe_bg,
        lateral_sum, la_gg, la_bg,
        reduce_sum, re_gg, re_bg,
        temporal_sum, te_gg, te_bg,
        expand_sum, ex_gg, ex_bg,
        shortcut_sum, sh_gg, sh_bg,
    )


def solution(mesh):
    dps, roles = mesh.shape["dp"], mesh.shape["mp"]
    sizes = (dps, roles // 2, 2)
    fine = Mesh(mesh.devices.reshape(sizes), ALL)
    mp = ROLE
    frames3 = P("dp", None, mp)
    fast3 = P("dp", None, None)
    none = P()
    in_specs = (
        (frames3, fast3) + (none,) * 10
        + (P(None, None, mp), P(mp), P(mp), P(None, mp), P(mp), P(mp), P(None, None, mp), P(mp), P(mp),
           P(mp, None), P(mp), P(mp), P(None, mp), P(mp), P(mp), frames3, fast3)
    )
    out_specs = (
        (frames3, fast3, frames3, fast3) + (none,) * 9
        + (P(None, None, mp), P(mp), P(mp), P(None, mp), P(mp), P(mp), P(None, None, mp), P(mp), P(mp),
           P(mp, None), P(mp), P(mp), P(None, mp), P(mp), P(mp))
    )
    return jax.shard_map(
        functools.partial(local, sizes), mesh=fine, in_specs=in_specs, out_specs=out_specs, check_vma=False
    )
```

```python
import functools

import jax
import jax.numpy as jnp
from jax import lax
from jax.experimental import pallas as pl
from jax.experimental.pallas import tpu as pltpu
from jax.sharding import Mesh, PartitionSpec as P

EPSILON = 1e-05
F32 = jnp.float32
BF16 = jnp.bfloat16
MESH = pl.DeviceIdType.MESH
LIMIT = 58 * 1024 * 1024
ROLE = ("yy", "hh")
ALL = ("dp", "yy", "hh")


def split(v):
    high = v.astype(BF16)
    return high, (v - high.astype(F32)).astype(BF16)


def dot(a, b, ca, cb):
    return lax.dot_general(a, b, (((ca,), (cb,)), ((), ())), preferred_element_type=F32)


def dot3(a, b, ca=1, cb=0):
    (ah, al), (bh, bl) = a, b
    return dot(ah, bh, ca, cb) + dot(ah, bl, ca, cb) + dot(al, bh, ca, cb)


def sigmoid(v):
    return 0.5 * jnp.tanh(0.5 * v) + 0.5


def silu(v):
    return v * sigmoid(v)


def slope(v):
    s = sigmoid(v)
    return s * (1.0 + v * (1.0 - s))


def colsum(v):
    return jnp.sum(v, axis=0, keepdims=True)


def moments(total, squares, number):
    mean = total * (1.0 / number)
    return mean, lax.rsqrt(squares * (1.0 / number) - mean * mean + EPSILON)


def back_terms(gain, mean, inverse, up, upz, number):
    alpha = gain * inverse
    beta = -alpha * inverse * (upz * inverse) * (1.0 / number)
    return alpha, beta, -alpha * up * (1.0 / number) - beta * mean


def fold32(v):
    return v + pltpu.roll(v, 32, 1) + pltpu.roll(v, 64, 1) + pltpu.roll(v, 96, 1)


def fold128(v):
    return v[:, 0:128] + v[:, 128:256] + v[:, 256:384] + v[:, 384:512]


def four(v):
    return jnp.concatenate([v, v, v, v], axis=1)


def rows_of(ref, g):
    pixels, count, lanes = ref.shape
    return ref[:, pl.ds(g, count // 4, stride=4), :].reshape(pixels * (count // 4), lanes)


def frames_of(ref):
    return jnp.concatenate([rows_of(ref, g) for g in range(4)], axis=1)


def masked(v, mask):
    frames = mask.shape[0]
    lanes = v.shape[1] // mask.shape[1]
    wide = mask[...] if lanes == 1 else jnp.concatenate([mask[...]] * lanes, axis=1)
    return (v.reshape(-1, frames, v.shape[1]) * wide[None]).reshape(v.shape)


def edge(ref, v, at, frames):
    rows = v.shape[0]
    parts = []
    for k in range(v.shape[1] // 128):
        ref[k] = v[:, 128 * k : 128 * (k + 1)]
        parts.append(ref[k, pl.ds(at, rows // frames, stride=frames), :])
    return jnp.concatenate(parts, axis=1)


def edges(ref, v, frames):
    rows = v.shape[0]
    first, last = [], []
    for k in range(v.shape[1] // 128):
        ref[k] = v[:, 128 * k : 128 * (k + 1)]
        first.append(ref[k, pl.ds(0, rows // frames, stride=frames), :])
        last.append(ref[k, pl.ds(frames - 1, rows // frames, stride=frames), :])
    return jnp.concatenate(first, axis=1), jnp.concatenate(last, axis=1)


def shifted(ref, v, step, frames, beyond):
    rows = v.shape[0]
    at = 0 if step == 1 else frames - 1
    parts = []
    for k in range(v.shape[1] // 128):
        lanes = slice(128 * k, 128 * (k + 1))
        ref[k] = pltpu.roll(v[:, lanes], 1 if step == 1 else rows - 1, 0)
        ref[k, pl.ds(at, rows // frames, stride=frames), :] = beyond[:, lanes]
        parts.append(ref[k])
    return jnp.concatenate(parts, axis=1)


def add_rows(ref, *rows):
    @pl.when(pl.program_id(0) == 0)
    def _():
        ref[...] = jnp.zeros_like(ref)

    for k, row in enumerate(rows):
        ref[k : k + 1, :] += row


def add_whole(ref, value):
    @pl.when(pl.program_id(0) == 0)
    def _():
        ref[...] = jnp.zeros_like(ref)

    ref[...] += value


def vmem():
    return pl.BlockSpec(memory_space=pltpu.VMEM)


def shape(*dims, dtype=F32):
    return jax.ShapeDtypeStruct(dims, dtype)


def cost(flops, nbytes):
    return pl.CostEstimate(flops=int(flops / 2), bytes_accessed=int(nbytes / 2), transcendentals=0)


def whole(x):
    rank = len(x.shape)
    return pl.BlockSpec(tuple(x.shape), lambda i, *s: (0,) * rank)


def part(x, rows, at=None):
    tail = (0,) * (len(x.shape) - 1)
    where = at or (lambda i, *s: i)
    return pl.BlockSpec((rows,) + tuple(x.shape[1:]), lambda i, *s: (where(i, *s),) + tail)


def stepped(body, name, steps, scalars, ins, outs, scratch=(), est=None):
    return pl.pallas_call(
        body,
        name=name,
        out_shape=[o for o, _ in outs],
        grid_spec=pltpu.PrefetchScalarGridSpec(
            num_scalar_prefetch=len(scalars),
            grid=(steps,),
            in_specs=[s for _, s in ins],
            out_specs=[s for _, s in outs],
            scratch_shapes=list(scratch),
        ),
        compiler_params=pltpu.CompilerParams(vmem_limit_bytes=LIMIT),
        cost_estimate=est,
    )(*scalars, *[a for a, _ in ins])


def sum_kernel(sizes, axes, widths, edges, *refs):
    dps, ys, hs = sizes
    roles = ys * hs if axes == ROLE else hs
    parts = len(widths)
    xs, refs = refs[:parts], refs[parts:]
    edge_in, refs = refs[:edges], refs[edges:]
    outs, refs = refs[:parts], refs[parts:]
    edge_out, refs = refs[:edges], refs[edges:]
    one_src, two_src, b1, b2, s1, r1, s2, r2 = refs[:8]
    d = lax.axis_index("dp")
    y = lax.axis_index("yy")
    h = lax.axis_index("hh")
    m = y * hs + h

    def role(i):
        if axes != ROLE:
            return {"hh": lax.rem(h + i, hs)}
        p = lax.rem(m + i, roles)
        return {"yy": p // hs, "hh": lax.rem(p, hs)}

    def along(i):
        return {"dp": lax.rem(d + i, dps)}

    def send(src, dst, ssem, rsem, to):
        c = pltpu.make_async_remote_copy(
            src_ref=src, dst_ref=dst, send_sem=ssem, recv_sem=rsem, device_id=to, device_id_type=MESH
        )
        c.start()
        return c

    bar = pltpu.get_barrier_semaphore()
    for i in range(1, roles):
        pl.semaphore_signal(bar, inc=1, device_id=role(i), device_id_type=MESH)
    for i in range(1, dps):
        pl.semaphore_signal(bar, inc=1, device_id=along(i), device_id_type=MESH)
    one_src[...] = jnp.zeros_like(one_src)
    start = 0
    for x, width in zip(xs, widths):
        one_src[start : start + x.shape[0], 0:width] = x[...]
        start += x.shape[0]
    pl.semaphore_wait(bar, roles + dps - 2)
    one = [send(one_src, b1.at[i - 1], s1.at[i - 1], r1.at[i - 1], role(i)) for i in range(1, roles)]
    rim = []
    if edges:
        s3, r3 = refs[8:]
        rim = [
            send(edge_in[k], edge_out[k], s3.at[k], r3.at[k], along(1 if k == 0 else dps - 1))
            for k in range(edges)
        ]
    acc = one_src[...]
    for i, c in enumerate(one):
        c.wait_recv()
        acc = acc + b1[i]
    two_src[...] = acc
    two = [send(two_src, b2.at[i - 1], s2.at[i - 1], r2.at[i - 1], along(i)) for i in range(1, dps)]
    for i, c in enumerate(two):
        c.wait_recv()
        acc = acc + b2[i]
    start = 0
    for o, width in zip(outs, widths):
        o[...] = acc[start : start + o.shape[0], 0:width]
        start += o.shape[0]
    for c in rim:
        c.wait_recv()
    for c in one + rim + two:
        c.wait_send()


def total(xs, cid, sizes, axes, rims=()):
    dps, ys, hs = sizes
    roles = ys * hs if axes == ROLE else hs
    widths = [x.shape[1] for x in xs]
    packed = (sum(x.shape[0] for x in xs), max(widths))
    dma = pltpu.SemaphoreType.DMA
    return pl.pallas_call(
        functools.partial(sum_kernel, sizes, axes, widths, len(rims)),
        name="sum%d" % cid,
        out_shape=[shape(*x.shape) for x in xs] + [shape(*r.shape) for r in rims],
        in_specs=[vmem()] * (len(xs) + len(rims)),
        out_specs=[vmem()] * (len(xs) + len(rims)),
        scratch_shapes=[
            pltpu.VMEM(packed, F32),
            pltpu.VMEM(packed, F32),
            pltpu.VMEM((roles - 1,) + packed, F32),
            pltpu.VMEM((dps - 1,) + packed, F32),
            dma((roles - 1,)), dma((roles - 1,)), dma((dps - 1,)), dma((dps - 1,)),
        ] + ([dma((2,)), dma((2,))] if rims else []),
        compiler_params=pltpu.CompilerParams(collective_id=cid, has_side_effects=True),
    )(*xs, *rims)


def last_sum_kernel(sizes, x_ref, v_ref, o_ref, w_ref, two_src, b1, b2, vb, s1, r1, s2, r2, s3, r3, s4, r4, s5, r5):
    dps, ys, hs = sizes
    d = lax.axis_index("dp")
    h = lax.axis_index("hh")

    def along(i):
        return lax.rem(d + i, dps)

    def send(src, dst, ssem, rsem, to):
        c = pltpu.make_async_remote_copy(
            src_ref=src, dst_ref=dst, send_sem=ssem, recv_sem=rsem, device_id=to, device_id_type=MESH
        )
        c.start()
        return c

    bar = pltpu.get_barrier_semaphore()
    other = {"hh": lax.rem(h + 1, hs)}
    pl.semaphore_signal(bar, inc=1, device_id=other, device_id_type=MESH)
    for i in range(1, dps):
        pl.semaphore_signal(bar, inc=1, device_id={"dp": along(i)}, device_id_type=MESH)
    pl.semaphore_wait(bar, dps)
    one = send(x_ref, b1, s1, r1, other)
    out = [
        send(v_ref.at[along(i)], vb.at[i - 1], s3.at[i - 1], r3.at[i - 1], {"dp": along(i)})
        for i in range(1, dps)
    ]
    one.wait_recv()
    acc = x_ref[...] + b1[...]
    two_src[...] = acc
    two = [
        send(two_src.at[along(i)], b2.at[i - 1], s2.at[i - 1], r2.at[i - 1], {"dp": along(i)})
        for i in range(1, dps)
    ]
    piece = v_ref[d]
    for i, c in enumerate(out):
        c.wait_recv()
        piece = piece + vb[i]
    w_ref[d] = piece
    back = [
        send(w_ref.at[d], w_ref.at[d], s4.at[i - 1], r4.at[i - 1], {"dp": along(i)}) for i in range(1, dps)
    ]
    piece = two_src[d]
    for i, c in enumerate(two):
        c.wait_recv()
        piece = piece + b2[i]
    o_ref[d] = piece
    last = [
        send(o_ref.at[d], o_ref.at[d], s5.at[i - 1], r5.at[i - 1], {"dp": along(i)}) for i in range(1, dps)
    ]
    for c in back + last:
        c.wait_recv()
    one.wait_send()
    for c in out + two + back + last:
        c.wait_send()


def last_total(x, v, cid, sizes):
    dps, ys, hs = sizes
    dma = pltpu.SemaphoreType.DMA
    return pl.pallas_call(
        functools.partial(last_sum_kernel, sizes),
        name="sum%d" % cid,
        out_shape=[shape(*x.shape), shape(*v.shape)],
        in_specs=[vmem()] * 2,
        out_specs=[vmem()] * 2,
        scratch_shapes=[
            pltpu.VMEM(x.shape, F32),
            pltpu.VMEM(x.shape, F32),
            pltpu.VMEM((dps - 1,) + x.shape[1:], F32),
            pltpu.VMEM((dps - 1,) + v.shape[1:], F32),
            dma, dma,
        ] + [dma((dps - 1,))] * 8,
        compiler_params=pltpu.CompilerParams(collective_id=cid, has_side_effects=True),
    )(x, v)


def fast1_kernel(frames, idx, x_ref, rh, rl, p_ref, e0, e1, st, tmp):
    p = dot3(split(frames_of(x_ref)), (rh[...], rl[...]))
    p_ref[...] = p
    e0[0], e1[0] = edges(tmp, p, frames)
    add_rows(st, colsum(p), colsum(p * p))


def lateral_taps(frames, mask, x_ref, halo, bz):
    x = [rows_of(x_ref, g) for g in range(4)]
    beyond = jnp.concatenate([halo[:, 6, :], halo[:, 7, :]], axis=1)
    early = shifted(bz, jnp.concatenate([x[2], x[3]], axis=1), 1, frames, beyond)
    return jnp.concatenate([masked(early, mask), x[0], x[1], x[2]], axis=1)


def lateral_kernel(frames, idx, mask, x_ref, halo, wh, wl, s_ref, e0, st, bz):
    p = dot3(split(lateral_taps(frames, mask, x_ref, halo, bz)), (wh[...], wl[...]), 1, 1)
    s_ref[...] = p
    e0[0] = edge(bz, p, 0, frames)
    add_rows(st, colsum(p), colsum(p * p))


def fast_norm(tot, number):
    return moments(fold32(tot[0:1, :]), fold32(tot[1:2, :]), number)


def wide_norm(tot, number):
    return moments(fold128(tot[0:1, :]), fold128(tot[1:2, :]), number)


def rims_of(v, prev, nxt):
    lane = lax.broadcasted_iota(jnp.int32, v.shape, 1)
    return jnp.where(lane >= 96, prev, jnp.where(lane < 32, nxt, 0.0))


def fast2_kernel(
    number, frames, mp, mn, tot, gain, bias, p1, before, after, wh, wl, a_ref, z_ref, p2, st, zp, zn
):
    mean, inverse = fast_norm(tot, number)
    scale = gain[...] * inverse
    shift = bias[...] - mean * scale
    a = silu(p1[...] * scale + shift)
    a_ref[...] = a
    prev = shifted(zp, a, 1, frames, silu(before[0] * scale + shift))
    nxt = shifted(zn, a, -1, frames, silu(after[0] * scale + shift))
    z = rims_of(a, masked(prev, mp), masked(nxt, mn))
    z_ref[...] = z
    p = dot3(split(jnp.concatenate([a, z], axis=1)), (wh[...], wl[...]))
    p2[...] = p
    add_rows(st, colsum(p), colsum(p * p))


def fast3_kernel(number, tot, gain, bias, p2, eh, el, b_ref, st):
    mean, inverse = fast_norm(tot, number)
    scale = gain[...] * inverse
    b = silu(p2[...] * scale + (bias[...] - mean * scale))
    b_ref[...] = b
    p = dot3(split(b), (eh[...], el[...]))
    add_rows(st, colsum(p), colsum(p * p))


def put_frames(ref, v):
    pixels, count, lanes = ref.shape
    for g in range(4):
        ref[:, pl.ds(g, count // 4, stride=4), :] = v[:, lanes * g : lanes * (g + 1)].reshape(
            pixels, count // 4, lanes
        )


def fast4_kernel(number, share, idx, tot, gain, bias, x_ref, c_ref, b_ref, eh, el, o_ref, f_ref, u_ref, st):
    mean, inverse = wide_norm(tot, number)
    scale = gain[...] * inverse
    shift = bias[...] - mean * scale
    p = dot3(split(b_ref[...]), (eh[...], el[...]))
    j = p * four(scale) + four(shift) + frames_of(x_ref)
    s = sigmoid(j)
    out = j * s
    put_frames(o_ref, out)
    put_frames(f_ref, out)
    u = frames_of(c_ref) * (s * (1.0 + j * (1.0 - s)))
    u_ref[...] = u
    add_rows(st, share * colsum(u), share * colsum(u * (p - four(mean))))


def fast5_kernel(
    number, frames, tot, back, gain, tot2, gain2, bias2, u_ref, b_ref, p2, eh, el, u2, eg, e0, e1, st, tmp
):
    mean, inverse = wide_norm(tot, number)
    alpha, beta, gamma = back_terms(
        gain[...], mean, inverse, fold128(back[0:1, :]), fold128(back[1:2, :]), number
    )
    bs = split(b_ref[...])
    e = (eh[...], el[...])
    g = split(four(alpha) * u_ref[...] + four(beta) * dot3(bs, e) + four(gamma))
    add_whole(eg, dot3(bs, g, 0, 0))
    v = dot3(g, e, 1, 1)
    mean2, inverse2 = fast_norm(tot2, number)
    z = p2[...] - mean2
    u = v * slope(z * (inverse2 * gain2[...]) + bias2[...])
    u2[...] = u
    e0[0, 0], e1[0, 0] = edges(tmp, u, frames)
    e0[0, 1], e1[0, 1] = edges(tmp, p2[...], frames)
    add_rows(st, colsum(u), colsum(u * z))


def fast6_kernel(
    number, frames, mp, mn, tot2, back2, gain2, tot1, gain1, bias1, u2, p2, before, after, a, z, p1,
    wh, wl, u1, tg, st, zp, zn
):
    mean2, inverse2 = fast_norm(tot2, number)
    alpha, beta, gamma = back_terms(
        gain2[...], mean2, inverse2, fold32(back2[0:1, :]), fold32(back2[1:2, :]), number
    )
    g = alpha * u2[...] + beta * p2[...] + gamma
    prev = shifted(zp, g, 1, frames, alpha * before[0, 0] + beta * before[0, 1] + gamma)
    nxt = shifted(zn, g, -1, frames, alpha * after[0, 0] + beta * after[0, 1] + gamma)
    gz = rims_of(g, masked(prev, mp), masked(nxt, mn))
    add_whole(tg, dot3(split(jnp.concatenate([a[...], z[...]], axis=1)), split(g), 0, 0))
    v = dot3(split(jnp.concatenate([g, gz], axis=1)), (wh[...], wl[...]), 1, 1)
    mean1, inverse1 = fast_norm(tot1, number)
    c = p1[...] - mean1
    u = v * slope(c * (gain1[...] * inverse1) + bias1[...])
    u1[...] = u
    add_rows(st, colsum(u), colsum(u * c))


def fast7_kernel(number, idx, tot1, back1, gain1, x_ref, u1, p1, g1, rg):
    mean, inverse = fast_norm(tot1, number)
    alpha, beta, gamma = back_terms(
        gain1[...], mean, inverse, fold32(back1[0:1, :]), fold32(back1[1:2, :]), number
    )
    g = alpha * u1[...] + beta * p1[...] + gamma
    g1[...] = g
    add_whole(rg, dot3(split(frames_of(x_ref)), split(g), 0, 0))


def slow1_kernel(
    number, frames, idx, tot, gain, bias, x0, x1, x2, x3, side, rh, rl, sh, sl,
    first, short, jh, jl, e0, e1, st, wide, tmp
):
    lanes = x0.shape[1]
    for r, x in enumerate((x0, x1, x2, x3)):
        at = pl.multiple_of(idx[3 + r] * lanes, lanes)
        wide[:, pl.ds(at, lanes)] = x[...]
    mean, inverse = moments(tot[0:1, :], tot[1:2, :], number)
    scale = gain[...] * inverse
    top = sh.shape[0] * lanes
    wide[:, top:] = silu(side[...] * scale + (bias[...] - mean * scale))
    joined = split(wide[...])
    jh[0], jl[0] = joined
    p = dot3(joined, (rh[...], rl[...]), 1, 1)
    first[...] = p
    e0[0], e1[0] = edges(tmp, p, frames)
    sums = [colsum(p)]
    squares = [colsum(p * p)]
    for n in range(sh.shape[0]):
        p = dot3(joined, (sh[n], sl[n]))
        short[:, n * lanes : (n + 1) * lanes] = p
        sums.append(colsum(p))
        squares.append(colsum(p * p))
    add_rows(st, jnp.concatenate(sums, axis=1), jnp.concatenate(squares, axis=1))


def slow2_kernel(
    number, frames, mp, mn, tot, gain, bias, first, before, after, wh, wl, th, tl, pm, st, zp, zn
):
    width = gain.shape[1]
    mean, inverse = moments(tot[0:1, 0:width], tot[1:2, 0:width], number)
    scale = gain[...] * inverse
    shift = bias[...] - mean * scale
    a = silu(first[...] * scale + shift)
    prev = shifted(zp, a, 1, frames, silu(before[0] * scale + shift))
    nxt = shifted(zn, a, -1, frames, silu(after[0] * scale + shift))
    taps = split(jnp.concatenate([masked(prev, mp), a, masked(nxt, mn)], axis=1))
    th[0], tl[0] = taps
    p = dot3(taps, (wh[...], wl[...]), 1, 1)
    pm[...] = p
    add_rows(st, colsum(p), colsum(p * p))


def slow3_kernel(number, tot, gain, bias, pm, eh, el, bh, bl, st):
    mean, inverse = moments(tot[0:1, :], tot[1:2, :], number)
    scale = gain[...] * inverse
    b = split(silu(pm[...] * scale + (bias[...] - mean * scale)))
    bh[0], bl[0] = b
    p = dot3(b, (eh[...], el[...]))
    add_rows(st, colsum(p), colsum(p * p))


def slow4_kernel(
    number, idx, tot_l, tot_s, gain_l, bias_l, gain_s, bias_s, bh, bl, short, c0, c1, c2, c3, eh, el,
    o0, o1, o2, o3, u_ref, st, wide
):
    lanes = c0.shape[1]
    for r, c in enumerate((c0, c1, c2, c3)):
        at = pl.multiple_of(idx[3 + r] * lanes, lanes)
        wide[:, pl.ds(at, lanes)] = c[...]
    off = tot_s.shape[1] - short.shape[1]
    bs = (bh[0], bl[0])
    sums = []
    for n in range(short.shape[1] // lanes):
        at = slice(n * lanes, (n + 1) * lanes)
        mean_l, inv_l = moments(tot_l[0:1, at], tot_l[1:2, at], number)
        far = slice(off + n * lanes, off + (n + 1) * lanes)
        mean_s, inv_s = moments(tot_s[0:1, far], tot_s[1:2, far], number)
        zl = dot3(bs, (eh[:, at], el[:, at])) - mean_l
        zs = short[:, at] - mean_s
        j = zl * (inv_l * gain_l[:, at]) + zs * (inv_s * gain_s[:, at]) + (bias_l[:, at] + bias_s[:, at])
        s = sigmoid(j)
        u = wide[:, at] * (s * (1.0 + j * (1.0 - s)))
        u_ref[:, at] = u
        sums.append((colsum(u), colsum(u * zl), colsum(u * zs)))
        wide[:, at] = j * s
    for r, o in enumerate((o0, o1, o2, o3)):
        at = pl.multiple_of(idx[3 + r] * lanes, lanes)
        o[...] = wide[:, pl.ds(at, lanes)]
    add_rows(st, *[jnp.concatenate(rows, axis=1) for rows in zip(*sums)])


def slow5_kernel(
    number, frames, tot_l, back, gain_l, tot_m, gain_m, bias_m, u_ref, bh, bl, pm, eh, el,
    um, eg, e0, e1, st, tmp
):
    mean, inverse = moments(tot_l[0:1, :], tot_l[1:2, :], number)
    alpha, beta, gamma = back_terms(gain_l[...], mean, inverse, back[0:1, :], back[1:2, :], number)
    bs = (bh[0], bl[0])
    e = (eh[...], el[...])
    g = split(alpha * u_ref[...] + beta * dot3(bs, e) + gamma)
    add_whole(eg, dot3(bs, g, 0, 0))
    v = dot3(g, e, 1, 1)
    mean_m, inv_m = moments(tot_m[0:1, :], tot_m[1:2, :], number)
    z = pm[...] - mean_m
    u = v * slope(z * (inv_m * gain_m[...]) + bias_m[...])
    um[...] = u
    e0[0, 0], e1[0, 0] = edges(tmp, u, frames)
    e0[0, 1], e1[0, 1] = edges(tmp, pm[...], frames)
    add_rows(st, colsum(u), colsum(u * z))


def slow6_kernel(number, tot_s, back, gain_s, u_ref, short, jh, jl, sh, sl, dx, grads):
    off = tot_s.shape[1] - short.shape[1]
    mean, inverse = moments(tot_s[0:1, off:], tot_s[1:2, off:], number)
    alpha, beta, gamma = back_terms(gain_s[...], mean, inverse, back[0:1, :], back[2:3, :], number)
    lanes = sh.shape[2]
    joined = (jh[0], jl[0])

    @pl.when(pl.program_id(0) == 0)
    def _():
        grads[...] = jnp.zeros_like(grads)

    out = None
    for n in range(sh.shape[0]):
        at = slice(n * lanes, (n + 1) * lanes)
        g = split(alpha[:, at] * u_ref[:, at] + beta[:, at] * short[:, at] + gamma[:, at])
        grads[n] += dot3(joined, g, 0, 0)
        part = dot3(g, (sh[n], sl[n]), 1, 1)
        out = part if out is None else out + part
    dx[...] = out


def slow7_kernel(
    number, frames, mp, mn, tot_m, back, gain_m, tot_f, gain_f, bias_f, um, pm, before, after, th, tl,
    first, wh, wl, uf, tg, st, zp, zn
):
    mean, inverse = moments(tot_m[0:1, :], tot_m[1:2, :], number)
    alpha, beta, gamma = back_terms(gain_m[...], mean, inverse, back[0:1, :], back[1:2, :], number)
    g = alpha * um[...] + beta * pm[...] + gamma
    prev = shifted(zp, g, 1, frames, alpha * before[0, 0] + beta * before[0, 1] + gamma)
    nxt = shifted(zn, g, -1, frames, alpha * after[0, 0] + beta * after[0, 1] + gamma)
    gs = split(g)
    add_whole(tg, dot3(gs, (th[0], tl[0]), 0, 0))
    width = gain_f.shape[1]
    v = dot3(split(masked(nxt, mn)), (wh[:, 0:width], wl[:, 0:width]))
    v += dot3(gs, (wh[:, width : 2 * width], wl[:, width : 2 * width]))
    v += dot3(split(masked(prev, mp)), (wh[:, 2 * width :], wl[:, 2 * width :]))
    mean_f, inv_f = moments(tot_f[0:1, 0:width], tot_f[1:2, 0:width], number)
    z = first[...] - mean_f
    u = v * slope(z * (gain_f[...] * inv_f) + bias_f[...])
    uf[...] = u
    add_rows(st, colsum(u), colsum(u * z))


def slow8_kernel(
    number, frames, idx, tot_f, back, gain_f, tot_a, gain_a, bias_a, uf, first, jh, jl, dx, side,
    rh, rl, o0, o1, o2, o3, us, rg, e0, st, wide, tmp
):
    width = gain_f.shape[1]
    mean, inverse = moments(tot_f[0:1, 0:width], tot_f[1:2, 0:width], number)
    alpha, beta, gamma = back_terms(gain_f[...], mean, inverse, back[0:1, :], back[1:2, :], number)
    g = split(alpha * uf[...] + beta * first[...] + gamma)
    add_whole(rg, dot3(g, (jh[0], jl[0]), 0, 0))
    lanes = o0.shape[1]
    wide[...] = dx[...] + dot3(g, (rh[...], rl[...]))
    for r, o in enumerate((o0, o1, o2, o3)):
        at = pl.multiple_of(idx[3 + r] * lanes, lanes)
        o[...] = wide[:, pl.ds(at, lanes)]
    mean_a, inv_a = moments(tot_a[0:1, :], tot_a[1:2, :], number)
    z = side[...] - mean_a
    top = wide.shape[1] - width
    u = wide[:, top:] * slope(z * (inv_a * gain_a[...]) + bias_a[...])
    us[...] = u
    e0[0] = edge(tmp, u, 0, frames)
    add_rows(st, colsum(u), colsum(u * z))


def side_terms(number, tot_a, back, gain_a):
    mean, inverse = moments(tot_a[0:1, :], tot_a[1:2, :], number)
    return back_terms(gain_a[...], mean, inverse, back[0:1, :], back[1:2, :], number)


def slow9_kernel(number, frames, idx, mask, tot_a, back, gain_a, us, side, x_ref, halo, lg, bz):
    alpha, beta, gamma = side_terms(number, tot_a, back, gain_a)
    g = split(alpha * us[...] + beta * side[...] + gamma)
    add_whole(lg, dot3(g, split(lateral_taps(frames, mask, x_ref, halo, bz)), 0, 0))


def last_kernel(
    number, frames, idx, mask, tot_a, back, gain_a, us, side, us_edge, side_edge, u3, g1, wh, wl,
    rh, rl, o_ref, f_ref, zn
):
    alpha, beta, gamma = side_terms(number, tot_a, back, gain_a)
    here = alpha * us[...] + beta * side[...] + gamma
    after = shifted(zn, here, -1, frames, alpha * us_edge[0] + beta * side_edge[0] + gamma)
    base = u3[...] + dot3(split(g1[...]), (rh[...], rl[...]), 1, 1)
    near = dot3(split(here), (wh[:, 256:], wl[:, 256:]))
    far = dot3(split(masked(after, mask)), (wh[:, 0:256], wl[:, 0:256]))
    both = jnp.concatenate(
        [near[:, 0:256], near[:, 256:384] + far[:, 0:128], far[:, 128:256]], axis=1
    )
    out = base + both
    put_frames(o_ref, out)
    put_frames(f_ref, out)


def weight_split(w):
    high = lax.reduce_precision(w, 8, 7)
    return high.astype(BF16), (w - high).astype(BF16)


def row(v):
    return v.reshape(1, -1)


def tiled_row(v):
    return jnp.tile(v.reshape(1, -1), (1, 4))


def by_pixel(v):
    return v.transpose(1, 0, 2)


def after(value, *events):
    return lax.optimization_barrier((value,) + events)[0]


def local(sizes, *args):
    (
        slow_input, fast_input, clip_starts,
        fast_reduce, fast_reduce_gain, fast_reduce_bias,
        fast_temporal, fast_temporal_gain, fast_temporal_bias,
        fast_expand, fast_expand_gain, fast_expand_bias,
        lateral_conv, lateral_gain, lateral_bias,
        slow_reduce, slow_reduce_gain, slow_reduce_bias,
        slow_temporal, slow_temporal_gain, slow_temporal_bias,
        slow_expand, slow_expand_gain, slow_expand_bias,
        shortcut_conv, shortcut_gain, shortcut_bias,
        slow_cotangent, fast_cotangent,
    ) = args
    dps, ys, hs = sizes
    roles = ys * hs
    d, y, h = (lax.axis_index(a) for a in ALL)
    m = y * hs + h
    frames, pixels, lanes = slow_input.shape
    shard_rows = slow_reduce.shape[1]
    inner = shard_rows * roles
    joined_width = slow_reduce.shape[0]
    wide = lanes * roles
    number = frames * dps * pixels
    fast_number = number * 4
    half = pixels // hs
    own = pixels // roles
    steps = 7
    half_block, own_block = half // steps, own // steps
    fast_rows, slow_rows = half_block * frames, own_block * frames

    slow_x = by_pixel(slow_input).reshape(pixels * frames, lanes)
    slow_c = by_pixel(slow_cotangent).reshape(pixels * frames, lanes)
    fast_x = by_pixel(fast_input)
    fast_c = by_pixel(fast_cotangent)

    def block_of(p):
        return (p % hs) * ys + p // hs

    def role_xor(r):
        return (y ^ (r // hs)) * hs + (h ^ (r % hs))

    peers = [role_xor(r) for r in range(roles)]
    q = block_of(m)
    idx = jnp.stack([h, q, y] + peers).astype(jnp.int32)
    own_rows = own * frames
    row_at = [own_rows * block_of(p) for p in peers]

    times = d * frames + jnp.arange(0, frames + 1, dtype=jnp.int32)

    def clip_of(t):
        return jnp.sum((clip_starts[None, :] <= t[:, None]).astype(jnp.int32), axis=1) - 1

    same = jnp.logical_and(
        clip_of(times) == clip_of(times - 1), jnp.logical_and(times >= 1, times < frames * dps)
    ).astype(F32)
    mask_prev = jnp.broadcast_to(same[:frames, None], (frames, 128))
    mask_next = jnp.broadcast_to(same[1:, None], (frames, 128))

    def role_pairs(r):
        return [(i, i ^ r) for i in range(roles)]

    def placed(out, got):
        for r in range(1, roles):
            out = lax.dynamic_update_slice_in_dim(out, got[r - 1], row_at[r], axis=0)
        return by_pixel(out.reshape(pixels, frames, lanes))

    swap = [(0, 1), (1, 0)]
    half_rows = half * frames

    def from_core(array):
        return lax.ppermute(
            lax.dynamic_slice_in_dim(array, half_rows * (1 - h), half_rows, axis=0), "hh", swap
        )

    def for_partner(array, here):
        return [
            lax.dynamic_slice_in_dim(array, half_rows * h + own_rows * (1 - y), own_rows, axis=0),
            lax.dynamic_slice_in_dim(here, own_rows * (1 - y), own_rows, axis=0),
        ]

    sho_y = lax.ppermute(shortcut_conv, "yy", swap)
    in_core = from_core(slow_x)
    in_send = jnp.concatenate(for_partner(slow_x, in_core), axis=0)
    in_y = lax.ppermute(in_send, "yy", swap)

    vectors = [
        lateral_gain, lateral_bias, slow_reduce_gain, slow_reduce_bias, slow_temporal_gain,
        slow_temporal_bias, slow_expand_gain, slow_expand_bias, shortcut_gain, shortcut_bias,
    ]
    vector = jnp.concatenate(vectors)
    share = shard_rows // dps
    across = -(-vector.shape[0] // (share * 128)) * 128
    vector = jnp.pad(vector, (0, share * across - vector.shape[0])).reshape(share, across)
    piece = jnp.concatenate(
        [
            lateral_conv.transpose(2, 0, 1).reshape(shard_rows, -1),
            slow_reduce.T,
            slow_temporal.transpose(2, 0, 1).reshape(shard_rows, -1),
            slow_expand,
        ],
        axis=1,
    )
    piece = jnp.concatenate([lax.dynamic_slice_in_dim(piece, d * share, share, axis=0), vector], axis=1)
    got = lax.all_gather(piece, ALL, axis=0, tiled=False).reshape((dps, roles) + piece.shape)
    matrix = got[:, :, :, : piece.shape[1] - across].transpose(1, 0, 2, 3).reshape(inner, -1)
    taps = lateral_conv.shape[0] * lateral_conv.shape[1]
    bounds = [0, taps, taps + joined_width, taps + joined_width + 3 * inner]
    bounds.append(bounds[-1] + wide)
    (lat_h, lat_l), (red_h, red_l), (tem_h, tem_l), (exp_h, exp_l) = [
        weight_split(matrix[:, bounds[k] : bounds[k + 1]]) for k in range(4)
    ]
    vector = got[0, :, :, piece.shape[1] - across :].reshape(roles, -1)
    full = []
    start = 0
    for v in vectors:
        full.append(vector[:, start : start + v.shape[0]].reshape(1, -1))
        start += v.shape[0]
    (
        lat_gain, lat_bias, red_gain, red_bias, tem_gain, tem_bias, exp_gain, exp_bias, sho_gain, sho_bias
    ) = full

    eye = jnp.eye(4, dtype=F32)
    up = jnp.eye(4, k=1, dtype=F32)
    down = jnp.eye(4, k=-1, dtype=F32)
    far_next = jnp.eye(4, k=3, dtype=F32)
    far_prev = jnp.eye(4, k=-3, dtype=F32)
    fr_h, fr_l = weight_split(after(jnp.kron(eye, fast_reduce), in_send))
    fe_h, fe_l = weight_split(jnp.kron(eye, fast_expand))
    centre = jnp.kron(eye, fast_temporal[1]) + jnp.kron(up, fast_temporal[0]) + jnp.kron(down, fast_temporal[2])
    outer = jnp.kron(far_next, fast_temporal[2]) + jnp.kron(far_prev, fast_temporal[0])
    ft_h, ft_l = weight_split(jnp.concatenate([centre, outer], axis=0))
    fb_h, fb_l = weight_split(jnp.concatenate([centre, outer], axis=1))
    fr_gain, fr_bias = tiled_row(fast_reduce_gain), tiled_row(fast_reduce_bias)
    ft_gain, ft_bias = tiled_row(fast_temporal_gain), tiled_row(fast_temporal_bias)
    fe_gain, fe_bias = row(fast_expand_gain), row(fast_expand_bias)

    forth = [(i, i + 1) for i in range(dps - 1)]
    backw = [(i + 1, i) for i in range(dps - 1)]
    halo = lax.dynamic_slice(fast_x, (half * h, frames * 4 - 8, 0), (half, 8, 128))
    halo = lax.ppermute(halo, "dp", forth)

    in_half = lambda i, s, *_: s[0] * steps + i
    in_own = lambda i, s, *_: s[1] * steps + i
    own_in_half = lambda i, s, *_: s[2] * steps + i

    def all_of(*arrays):
        return [(x, whole(x)) for x in arrays]

    def const(*dims):
        o = shape(*dims)
        return (o, whole(o))

    def by_block(x, at=None):
        return (x, part(x, x.shape[0] // steps, at))

    def out_rows(rows, width):
        return by_block(shape(rows * steps, width))

    def out_blocks(*dims, dtype=F32):
        return by_block(shape(steps, *dims, dtype=dtype))

    def tmp(*dims):
        return pltpu.VMEM(dims, F32)

    def cut(rows, width):
        return tmp(width // 128, rows, 128)

    other_y = lambda i, s, *_: (1 - s[2]) * steps + i

    fr, sr = fast_rows, slow_rows
    nf, ns = fr * steps, sr * steps
    fx = (fast_x, part(fast_x, half_block, in_half))
    fc = (fast_c, part(fast_c, half_block, in_half))
    masks = all_of(mask_prev, mask_next)
    core = ("hh",)

    p1, e0, e1, st = stepped(
        functools.partial(fast1_kernel, frames), "fast1", steps, [idx], [fx] + all_of(fr_h, fr_l),
        [out_rows(fr, 128), out_blocks(half_block, 128), out_blocks(half_block, 128), const(2, 128)],
        scratch=[cut(fr, 128)],
        est=cost(2 * 3 * nf * 512 * 256, nf * 640 * 4),
    )
    st_f1 = st
    tot_f1, before, beyond = total([st], 1, sizes, core, (e1, e0))
    a1, z1, p2, st = stepped(
        functools.partial(fast2_kernel, fast_number, frames), "fast2", steps, [],
        masks + all_of(tot_f1, fr_gain, fr_bias)
        + [by_block(p1), by_block(before), by_block(beyond)] + all_of(ft_h, ft_l),
        [out_rows(fr, 128)] * 3 + [const(2, 128)],
        scratch=[cut(fr, 128)] * 2,
        est=cost(2 * 3 * nf * 256 * 256, 4 * nf * 128 * 4),
    )
    (tot_f2,) = total([st], 2, sizes, core)

    def role_table(mine, from_y, event):
        column = jnp.stack([after(mine, event), from_y])
        other = lax.ppermute(column, "hh", swap)
        table = jnp.stack([column[0], other[0], column[1], other[1]])
        return jnp.stack([lax.dynamic_index_in_dim(table, p, 0, keepdims=False) for p in peers])

    sho_h, sho_l = weight_split(role_table(shortcut_conv, sho_y, tot_f1))
    cot_core = from_core(after(slow_c, tot_f1))
    slow_cot = [cot_core] + [
        lax.all_gather(after(v, matrix), "yy", axis=0, tiled=True) for v in for_partner(slow_c, cot_core)
    ]
    side, side_edge, st_a = stepped(
        functools.partial(lateral_kernel, frames), "lateral", steps, [idx],
        all_of(mask_prev) + [fx, by_block(halo)] + all_of(after(lat_h, st), lat_l),
        [out_rows(fr, inner), out_blocks(half_block, inner), const(2, inner)],
        scratch=[cut(fr, 256)],
        est=cost(2 * 3 * nf * 768 * 256, nf * 768 * 4),
    )
    side_edge = lax.ppermute(side_edge, "dp", backw)
    b1, st = stepped(
        functools.partial(fast3_kernel, fast_number), "fast3", steps, [],
        all_of(tot_f2, ft_gain, ft_bias) + [by_block(p2)] + all_of(fe_h, fe_l),
        [out_rows(fr, 128), const(2, 512)],
        est=cost(2 * 3 * nf * 256 * 512, 2 * nf * 128 * 4),
    )
    tot_f3, tot_a = total([st, st_a], 3, sizes, core)
    half_out = shape(half, frames * 4, 128)
    full_out = shape(pixels, frames * 4, 128)
    fast_half, fast_full, u3, st_f4 = stepped(
        functools.partial(fast4_kernel, fast_number, 1.0 / ys), "fast4", steps, [idx],
        all_of(tot_f3, fe_gain, fe_bias) + [fx, fc, by_block(b1)] + all_of(fe_h, fe_l),
        [by_block(half_out), (full_out, part(full_out, half_block, in_half)), out_rows(fr, 512), const(2, 512)],
        est=cost(2 * 3 * nf * 256 * 512, nf * 5 * 512 * 4),
    )

    side_own = (side, part(side, slow_rows, own_in_half))
    sx = (slow_x, part(slow_x, slow_rows, in_own))
    sc = (slow_c, part(slow_c, slow_rows, in_own))
    bf_joined = out_blocks(sr, joined_width, dtype=BF16)
    first, short, jh, jl, e0, e1, st = stepped(
        functools.partial(slow1_kernel, number, frames), "slow1", steps, [idx],
        all_of(after(tot_a, st_f4), lat_gain, lat_bias) + [sx, (in_core, part(in_core, slow_rows, own_in_half))]
        + [(in_y, part(in_y, slow_rows, at)) for at in (lambda i, *s: i, lambda i, *s: steps + i)]
        + [side_own]
        + all_of(red_h, red_l, sho_h, sho_l),
        [
            out_rows(sr, inner), out_rows(sr, wide), bf_joined, bf_joined,
            out_blocks(own_block, inner), out_blocks(own_block, inner), const(2, inner + wide),
        ],
        scratch=[tmp(sr, joined_width), cut(sr, inner)],
        est=cost(2 * 3 * ns * 1280 * 1280, ns * 4 * 3840 + 7e6),
    )
    tot_s, back_f3, before, beyond = total([st, st_f4], 8, sizes, ROLE, (e1, e0))
    bf_taps = out_blocks(sr, 3 * inner, dtype=BF16)
    wide_masks = all_of(*[jnp.concatenate([v, v], axis=1) for v in (mask_prev, mask_next)])
    th, tl, pm, st = stepped(
        functools.partial(slow2_kernel, number, frames), "slow2", steps, [],
        wide_masks + all_of(tot_s, red_gain, red_bias) + [by_block(x) for x in (first, before, beyond)]
        + all_of(tem_h, tem_l),
        [bf_taps, bf_taps, out_rows(sr, inner), const(2, inner)],
        scratch=[cut(sr, inner)] * 2,
        est=cost(2 * 3 * ns * 768 * 256, ns * 4 * 1500),
    )
    (tot_m,) = total([st], 9, sizes, ROLE)
    bf_mid = out_blocks(sr, inner, dtype=BF16)
    bh, bl, st = stepped(
        functools.partial(slow3_kernel, number), "slow3", steps, [],
        all_of(tot_m, tem_gain, tem_bias) + [by_block(pm)] + all_of(exp_h, exp_l),
        [bf_mid, bf_mid, const(2, wide)],
        est=cost(2 * 3 * ns * 1024 * 256, ns * 4 * 512),
    )
    (tot_l,) = total([st], 10, sizes, ROLE)
    slow_full = shape(pixels * frames, lanes)
    own_out = (slow_full, part(slow_full, slow_rows, in_own))
    *outs, u, st = stepped(
        functools.partial(slow4_kernel, number), "slow4", steps, [idx],
        all_of(tot_l, tot_s, exp_gain, exp_bias, sho_gain, sho_bias)
        + [by_block(x) for x in (bh, bl, short)] + [sc]
        + [(slow_cot[0], part(slow_cot[0], slow_rows, own_in_half))]
        + [(x, part(x, slow_rows, other_y)) for x in slow_cot[1:]]
        + all_of(exp_h, exp_l),
        [own_out] + [out_rows(sr, lanes)] * (roles - 1) + [out_rows(sr, wide), const(4, wide)],
        scratch=[tmp(sr, wide)],
        est=cost(2 * 3 * ns * 1024 * 256, ns * 4 * 4352),
    )
    (back_ls,) = total([st], 11, sizes, ROLE)
    near_rows = lax.ppermute(outs[1], "hh", swap)
    far_rows = lax.ppermute(outs[3], "hh", swap)
    from_y = [lax.all_gather(v, "yy", axis=0, tiled=False) for v in (outs[2], far_rows)]

    dx, short_grads = stepped(
        functools.partial(slow6_kernel, number), "slow6", steps, [],
        all_of(tot_s, back_ls, sho_gain) + [by_block(x) for x in (u, short, jh, jl)] + all_of(sho_h, sho_l),
        [out_rows(sr, joined_width), const(roles, joined_width, lanes)],
        est=cost(2 * 6 * ns * 1280 * 1024, ns * 4 * 4600 + 12e6),
    )
    um, expand_grad, e0, e1, st = stepped(
        functools.partial(slow5_kernel, number, frames), "slow5", steps, [],
        all_of(tot_l, after(back_ls, dx), exp_gain, tot_m, tem_gain, tem_bias)
        + [by_block(x) for x in (u, bh, bl, pm)] + all_of(exp_h, exp_l),
        [
            out_rows(sr, inner), const(inner, wide), out_blocks(2, own_block, inner),
            out_blocks(2, own_block, inner), const(2, inner),
        ],
        scratch=[cut(sr, inner)],
        est=cost(2 * 9 * ns * 1024 * 256, ns * 4 * 1800),
    )
    slow_out = outs[0]
    back_m, before, beyond = total([st], 12, sizes, ROLE, (e1, e0))
    def by_peer(g):
        rows = g.shape[0] // roles
        parts = [lax.dynamic_slice_in_dim(g, p * rows, rows, axis=0) for p in peers]
        return jnp.stack([parts[0], parts[2]]), jnp.stack([parts[1], parts[3]])

    def chip_sum(near, far):
        return near + lax.ppermute(far, "hh", swap)

    expand_pair = lax.psum_scatter(
        after(expand_grad, *from_y).reshape(roles, shard_rows, wide), ROLE, scatter_dimension=0, tiled=False
    )
    short_pair = lax.psum_scatter(after(short_grads, *from_y), ROLE, scatter_dimension=0, tiled=False)
    uf, temporal_grad, st = stepped(
        functools.partial(slow7_kernel, number, frames), "slow7", steps, [],
        wide_masks + all_of(tot_m, back_m, tem_gain, tot_s, red_gain, red_bias)
        + [by_block(x) for x in (um, pm, before, beyond, th, tl, first)] + all_of(tem_h, tem_l),
        [out_rows(sr, inner), const(inner, 3 * inner), const(2, inner)],
        scratch=[cut(sr, inner)] * 2,
        est=cost(2 * 6 * ns * 768 * 256, ns * 4 * 1500),
    )
    (back_f,) = total([st], 13, sizes, ROLE)
    *outs, us, reduce_grad, us_edge, st = stepped(
        functools.partial(slow8_kernel, number, frames), "slow8", steps, [idx],
        all_of(tot_s, back_f, red_gain, tot_a, lat_gain, lat_bias)
        + [by_block(x) for x in (uf, first, jh, jl, dx)] + [side_own] + all_of(red_h, red_l),
        [own_out] + [out_rows(sr, lanes)] * (roles - 1)
        + [out_rows(sr, inner), const(inner, joined_width), out_blocks(own_block, inner), const(2, inner)],
        scratch=[tmp(sr, joined_width), cut(sr, inner)],
        est=cost(2 * 6 * ns * 1280 * 256, ns * 4 * 5000),
    )
    (back_a,) = total([st], 14, sizes, ROLE)
    shortcut_sum, expand_sum = lax.psum((short_pair, expand_pair), "dp")
    edge_sent = after(us_edge, back_a)
    edge_same = lax.ppermute(edge_sent, "dp", backw)
    edge_cross = lax.ppermute(
        edge_sent, ("dp", "yy"), [(i * ys + j, (i - 1) * ys + 1 - j) for i in range(1, dps) for j in range(ys)]
    )

    own_halo = (halo, part(halo, own_block, own_in_half))
    (lateral_grad,) = stepped(
        functools.partial(slow9_kernel, number, frames), "slow9", steps, [idx],
        all_of(mask_prev, tot_a, back_a, lat_gain)
        + [by_block(us), side_own, (fast_x, part(fast_x, own_block, in_own)), own_halo],
        [const(inner, 640)],
        scratch=[cut(sr, 256)],
        est=cost(2 * 3 * ns * 640 * 256, ns * 4 * 1500),
    )

    both = chip_sum(*by_peer(jnp.concatenate([lateral_grad, reduce_grad, temporal_grad], axis=1)))
    rest_y = lax.ppermute(both[1], "yy", swap)
    us_other = lax.ppermute(after(us, both), "yy", swap)

    u2, expand_packed, e0, e1, st = stepped(
        functools.partial(fast5_kernel, fast_number, frames), "fast5", steps, [],
        all_of(tot_f3, after(back_f3, back_a, both, short_pair, expand_pair), fe_gain, tot_f2, ft_gain, ft_bias)
        + [by_block(u3), by_block(b1), by_block(p2)] + all_of(fe_h, fe_l),
        [
            out_rows(fr, 128), const(128, 512), out_blocks(2, half_block, 128),
            out_blocks(2, half_block, 128), const(2, 128),
        ],
        scratch=[cut(fr, 128)],
        est=cost(2 * 9 * nf * 256 * 512, nf * 900 * 4),
    )
    rest = both[0] + after(rest_y, u2)
    back_f2, before, beyond = total([st], 5, sizes, core, (e1, e0))
    grads_sent = [
        lax.ppermute(after(outs[r], back_a if r == 1 else rest), ROLE, role_pairs(r))
        for r in range(1, roles)
    ]
    slow_input_gradient = placed(outs[0], grads_sent)

    u1, temporal_packed, st = stepped(
        functools.partial(fast6_kernel, fast_number, frames), "fast6", steps, [],
        masks + all_of(tot_f2, after(back_f2, rest), ft_gain, tot_f1, fr_gain, fr_bias)
        + [by_block(x) for x in (u2, p2, before, beyond, a1, z1, p1)] + all_of(fb_h, fb_l),
        [out_rows(fr, 128), const(256, 128), const(2, 128)],
        scratch=[cut(fr, 128)] * 2,
        est=cost(2 * 6 * nf * 256 * 256, 6 * nf * 128 * 4),
    )
    (back_f1,) = total([st], 6, sizes, core)
    g1, reduce_packed = stepped(
        functools.partial(fast7_kernel, fast_number), "fast7", steps, [idx],
        all_of(tot_f1, after(back_f1, us_other), fr_gain) + [fx, by_block(u1), by_block(p1)],
        [out_rows(fr, 128), const(512, 128)],
        est=cost(2 * 3 * nf * 512 * 256, nf * 900 * 4),
    )

    def in_order(mine, other):
        return jnp.concatenate([jnp.where(y == 0, mine, other), jnp.where(y == 0, other, mine)], axis=0)

    eb = expand_packed.reshape(4, 32, 4, 128)
    expand_small = eb[0, :, 0] + eb[1, :, 1] + eb[2, :, 2] + eb[3, :, 3]
    rb = reduce_packed.reshape(4, 128, 4, 32)
    reduce_small = rb[0, :, 0] + rb[1, :, 1] + rb[2, :, 2] + rb[3, :, 3]
    tb = temporal_packed.reshape(8, 32, 4, 32)
    tap0 = tb[0, :, 1] + tb[1, :, 2] + tb[2, :, 3] + tb[7, :, 0]
    tap1 = tb[0, :, 0] + tb[1, :, 1] + tb[2, :, 2] + tb[3, :, 3]
    tap2 = tb[1, :, 0] + tb[2, :, 1] + tb[3, :, 2] + tb[4, :, 3]
    small = jnp.concatenate(
        [expand_small, reduce_small.reshape(32, 128), jnp.stack([tap0, tap1, tap2]).reshape(24, 128)], axis=0
    )
    count = small.shape[0]
    small = jnp.pad(small, ((0, -count % dps), (0, 0)))
    small, rest = last_total(small.reshape(dps, -1, 128), rest.reshape(dps, -1, rest.shape[1]), 15, sizes)
    small = small.reshape(-1, 128)[:count]
    rest = rest.reshape(shard_rows, -1)
    lateral_sum = rest[:, 0:taps].reshape(shard_rows, -1, 128).transpose(1, 2, 0)
    reduce_sum = rest[:, taps : taps + joined_width].T
    temporal_sum = rest[:, taps + joined_width :].reshape(shard_rows, 3, inner).transpose(1, 2, 0)
    us_half = in_order(us, after(us_other, g1))
    rim = in_order(edge_same.reshape(own, inner), edge_cross.reshape(own, inner))
    grad_half, grad_full = stepped(
        functools.partial(last_kernel, number, frames), "last", steps, [idx],
        all_of(mask_next, tot_a, after(back_a, grads_sent[1], grads_sent[2], shortcut_sum, small), lat_gain)
        + [by_block(x) for x in (us_half, side, rim.reshape(steps, half_block, inner), side_edge, u3, g1)]
        + all_of(lat_h, lat_l, fr_h, fr_l),
        [by_block(half_out), (full_out, part(full_out, half_block, in_half))],
        scratch=[cut(fr, inner)],
        est=cost(2 * 3 * nf * 1024 * 256, nf * 4 * 2000),
    )

    def fast_whole(mine, full):
        got = lax.ppermute(mine, "hh", swap)
        return by_pixel(lax.dynamic_update_slice_in_dim(full, got, half * (1 - h), axis=0))

    from_y = [lax.dynamic_index_in_dim(v, 1 - y, 0, keepdims=False) for v in from_y]
    slow_output = placed(after(slow_out, small), [near_rows] + from_y)
    fast_output = fast_whole(after(fast_half, small), after(fast_full, small))
    fast_input_gradient = fast_whole(grad_half, grad_full)

    def fold(v):
        return jnp.sum(v.reshape(4, -1), axis=0)

    def zhat(back, tot, n, row_at=1, off=0):
        mean = tot[0, off:] / n
        return back[row_at] * lax.rsqrt(tot[1, off:] / n - mean * mean + EPSILON)

    def fast_pair(back, tot):
        sums = jnp.sum(tot.reshape(2, 4, -1), axis=1)
        bias = fold(back[0])
        mean = sums[0] / fast_number
        return fold(back[1]) * lax.rsqrt(sums[1] / fast_number - mean * mean + EPSILON), bias

    def shard(v):
        size = v.shape[0] // roles
        return lax.dynamic_slice_in_dim(v, m * size, size, axis=0)

    def slow_pair(back, tot, n=number, row_at=1, off=0, width=None):
        tot = tot[:, : width] if width else tot
        return shard(zhat(back, tot, n, row_at, off)), shard(back[0])

    fr_gg, fr_bg = fast_pair(back_f1, tot_f1)
    ft_gg, ft_bg = fast_pair(back_f2, tot_f2)
    fe_gg, fe_bg = fast_pair(back_f3, tot_f3)
    la_gg, la_bg = slow_pair(back_a, tot_a, number)
    re_gg, re_bg = slow_pair(back_f, tot_s, width=inner)
    te_gg, te_bg = slow_pair(back_m, tot_m)
    ex_gg, ex_bg = slow_pair(back_ls, tot_l)
    sh_gg, sh_bg = slow_pair(back_ls, tot_s, row_at=2, off=inner)
    return (
        slow_output, fast_output, slow_input_gradient, fast_input_gradient,
        small[32:64].reshape(128, 32), fr_gg, fr_bg,
        small[64:88].reshape(3, 32, 32), ft_gg, ft_bg,
        small[0:32], fe_gg, fe_bg,
        lateral_sum, la_gg, la_bg,
        reduce_sum, re_gg, re_bg,
        temporal_sum, te_gg, te_bg,
        expand_sum, ex_gg, ex_bg,
        shortcut_sum, sh_gg, sh_bg,
    )


def solution(mesh):
    dps, roles = mesh.shape["dp"], mesh.shape["mp"]
    sizes = (dps, roles // 2, 2)
    fine = Mesh(mesh.devices.reshape(sizes), ALL)
    mp = ROLE
    frames3 = P("dp", None, mp)
    fast3 = P("dp", None, None)
    none = P()
    in_specs = (
        (frames3, fast3) + (none,) * 10
        + (P(None, None, mp), P(mp), P(mp), P(None, mp), P(mp), P(mp), P(None, None, mp), P(mp), P(mp),
           P(mp, None), P(mp), P(mp), P(None, mp), P(mp), P(mp), frames3, fast3)
    )
    out_specs = (
        (frames3, fast3, frames3, fast3) + (none,) * 9
        + (P(None, None, mp), P(mp), P(mp), P(None, mp), P(mp), P(mp), P(None, None, mp), P(mp), P(mp),
           P(mp, None), P(mp), P(mp), P(None, mp), P(mp), P(mp))
    )
    return jax.shard_map(
        functools.partial(local, sizes), mesh=fine, in_specs=in_specs, out_specs=out_specs, check_vma=False
    )
```
